32 devices in a mesh: dp: 4 (over y, x), fsdp: 8 (over z, core).
Axes of the slice: x: 2, y: 2, z: 4, core: 2. Of those that a mesh axis runs over, the one named last changes fastest.
Arguments:
- tokens: bfloat16 [32768, 768], P(('dp', 'fsdp')), may hold values from -6 to 6
- cotangent: bfloat16 [32768, 768], P(('dp', 'fsdp')), may hold values from -6 to 6
- segment_ids: int32 [256, 128], P(('dp', 'fsdp')), may hold values from 0 to 3, never falling along the last dimension, each value on 1 to 64 neighbouring positions
- live_mask: int32 [256, 128], P(('dp', 'fsdp')), may hold values 0 or 1
- predicted: int32 [32768], P(('dp', 'fsdp')), may hold values from 0 to 23
- targets: int32 [32768], P(('dp', 'fsdp')), may hold values from 0 to 23
- w_qkv: bfloat16 [768, 2304], P(('dp', 'fsdp')), may hold values from -0.21875 to 0.21875
- bias_query: bfloat16 [768], P(('dp', 'fsdp')), may hold values from -1 to 1
- bias_value: bfloat16 [768], P(('dp', 'fsdp')), may hold values from -1 to 1
- w_out: bfloat16 [768, 768], P(('dp', 'fsdp')), may hold values from -0.4375 to 0.4375
- bias_out: bfloat16 [768], P(('dp', 'fsdp')), may hold values from -1 to 1
- gain_attn: bfloat16 [768], P(('dp', 'fsdp')), may hold values from 0.5 to 1.5
- shift_attn: bfloat16 [768], P(('dp', 'fsdp')), may hold values from -1 to 1
- w_up: bfloat16 [768, 3072], P(('dp', 'fsdp')), may hold values from -0.21875 to 0.21875
- bias_up: bfloat16 [3072], P(('dp', 'fsdp')), may hold values from -1 to 1
- w_down: bfloat16 [3072, 768], P(('dp', 'fsdp')), may hold values from -0.15625 to 0.15625
- bias_down: bfloat16 [768], P(('dp', 'fsdp')), may hold values from -1 to 1
- gain_ffn: bfloat16 [768], P(('dp', 'fsdp')), may hold values from 0.5 to 1.5
- shift_ffn: bfloat16 [768], P(('dp', 'fsdp')), may hold values from -1 to 1
Outputs:
- layer_output: bfloat16 [32768, 768], P(('dp', 'fsdp'))
- grad_tokens: float32 [32768, 768], P(('dp', 'fsdp'))
- grad_w_qkv: float32 [768, 2304], P(('dp', 'fsdp'))
- grad_bias_query: float32 [768], P(('dp', 'fsdp'))
- grad_bias_value: float32 [768], P(('dp', 'fsdp'))
- grad_w_out: float32 [768, 768], P(('dp', 'fsdp'))
- grad_bias_out: float32 [768], P(('dp', 'fsdp'))
- grad_gain_attn: float32 [768], P(('dp', 'fsdp'))
- grad_shift_attn: float32 [768], P(('dp', 'fsdp'))
- grad_w_up: float32 [768, 3072], P(('dp', 'fsdp'))
- grad_bias_up: float32 [3072], P(('dp', 'fsdp'))
- grad_w_down: float32 [3072, 768], P(('dp', 'fsdp'))
- grad_bias_down: float32 [768], P(('dp', 'fsdp'))
- grad_gain_ffn: float32 [768], P(('dp', 'fsdp'))
- grad_shift_ffn: float32 [768], P(('dp', 'fsdp'))
- tallies: int32 [2, 24], replicated
The draws below stay inside these ranges and needn't reach their ends.
Inputs may be any that keep to these rules, and one draw needn't show every extreme that they name: `segment_ids`: within each packed row of 128 tokens the ids never fall and restart at 0; one sequence holds 1 to 64 tokens.
All inputs are finite; a program needn't handle non-finite values. No bound on the sum of `live_mask` on one device may be relied on, other than what follows from the above.
Results may differ from the reference program's by a relative error of at most 0.012.
Values may be sent and summed in bfloat16 or wider, within the bound.
A program may use at most 192 MiB of HBM per device.

```python
import math
import jax
import jax.numpy as jnp
import numpy as np
from jax import lax

D = 768
FF = 3072
HEADS = 12
HEAD_DIM = 64
CLASSES = 24
SEQ = 128
ROWS = 256
TOKENS = 32768


def place_ends(entries, key, least, high):
    longest = entries.shape.index(max(entries.shape))
    spots = []
    for shift in (0, 1):
        where = [jax.random.randint(jax.random.fold_in(key, axis), (), 0, length) for axis, length in enumerate(entries.shape)]
        where[longest] = (where[longest] + shift) % entries.shape[longest]
        spots.append(tuple(where))
    return entries.at[spots[0]].set(least).at[spots[1]].set(high)


def block_scale(rng, shape, cuts, low, high):
    gain = 1.0
    for axis_at, shards_of in cuts:
        heights = jax.random.uniform(jax.random.fold_in(jax.random.fold_in(rng, 6), axis_at), (shards_of,), jnp.float32, low / len(cuts), high / len(cuts))
        gain = gain * jnp.repeat(jnp.exp(heights), shape[axis_at] // shards_of).reshape((-1,) + (1,) * (len(shape) - 1 - axis_at))
    return gain


def length_profile(count, total, reach, lean):
    portions = [(1 << 20) // math.isqrt(standing ** lean) + 1 for standing in range(2, count + 1)]
    rest, counts = total - reach - (count - 1), [1] * (count - 1)
    while rest > 0:
        free = [i for i in range(count - 1) if counts[i] < reach]
        whole, budget = sum([portions[i] for i in free]), rest
        for i in free:
            addition = min(reach - counts[i], max(1, budget * portions[i] // whole), rest)
            counts[i] = counts[i] + addition
            rest = rest - addition
    return np.array([reach] + counts)


def uneven_parts(own_key, count, total, most, slope):
    if count == 2:
        one = jax.random.randint(own_key, (), max(1, total - most), min(most, total - 1) + 1)
        return jnp.stack([one, total - one])
    sizes = jnp.asarray(length_profile(count, total, most, slope), jnp.int32)
    couples = (count - 1) // 2
    donor, receiver = sizes[1:1 + 2 * couples:2], sizes[2:2 + 2 * couples:2]
    room = jnp.minimum(donor - 1, most - receiver)
    shifted = jax.random.randint(jax.random.fold_in(own_key, 1), (couples,), 0, 1 << 20) % (room + 1)
    sizes = sizes.at[1:1 + 2 * couples:2].set(donor - shifted).at[2:2 + 2 * couples:2].set(receiver + shifted)
    return sizes[jax.random.permutation(jax.random.fold_in(own_key, 2), count)]


def centred(key, dims, deviation, limit, shards=(), kind=jnp.bfloat16):
    entries = jax.random.normal(key, dims, jnp.float32) * deviation
    if len(shards) > 0:
        entries = block_scale(key, dims, shards, -0.22, 0.18) * entries
    return jnp.clip(entries, min=-limit, max=limit).astype(kind)


def setup_inputs(seed: int = 0) -> dict:
    seeds = jax.random.split(jax.random.key(seed), 20)
    return {
        "tokens": centred(seeds[0], (TOKENS, D), 1.0, 6.0, ((0, 32),)),
        "cotangent": centred(seeds[1], (TOKENS, D), 1.0, 6.0, ((0, 32),)),
        "segment_ids": jax.vmap(lambda own: jnp.searchsorted(jnp.cumsum(uneven_parts(own, 4, SEQ, SEQ // 2, 1)), jnp.arange(SEQ), side="right"))(jax.random.split(seeds[2], ROWS)).reshape((ROWS, SEQ)).astype(jnp.int32),
        "live_mask": place_ends((jax.random.randint(seeds[3], (ROWS, SEQ), 0, 8) < 7).astype(jnp.int32), jax.random.fold_in(seeds[3], 1), 0, 1),
        "predicted": place_ends(jax.random.randint(seeds[4], (TOKENS,), 0, CLASSES), jax.random.fold_in(seeds[4], 1), 0, CLASSES - 1).astype(jnp.int32),
        "targets": place_ends(jax.random.randint(seeds[5], (TOKENS,), 0, CLASSES), jax.random.fold_in(seeds[5], 1), 0, CLASSES - 1).astype(jnp.int32),
        "w_qkv": centred(seeds[6], (D, 3 * D), D ** -0.5, 0.21875, ((0, 32),)),
        "bias_query": centred(seeds[7], (D,), 0.2, 1.0, ((0, 32),)),
        "bias_value": centred(seeds[8], (D,), 0.2, 1.0, ((0, 32),)),
        "w_out": centred(seeds[9], (D, D), (D // 4) ** -0.5, 0.4375, ((0, 32),)),
        "bias_out": centred(seeds[10], (D,), 0.2, 1.0, ((0, 32),)),
        "gain_attn": jnp.clip(1.0 + 0.1 * jax.random.normal(seeds[11], (D,), jnp.float32), 0.5, 1.5).astype(jnp.bfloat16),
        "shift_attn": centred(seeds[12], (D,), 0.2, 1.0, ((0, 32),)),
        "w_up": centred(seeds[13], (D, FF), D ** -0.5, 0.21875, ((0, 32),)),
        "bias_up": centred(seeds[14], (FF,), 0.2, 1.0, ((0, 32),)),
        "w_down": centred(seeds[15], (FF, D), (FF // 2) ** -0.5, 0.15625, ((0, 32),)),
        "bias_down": centred(seeds[16], (D,), 0.2, 1.0, ((0, 32),)),
        "gain_ffn": jnp.clip(1.0 + 0.1 * jax.random.normal(seeds[17], (D,), jnp.float32), 0.5, 1.5).astype(jnp.bfloat16),
        "shift_ffn": centred(seeds[18], (D,), 0.2, 1.0, ((0, 32),)),
    }


@jax.custom_vjp
def low(v):
    return lax.optimization_barrier(v.astype(jnp.bfloat16)).astype(jnp.float32)

@jax.custom_vjp
def low_back(v):
    return v

def low_keep(v):
    return (low(v), None)

def low_pass(kept, grad):
    return (grad,)

def back_keep(v):
    return (v, None)

def back_low(kept, grad):
    return (low(grad),)
low.defvjp(low_keep, low_pass)
low_back.defvjp(back_keep, back_low)

def both_round(operand):
    return low(low_back(operand))

def layer_norm(operand, scale_vec, shift_vec):
    center = operand - lax.optimization_barrier(jnp.mean(operand, axis=-1, keepdims=True))
    spread = lax.optimization_barrier(jnp.mean(center * center, axis=-1, keepdims=True))
    return center * lax.rsqrt(spread + 1e-05) * scale_vec + shift_vec

def block_forward(params, tokens_blk, seg_blk, live_blk):
    w_qkv, bias_query, bias_value, w_out, bias_out, gain_attn, shift_attn, w_up, bias_up, w_down, bias_down, gain_ffn, shift_ffn = params
    precise = lax.Precision.HIGHEST
    row_count = tokens_blk.shape[0]
    projected = jnp.einsum('bsd,de->bse', tokens_blk, w_qkv, precision=precise)
    queries = both_round(projected[..., :D] + bias_query).reshape(row_count, SEQ, HEADS, HEAD_DIM)
    keys_part = both_round(projected[..., D:2 * D]).reshape(row_count, SEQ, HEADS, HEAD_DIM)
    values = both_round(projected[..., 2 * D:] + bias_value).reshape(row_count, SEQ, HEADS, HEAD_DIM)
    scores = low_back(jnp.einsum('bqhc,bkhc->bhqk', queries, keys_part, precision=precise) * HEAD_DIM ** (-0.5))
    diagonal = jnp.eye(SEQ, dtype=bool)
    allowed = (seg_blk[:, :, None] == seg_blk[:, None, :]) & ((live_blk[:, None, :] == 1) | diagonal[None])
    scores = jnp.where(allowed[:, None], scores, -1000000000.0)
    soft_weights = jax.nn.softmax(scores, axis=-1)
    context = jnp.einsum('bhqk,bkhc->bqhc', low(soft_weights), values, precision=precise)
    context = both_round(context.reshape(row_count, SEQ, D))
    attended = low_back(jnp.einsum('bsd,de->bse', context, w_out, precision=precise)) + bias_out
    hidden = layer_norm(tokens_blk + attended, gain_attn, shift_attn)
    up_value = low_back(jnp.einsum('bsd,df->bsf', low(hidden), w_up, precision=precise) + bias_up)
    activated = low(jax.nn.gelu(up_value, approximate=False))
    ffn_out = low_back(jnp.einsum('bsf,fd->bsd', activated, w_down, precision=precise)) + bias_down
    return layer_norm(hidden + ffn_out, gain_ffn, shift_ffn)

def reference(tokens, cotangent, segment_ids, live_mask, predicted, targets, w_qkv, bias_query, bias_value, w_out, bias_out, gain_attn, shift_attn, w_up, bias_up, w_down, bias_down, gain_ffn, shift_ffn):
    params = tuple((item.astype(jnp.float32) for item in (w_qkv, bias_query, bias_value, w_out, bias_out, gain_attn, shift_attn, w_up, bias_up, w_down, bias_down, gain_ffn, shift_ffn)))
    block_rows = math.gcd(ROWS, max(1, 4096 // SEQ))
    blocks = ROWS // block_rows
    token_blocks = tokens.astype(jnp.float32).reshape(blocks, block_rows, SEQ, D)
    seg_blocks = segment_ids.reshape(blocks, block_rows, SEQ)
    live_blocks = live_mask.reshape(blocks, block_rows, SEQ)

    def forward(weights, inputs):
        runner = jax.checkpoint(lambda pieces: block_forward(weights, pieces[0], pieces[1], pieces[2]))
        return lax.map(runner, (inputs, seg_blocks, live_blocks))
    layer_out, pullback = jax.vjp(forward, params, token_blocks)
    gradients, grad_in = pullback(cotangent.astype(jnp.float32).reshape(blocks, block_rows, SEQ, D))
    classes = jnp.arange(CLASSES, dtype=jnp.int32)
    live_flat = live_mask.reshape(-1) == 1
    target_hits = (targets[:, None] == classes[None, :]) & live_flat[:, None]
    correct = target_hits & (predicted[:, None] == targets[:, None])
    tallies = jnp.stack([lax.optimization_barrier(jnp.sum(correct, axis=0, dtype=jnp.int32)), lax.optimization_barrier(jnp.sum(target_hits, axis=0, dtype=jnp.int32))])
    return (layer_out.reshape(TOKENS, D).astype(jnp.bfloat16), grad_in.reshape(TOKENS, D), gradients[0], gradients[1], gradients[2], gradients[3], gradients[4], gradients[5], gradients[6], gradients[7], gradients[8], gradients[9], gradients[10], gradients[11], gradients[12], tallies)
```

```python
from functools import partial

import jax
import jax.numpy as jnp
from jax import lax
from jax.experimental import pallas as pl
from jax.experimental.pallas import tpu as pltpu
from jax.sharding import PartitionSpec as P

D = 768
HEADS = 12
HEAD_DIM = 64
CLASSES = 24


EPSILON = 1e-05


def normalize(operand, scale_vec, shift_vec):
    center = operand - jnp.mean(operand, axis=-1, keepdims=True)
    inverse = lax.rsqrt(jnp.mean(center * center, axis=-1, keepdims=True) + EPSILON)
    normed = center * inverse
    return (normed * scale_vec + shift_vec, normed, inverse)


def normalize_back(grad_out, normed, inverse, scale_vec):
    scaled = grad_out * scale_vec
    return inverse * (
        scaled
        - jnp.mean(scaled, axis=-1, keepdims=True)
        - normed * jnp.mean(scaled * normed, axis=-1, keepdims=True)
    )


def contract_rows(left, right):
    return lax.dot_general(
        left, right, (((0,), (0,)), ((), ())), preferred_element_type=jnp.float32
    )


def times_transposed(left, right):
    return lax.dot_general(
        left, right, (((1,), (1,)), ((), ())), preferred_element_type=jnp.float32
    )


def split_heads(matrix, row_count, seq_len):
    return matrix.reshape(row_count, seq_len, HEADS, HEAD_DIM)


def masked_scores(query_heads, key_heads, allowed):
    scores = jnp.einsum(
        "bqhc,bkhc->bhqk", query_heads, key_heads, preferred_element_type=jnp.float32
    ) * HEAD_DIM ** (-0.5)
    return jnp.where(allowed[:, None], scores, -1000000000.0)


MESH = pl.DeviceIdType.MESH
BF = jnp.bfloat16
F32 = jnp.float32
HALF = 384
LIMIT = 60 * 2**20


def place():
    dp, fsdp = lax.axis_index("dp"), lax.axis_index("fsdp")
    return dp // 2, dp % 2, fsdp // 2, fsdp % 2


class Wires:
    def __init__(self, send_sems, recv_sems):
        self.y, self.x, self.z, self.core = place()
        self.send_sems, self.recv_sems, self.used, self.open = send_sems, recv_sems, 0, []

    def device(self, y=None, x=None, z=None, core=None):
        y = self.y if y is None else y
        x = self.x if x is None else x
        z = self.z if z is None else z
        core = self.core if core is None else core
        return (y * 2 + x, z * 2 + core)

    def partner(self):
        return self.device(core=1 - self.core)

    def over_x(self):
        return self.device(x=1 - self.x)

    def over_y(self):
        return self.device(y=1 - self.y)

    def along_z(self, jump):
        return self.device(z=(self.z + jump) % 4)

    def peers(self):
        return [self.partner(), self.over_x(), self.over_y()] + [self.along_z(j) for j in (1, 2, 3)]

    def barrier(self):
        semaphore = pltpu.get_barrier_semaphore()
        for peer in self.peers():
            pl.semaphore_signal(semaphore, inc=1, device_id=peer, device_id_type=MESH)
        pl.semaphore_wait(semaphore, 6)

    def send(self, source, target, device):
        number = self.used
        self.used += 1
        copy = pltpu.make_async_remote_copy(
            src_ref=source,
            dst_ref=target,
            send_sem=self.send_sems.at[number],
            recv_sem=self.recv_sems.at[number],
            device_id=device,
            device_id_type=MESH,
        )
        copy.start()
        self.open.append(copy)
        return copy

    def drain(self):
        for copy in self.open:
            copy.wait_send()
        self.open = []


def arrived(copies):
    for copy in copies:
        copy.wait_recv()


def rows_at(start, count, slab):
    return pl.ds(pl.multiple_of(start * slab, 16), count * slab)


class Gather:
    def __init__(self, wires, ref, slab, first, width, order):
        self.w, self.ref, self.slab, self.order, self.width = wires, ref, slab, order, width
        self.first = first
        self.back = []
        self.steps = {"A": [self.z0, self.a1, self.a2, self.a3], "B": [self.z0, self.b1, self.b2, self.b3]}[order] + [self.done]
        self.at = 0

    def view(self, slabs, count):
        start = pl.multiple_of(self.first, 128)
        return self.ref.at[rows_at(slabs, count, self.slab), pl.ds(start, self.width)]

    def send(self, slabs, count, device):
        return self.w.send(self.view(slabs, count), self.view(slabs, count), device)

    def step(self):
        if self.at < len(self.steps):
            self.steps[self.at]()
            self.at += 1

    def finish(self):
        while self.at < len(self.steps):
            self.step()

    def z0(self):
        w = self.w
        chip = (w.y * 2 + w.x) * 4 + w.z
        self.into = [self.send(chip, 1, w.along_z(j)) for j in (1, 2, 3)]

    def a1(self):
        w = self.w
        arrived(self.into)
        mine = (w.y * 2 + w.x) * 4
        self.into = [self.send(mine, 4, w.over_x())]
        self.back.append(self.send(mine, 4, w.partner()))

    def a2(self):
        w = self.w
        arrived(self.into)
        self.into = [self.send(w.y * 8, 8, w.over_y())]
        self.back.append(self.send((w.y * 2 + 1 - w.x) * 4, 4, w.partner()))

    def a3(self):
        w = self.w
        arrived(self.into)
        self.back.append(self.send((1 - w.y) * 8, 8, w.partner()))

    def b1(self):
        w = self.w
        arrived(self.into)
        mine = (w.y * 2 + w.x) * 4
        self.into = [self.send(mine, 4, w.over_y())]
        self.back.append(self.send(mine, 4, w.partner()))

    def b2(self):
        w = self.w
        arrived(self.into)
        other = ((1 - w.y) * 2 + w.x) * 4
        self.into = [self.send((w.y * 2 + w.x) * 4, 4, w.over_x()), self.send(other, 4, w.over_x())]
        self.back.append(self.send(other, 4, w.partner()))

    def b3(self):
        w = self.w
        arrived(self.into)
        for y in (w.y, 1 - w.y):
            self.back.append(self.send((y * 2 + 1 - w.x) * 4, 4, w.partner()))

    def done(self):
        arrived(self.back)


def add_rows(target, target_at, source, source_at, count, tile):
    width = source.shape[1]

    def body(i, carry):
        there = pl.ds(pl.multiple_of(target_at[0] + i * tile, 16), tile)
        cols = pl.ds(pl.multiple_of(target_at[1], 128), width)
        here = pl.ds(pl.multiple_of(source_at + i * tile, 16), tile)
        target[there, cols] = (target[there, cols].astype(F32) + source[here, :].astype(F32)).astype(BF)
        return carry

    lax.fori_loop(0, count // tile, body, 0)


class Scatter:
    def __init__(self, wires, ref, slab, first, far, width, order, p, r1, r2, rz):
        self.w, self.ref, self.slab, self.first, self.far, self.width = wires, ref, slab, first, far, width
        self.p, self.r1, self.r2, self.rz = p, r1, r2, rz
        self.steps = {"A": [self.p0, self.a1, self.a2, self.a3], "B": [self.p0, self.b1, self.b2, self.b3]}[order]
        self.at = 0

    def step(self):
        if self.at < len(self.steps):
            self.steps[self.at]()
            self.at += 1

    def view(self, slabs, count, first=None):
        start = pl.multiple_of(self.first if first is None else first, 128)
        return self.ref.at[rows_at(slabs, count, self.slab), pl.ds(start, self.width)]

    def p0(self):
        self.into = [self.w.send(self.view(0, 16, self.far), self.p, self.w.partner())]

    def add(self, slabs, count, source, source_slab=0):
        add_rows(self.ref, (slabs * self.slab, self.first), source, source_slab * self.slab, count * self.slab, 48)

    def a1(self):
        w = self.w
        arrived(self.into)
        self.add((1 - w.y) * 8, 8, self.p, (1 - w.y) * 8)
        self.into = [w.send(self.view((1 - w.y) * 8, 8), self.r1, w.over_y())]
        self.add(w.y * 8, 8, self.p, w.y * 8)

    def a2(self):
        w = self.w
        arrived(self.into)
        other = (w.y * 2 + 1 - w.x) * 4
        self.add(other, 4, self.r1, (1 - w.x) * 4)
        self.into = [w.send(self.view(other, 4), self.r2, w.over_x())]
        self.add((w.y * 2 + w.x) * 4, 4, self.r1, w.x * 4)

    def z3(self):
        w = self.w
        mine = (w.y * 2 + w.x) * 4
        self.add(mine, 4, self.r2)
        self.into = []
        for j in (1, 2, 3):
            there = (w.z + j) % 4
            self.into.append(w.send(self.view(mine + there, 1), self.rz.at[j - 1], w.along_z(j)))

    def a3(self):
        arrived(self.into)
        self.z3()

    def b1(self):
        w = self.w
        arrived(self.into)
        self.into = []
        for y in (0, 1):
            slabs = (y * 2 + 1 - w.x) * 4
            self.add(slabs, 4, self.p, slabs)
            self.into.append(w.send(self.view(slabs, 4), self.r1.at[pl.ds(y * 4 * self.slab, 4 * self.slab), :], w.over_x()))
        for y in (0, 1):
            slabs = (y * 2 + w.x) * 4
            self.add(slabs, 4, self.p, slabs)

    def b2(self):
        w = self.w
        arrived(self.into)
        other = ((1 - w.y) * 2 + w.x) * 4
        self.add(other, 4, self.r1, (1 - w.y) * 4)
        self.into = [w.send(self.view(other, 4), self.r2, w.over_y())]
        self.add((w.y * 2 + w.x) * 4, 4, self.r1, w.y * 4)

    def b3(self):
        arrived(self.into)
        self.z3()

    def total(self):
        w = self.w
        arrived(self.into)
        mine = rows_at((w.y * 2 + w.x) * 4 + w.z, 1, self.slab)
        total = self.ref[mine, pl.ds(pl.multiple_of(self.first, 128), self.width)].astype(F32)
        for j in range(3):
            total = total + self.rz[j].astype(F32)
        return total


CHIPS = 16


def gather_kernel(
    sqkv, sout, sup, sdown, vec, wqkv, wout, wup, wdown, vecs, mine, theirs, mine_down, theirs_down, sends, recvs
):
    w = Wires(sends, recvs)
    w.barrier()
    chip = (w.y * 2 + w.x) * 4 + w.z
    core = w.core
    for h in (0, 1):
        for b in range(8):
            ref, at = ((sqkv, b), (sout, 0), (sup, b - 4))[0 if b < 3 else 1 if b < 4 else 2]
            cols = pl.ds(at * 768 + h * HALF, HALF)
            mine[h, 0:32, b * HALF : (b + 1) * HALF] = jnp.concatenate(
                [ref[:, cols].astype(F32), jnp.zeros((8, HALF), F32)], axis=0
            ).astype(BF)
        mine_down[h] = sdown[:, h * HALF : (h + 1) * HALF]
    early = w.send(mine.at[1 - core], theirs, w.partner())
    late = w.send(mine_down.at[1 - core], theirs_down, w.partner())
    tile = vecs.at[pl.ds(pl.multiple_of((chip * 2 + core) * 8, 8), 8), :]
    tile[...] = vec[...]

    def share(start, tiles, device):
        part = vecs.at[pl.ds(pl.multiple_of(start * 8, 8), tiles * 8), :]
        return w.send(part, part, device)

    v0 = share(chip * 2 + core, 1, w.partner())
    early.wait_recv()
    for b in range(8):
        ref, at = ((wqkv, b), (wout, 0), (wup, b - 4))[0 if b < 3 else 1 if b < 4 else 2]
        cols = slice(b * HALF, (b + 1) * HALF)
        own = mine[core, 0:32, cols].astype(F32)[:24]
        got = theirs[:, cols].astype(F32)[:24]
        low = jnp.where(core == 0, own, got)
        high = jnp.where(core == 0, got, own)
        ref[rows_at(chip, 1, 48), pl.ds(pl.multiple_of(at * 768 + core * HALF, 128), HALF)] = jnp.concatenate(
            [low, high], axis=0
        ).astype(BF)
    v0.wait_recv()
    v1 = [share(chip * 2, 2, w.along_z(j)) for j in (1, 2, 3)]
    late.wait_recv()
    cols = pl.ds(pl.multiple_of(core * HALF, 128), HALF)
    wdown[pl.ds(pl.multiple_of(chip * 192 + core * 96, 16), 96), cols] = mine_down[core]
    wdown[pl.ds(pl.multiple_of(chip * 192 + (1 - core) * 96, 16), 96), cols] = theirs_down[...]
    pieces = []
    for b in range(8):
        ref, at = ((wqkv, b), (wout, 0), (wup, b - 4))[0 if b < 3 else 1 if b < 4 else 2]
        pieces.append(Gather(w, ref, 48, at * 768 + core * HALF, HALF, "AB"[b % 2]))
    pieces.append(Gather(w, wdown, 192, core * HALF, 128, "A"))
    pieces.append(Gather(w, wdown, 192, core * HALF + 128, 256, "B"))
    for p in pieces[:2]:
        p.step()
    arrived(v1)
    v2 = share((w.y * 2 + w.x) * 8, 8, w.over_x())
    for t in range(0, len(pieces) + 8, 2):
        for back in range(4, -1, -1):
            for i in (t - 2 * back, t - 2 * back + 1):
                if 0 <= i < len(pieces) and not (t == 0 and back == 0):
                    pieces[i].step()
        if t == 0:
            v2.wait_recv()
            v3 = share(w.y * 16, 16, w.over_y())
        if t == 2:
            v3.wait_recv()
    for p in pieces:
        p.finish()
    w.drain()


def gather_all(w_qkv, w_out, w_up, w_down, vec):
    return pl.pallas_call(
        gather_kernel,
        out_shape=(
            jax.ShapeDtypeStruct((768, 2304), BF),
            jax.ShapeDtypeStruct((768, 768), BF),
            jax.ShapeDtypeStruct((768, 3072), BF),
            jax.ShapeDtypeStruct((3072, 768), BF),
            jax.ShapeDtypeStruct((256, 128), F32),
        ),
        in_specs=[pl.BlockSpec(memory_space=pltpu.VMEM)] * 5,
        out_specs=[pl.BlockSpec(memory_space=pltpu.VMEM)] * 5,
        scratch_shapes=[
            pltpu.VMEM((2, 32, 8 * HALF), BF),
            pltpu.VMEM((32, 8 * HALF), BF),
            pltpu.VMEM((2, 96, HALF), BF),
            pltpu.VMEM((96, HALF), BF),
            pltpu.SemaphoreType.DMA((128,)),
            pltpu.SemaphoreType.DMA((128,)),
        ],
        compiler_params=pltpu.CompilerParams(collective_id=0, has_side_effects=True, vmem_limit_bytes=LIMIT),
    )(w_qkv, w_out, w_up, w_down, vec)


def scatter_kernel(
    gqkv_in, gout_in, gup_in, gdown_in, sums,
    oqkv, oout, oup, odown, ovec,
    gqkv, gout, gup, gdown, *rest,
):
    p = rest[0:10]
    r1 = rest[10:20]
    r2 = rest[20:30]
    rz = rest[30:40]
    slab48, slab192, vp, vx, vy, vz, vsum, loads, sends, recvs = rest[40:]
    w = Wires(sends, recvs)
    core = w.core
    copies = []
    for i, (a, b) in enumerate(((gdown_in, gdown), (gup_in, gup), (gout_in, gout), (gqkv_in, gqkv))):
        copies.append(pltpu.make_async_copy(a, b, loads.at[i]))
        copies[-1].start()
    w.barrier()
    specs = [(gdown, 192, 0, 128, "A"), (gdown, 192, 128, 256, "B")]
    for b in range(4):
        specs.append((gup, 48, b * 768, HALF, "AB"[b % 2]))
    specs.append((gout, 48, 0, HALF, "A"))
    for b in range(3):
        specs.append((gqkv, 48, b * 768, HALF, "BAB"[b]))
    pieces = []
    for i, (ref, slab, at, width, order) in enumerate(specs):
        pieces.append(Scatter(w, ref, slab, at + core * HALF, at + (1 - core) * HALF, width, order, p[i], r1[i], r2[i], rz[i]))
    half = pl.ds(pl.multiple_of(core * HALF, 128), HALF)
    far = pl.ds(pl.multiple_of((1 - core) * HALF, 128), HALF)
    v = w.send(sums.at[:, far], vp, w.partner())
    v.wait_recv()
    vsum[:, half] = sums[:, half] + vp[...]
    v = w.send(vsum.at[:, half], vx, w.over_x())
    for c in copies[:1]:
        c.wait()
    pieces[0].step()
    pieces[1].step()
    copies[1].wait()
    pieces[2].step()
    pieces[3].step()
    copies[2].wait()
    copies[3].wait()
    v.wait_recv()
    vy_out = vz.at[3]
    vy_out[...] = vsum[:, half] + vx[...]
    v = w.send(vy_out, vy, w.over_y())
    v.wait_recv()
    vz_out = vz.at[4]
    vz_out[...] = vy_out[...] + vy[...]
    vs = [w.send(vz_out, vz.at[j - 1], w.along_z(j)) for j in (1, 2, 3)]
    todo = list(range(len(pieces)))
    for t in range(2, len(pieces) + 8, 2):
        for back in range(3, -1, -1):
            for i in (t - 2 * back, t - 2 * back + 1):
                if 0 <= i < len(pieces) and not (back == 0 and i < 4):
                    pieces[i].step()
    arrived(vs)
    vlast = vz.at[5]
    vlast[...] = vz_out[...] + vz[0] + vz[1] + vz[2]
    v = w.send(vlast, ovec.at[:, half], w.partner())
    ovec[:, half] = vlast[...]
    lasts = [v]
    for i, (ref, slab, at, width, order) in enumerate(specs):
        total = pieces[i].total()
        out, keep, rows = ((odown, slab192, 96) if slab == 192 else (None, slab48, 24))
        if out is None:
            out = {id(gup): oup, id(gout): oout, id(gqkv): oqkv}[id(ref)]
        stage = keep.at[i if slab == 192 else i - 2]
        stage = stage.at[:, 0:width]
        stage[...] = total
        cols = pl.ds(pl.multiple_of(at + core * HALF, 128), width)
        out[:, cols] = stage[pl.ds(pl.multiple_of(rows * core, 8), rows), :]
        lasts.append(w.send(stage.at[pl.ds(pl.multiple_of(rows * (1 - core), 8), rows), :], out.at[:, cols], w.partner()))
    arrived(lasts)
    w.drain()


def scatter_all(gqkv, gout, gup, gdown, sums):
    dims = [(3072, 128), (3072, 256)] + [(768, HALF)] * 8
    return pl.pallas_call(
        scatter_kernel,
        out_shape=(
            jax.ShapeDtypeStruct((24, 2304), F32),
            jax.ShapeDtypeStruct((24, 768), F32),
            jax.ShapeDtypeStruct((24, 3072), F32),
            jax.ShapeDtypeStruct((96, 768), F32),
            jax.ShapeDtypeStruct((16, 768), F32),
        ),
        in_specs=[pl.BlockSpec(memory_space=pl.ANY)] * 4 + [pl.BlockSpec(memory_space=pltpu.VMEM)],
        out_specs=[pl.BlockSpec(memory_space=pltpu.VMEM)] * 5,
        scratch_shapes=[
            pltpu.VMEM((768, 2304), BF),
            pltpu.VMEM((768, 768), BF),
            pltpu.VMEM((768, 3072), BF),
            pltpu.VMEM((3072, 768), BF),
        ]
        + [pltpu.VMEM(d, BF) for d in dims]
        + [pltpu.VMEM((d[0] // 2, d[1]), BF) for d in dims]
        + [pltpu.VMEM((d[0] // 4, d[1]), BF) for d in dims]
        + [pltpu.VMEM((3, d[0] // 16, d[1]), BF) for d in dims]
        + [
            pltpu.VMEM((8, 48, HALF), F32),
            pltpu.VMEM((2, 192, 256), F32),
            pltpu.VMEM((16, HALF), F32),
            pltpu.VMEM((16, HALF), F32),
            pltpu.VMEM((16, HALF), F32),
            pltpu.VMEM((6, 16, HALF), F32),
            pltpu.VMEM((16, 768), F32),
            pltpu.SemaphoreType.DMA((4,)),
            pltpu.SemaphoreType.DMA((128,)),
            pltpu.SemaphoreType.DMA((128,)),
        ],
        compiler_params=pltpu.CompilerParams(collective_id=1, has_side_effects=True, vmem_limit_bytes=LIMIT),
    )(gqkv, gout, gup, gdown, sums)


def plain_device(
    tokens,
    cotangent,
    segment_ids,
    live_mask,
    predicted,
    targets,
    w_qkv,
    bias_query,
    bias_value,
    w_out,
    bias_out,
    gain_attn,
    shift_attn,
    w_up,
    bias_up,
    w_down,
    bias_down,
    gain_ffn,
    shift_ffn,
):
    row_count, seq_len = segment_ids.shape
    classes = jnp.arange(CLASSES, dtype=jnp.int32)
    live_flat = live_mask.reshape(-1) == 1
    target_hits = (targets[:, None] == classes[None, :]) & live_flat[:, None]
    correct = target_hits & (predicted[:, None] == targets[:, None])
    local_tally = jnp.stack(
        [jnp.sum(correct, axis=0, dtype=jnp.int32), jnp.sum(target_hits, axis=0, dtype=jnp.int32)]
    )
    tallies = lax.psum(local_tally, ("dp", "fsdp"))
    (
        whole_qkv,
        whole_query_bias,
        whole_value_bias,
        whole_out,
        whole_out_bias,
        whole_gain_attn,
        whole_shift_attn,
        whole_up,
        whole_up_bias,
        whole_down,
        whole_down_bias,
        whole_gain_ffn,
        whole_shift_ffn,
    ) = (
        lax.all_gather(w_qkv, ("dp", "fsdp"), axis=0, tiled=True),
        lax.all_gather(bias_query, ("dp", "fsdp"), axis=0, tiled=True),
        lax.all_gather(bias_value, ("dp", "fsdp"), axis=0, tiled=True),
        lax.all_gather(w_out, ("dp", "fsdp"), axis=0, tiled=True),
        lax.all_gather(bias_out, ("dp", "fsdp"), axis=0, tiled=True),
        lax.all_gather(gain_attn, ("dp", "fsdp"), axis=0, tiled=True),
        lax.all_gather(shift_attn, ("dp", "fsdp"), axis=0, tiled=True),
        lax.all_gather(w_up, ("dp", "fsdp"), axis=0, tiled=True),
        lax.all_gather(bias_up, ("dp", "fsdp"), axis=0, tiled=True),
        lax.all_gather(w_down, ("dp", "fsdp"), axis=0, tiled=True),
        lax.all_gather(bias_down, ("dp", "fsdp"), axis=0, tiled=True),
        lax.all_gather(gain_ffn, ("dp", "fsdp"), axis=0, tiled=True),
        lax.all_gather(shift_ffn, ("dp", "fsdp"), axis=0, tiled=True),
    )
    projected = jnp.dot(tokens, whole_qkv, preferred_element_type=jnp.float32)
    queries = (projected[:, :D] + whole_query_bias.astype(jnp.float32)).astype(jnp.bfloat16)
    keys_part = projected[:, D : 2 * D].astype(jnp.bfloat16)
    values = (projected[:, 2 * D :] + whole_value_bias.astype(jnp.float32)).astype(jnp.bfloat16)
    query_heads = split_heads(queries, row_count, seq_len)
    key_heads = split_heads(keys_part, row_count, seq_len)
    value_heads = split_heads(values, row_count, seq_len)
    diagonal = jnp.eye(seq_len, dtype=bool)
    allowed = (segment_ids[:, :, None] == segment_ids[:, None, :]) & (
        (live_mask[:, None, :] == 1) | diagonal[None]
    )
    scores = masked_scores(query_heads, key_heads, allowed)
    highest = jnp.max(scores, axis=-1, keepdims=True)
    raised = jnp.exp(scores - highest)
    total = jnp.sum(raised, axis=-1, keepdims=True)
    soft_weights = raised / total
    log_total = highest + jnp.log(total)
    context = (
        jnp.einsum(
            "bhqk,bkhc->bqhc",
            soft_weights.astype(jnp.bfloat16),
            value_heads,
            preferred_element_type=jnp.float32,
        )
        .reshape(-1, D)
        .astype(jnp.bfloat16)
    )
    attended = jnp.dot(
        context, whole_out, preferred_element_type=jnp.float32
    ) + whole_out_bias.astype(jnp.float32)
    hidden, normed_one, inverse_one = normalize(
        tokens.astype(jnp.float32) + attended,
        whole_gain_attn.astype(jnp.float32),
        whole_shift_attn.astype(jnp.float32),
    )
    hidden_low = hidden.astype(jnp.bfloat16)
    up_value = jnp.dot(
        hidden_low, whole_up, preferred_element_type=jnp.float32
    ) + whole_up_bias.astype(jnp.float32)
    activated_low = jax.nn.gelu(up_value, approximate=False).astype(jnp.bfloat16)
    ffn_out = jnp.dot(
        activated_low, whole_down, preferred_element_type=jnp.float32
    ) + whole_down_bias.astype(jnp.float32)
    layer_out, normed_two, inverse_two = normalize(
        hidden + ffn_out, whole_gain_ffn.astype(jnp.float32), whole_shift_ffn.astype(jnp.float32)
    )
    back_qkv, back_out, back_up, back_down, back_gain_attn, back_gain_ffn = (
        lax.all_gather(w_qkv, ("dp", "fsdp"), axis=0, tiled=True),
        lax.all_gather(w_out, ("dp", "fsdp"), axis=0, tiled=True),
        lax.all_gather(w_up, ("dp", "fsdp"), axis=0, tiled=True),
        lax.all_gather(w_down, ("dp", "fsdp"), axis=0, tiled=True),
        lax.all_gather(gain_attn, ("dp", "fsdp"), axis=0, tiled=True),
        lax.all_gather(gain_ffn, ("dp", "fsdp"), axis=0, tiled=True),
    )
    upstream = cotangent.astype(jnp.float32)
    grad_gain_ffn = jnp.sum(upstream * normed_two, axis=0)
    grad_shift_ffn = jnp.sum(upstream, axis=0)
    d_resid_two = normalize_back(
        upstream, normed_two, inverse_two, back_gain_ffn.astype(jnp.float32)
    )
    d_two_low = d_resid_two.astype(jnp.bfloat16)
    grad_down = contract_rows(activated_low, d_two_low)
    grad_down_bias = jnp.sum(d_resid_two, axis=0)
    d_activated = times_transposed(d_two_low, back_down)
    gelu_pullback = jax.vjp(partial(jax.nn.gelu, approximate=False), up_value)[1]
    d_up = gelu_pullback(d_activated)[0].astype(jnp.bfloat16)
    grad_up_bias = jnp.sum(d_up.astype(jnp.float32), axis=0)
    grad_up = contract_rows(hidden_low, d_up)
    d_hidden = d_resid_two + times_transposed(d_up, back_up)
    grad_gain_attn = jnp.sum(d_hidden * normed_one, axis=0)
    grad_shift_attn = jnp.sum(d_hidden, axis=0)
    d_resid_one = normalize_back(
        d_hidden, normed_one, inverse_one, back_gain_attn.astype(jnp.float32)
    )
    d_one_low = d_resid_one.astype(jnp.bfloat16)
    grad_out_bias = jnp.sum(d_resid_one, axis=0)
    grad_out = contract_rows(context, d_one_low)
    d_context = times_transposed(d_one_low, back_out).astype(jnp.bfloat16)
    d_context_heads = split_heads(d_context, row_count, seq_len)
    d_soft = jnp.einsum(
        "bqhc,bkhc->bhqk", d_context_heads, value_heads, preferred_element_type=jnp.float32
    )
    soft_again = jnp.exp(masked_scores(query_heads, key_heads, allowed) - log_total)
    d_values = (
        jnp.einsum(
            "bhqk,bqhc->bkhc",
            soft_again.astype(jnp.bfloat16),
            d_context_heads,
            preferred_element_type=jnp.float32,
        )
        .reshape(-1, D)
        .astype(jnp.bfloat16)
    )
    inner = jnp.sum(soft_again * d_soft, axis=-1, keepdims=True)
    d_scores = (soft_again * (d_soft - inner)).astype(jnp.bfloat16)
    d_queries = (
        (
            jnp.einsum("bhqk,bkhc->bqhc", d_scores, key_heads, preferred_element_type=jnp.float32)
            * HEAD_DIM ** (-0.5)
        )
        .reshape(-1, D)
        .astype(jnp.bfloat16)
    )
    d_keys = (
        (
            jnp.einsum("bhqk,bqhc->bkhc", d_scores, query_heads, preferred_element_type=jnp.float32)
            * HEAD_DIM ** (-0.5)
        )
        .reshape(-1, D)
        .astype(jnp.bfloat16)
    )
    d_projected = jnp.concatenate([d_queries, d_keys, d_values], axis=1)
    grad_query_bias = jnp.sum(d_queries.astype(jnp.float32), axis=0)
    grad_value_bias = jnp.sum(d_values.astype(jnp.float32), axis=0)
    grad_qkv = contract_rows(tokens, d_projected)
    grad_tokens = d_resid_one + times_transposed(d_projected, back_qkv)
    summed = tuple(
        (
            lax.psum_scatter(grad_qkv, ("dp", "fsdp"), scatter_dimension=0, tiled=True),
            lax.psum_scatter(grad_query_bias, ("dp", "fsdp"), scatter_dimension=0, tiled=True),
            lax.psum_scatter(grad_value_bias, ("dp", "fsdp"), scatter_dimension=0, tiled=True),
            lax.psum_scatter(grad_out, ("dp", "fsdp"), scatter_dimension=0, tiled=True),
            lax.psum_scatter(grad_out_bias, ("dp", "fsdp"), scatter_dimension=0, tiled=True),
            lax.psum_scatter(grad_gain_attn, ("dp", "fsdp"), scatter_dimension=0, tiled=True),
            lax.psum_scatter(grad_shift_attn, ("dp", "fsdp"), scatter_dimension=0, tiled=True),
            lax.psum_scatter(grad_up, ("dp", "fsdp"), scatter_dimension=0, tiled=True),
            lax.psum_scatter(grad_up_bias, ("dp", "fsdp"), scatter_dimension=0, tiled=True),
            lax.psum_scatter(grad_down, ("dp", "fsdp"), scatter_dimension=0, tiled=True),
            lax.psum_scatter(grad_down_bias, ("dp", "fsdp"), scatter_dimension=0, tiled=True),
            lax.psum_scatter(grad_gain_ffn, ("dp", "fsdp"), scatter_dimension=0, tiled=True),
            lax.psum_scatter(grad_shift_ffn, ("dp", "fsdp"), scatter_dimension=0, tiled=True),
        )
    )
    return (layer_out.astype(jnp.bfloat16), grad_tokens) + summed + (tallies,)


def fast_device(
    tokens,
    cotangent,
    segment_ids,
    live_mask,
    predicted,
    targets,
    w_qkv,
    bias_query,
    bias_value,
    w_out,
    bias_out,
    gain_attn,
    shift_attn,
    w_up,
    bias_up,
    w_down,
    bias_down,
    gain_ffn,
    shift_ffn,
):
    row_count, seq_len = segment_ids.shape
    classes = jnp.arange(CLASSES, dtype=jnp.int32)
    live_flat = live_mask.reshape(-1) == 1
    target_hits = (targets[:, None] == classes[None, :]) & live_flat[:, None]
    correct = target_hits & (predicted[:, None] == targets[:, None])
    local_tally = jnp.stack(
        [jnp.sum(correct, axis=0, dtype=jnp.int32), jnp.sum(target_hits, axis=0, dtype=jnp.int32)]
    )
    small = jnp.stack([bias_query, bias_value, bias_out, gain_attn, shift_attn, bias_down, gain_ffn, shift_ffn]).astype(F32)
    vec = jnp.concatenate([small, jnp.zeros((8, 8), F32), jnp.pad(bias_up.astype(F32)[None], ((0, 7), (0, 0)))], axis=1)
    whole_qkv, whole_out, whole_up, whole_down, vecs = gather_all(w_qkv, w_out, w_up, w_down, vec)
    vecs = vecs.reshape(32, 8, 128)
    lines = vecs[:, :, :24].transpose(1, 0, 2).reshape(8, 768).astype(jnp.bfloat16)
    (
        whole_query_bias,
        whole_value_bias,
        whole_out_bias,
        whole_gain_attn,
        whole_shift_attn,
        whole_down_bias,
        whole_gain_ffn,
        whole_shift_ffn,
    ) = [lines[i] for i in range(8)]
    whole_up_bias = vecs[:, 0, 32:].reshape(3072).astype(jnp.bfloat16)
    projected = jnp.dot(tokens, whole_qkv, preferred_element_type=jnp.float32)
    queries = (projected[:, :D] + whole_query_bias.astype(jnp.float32)).astype(jnp.bfloat16)
    keys_part = projected[:, D : 2 * D].astype(jnp.bfloat16)
    values = (projected[:, 2 * D :] + whole_value_bias.astype(jnp.float32)).astype(jnp.bfloat16)
    query_heads = split_heads(queries, row_count, seq_len)
    key_heads = split_heads(keys_part, row_count, seq_len)
    value_heads = split_heads(values, row_count, seq_len)
    diagonal = jnp.eye(seq_len, dtype=bool)
    allowed = (segment_ids[:, :, None] == segment_ids[:, None, :]) & (
        (live_mask[:, None, :] == 1) | diagonal[None]
    )
    scores = masked_scores(query_heads, key_heads, allowed)
    highest = jnp.max(scores, axis=-1, keepdims=True)
    raised = jnp.exp(scores - highest)
    total = jnp.sum(raised, axis=-1, keepdims=True)
    soft_weights = raised / total
    log_total = highest + jnp.log(total)
    context = (
        jnp.einsum(
            "bhqk,bkhc->bqhc",
            soft_weights.astype(jnp.bfloat16),
            value_heads,
            preferred_element_type=jnp.float32,
        )
        .reshape(-1, D)
        .astype(jnp.bfloat16)
    )
    attended = jnp.dot(
        context, whole_out, preferred_element_type=jnp.float32
    ) + whole_out_bias.astype(jnp.float32)
    hidden, normed_one, inverse_one = normalize(
        tokens.astype(jnp.float32) + attended,
        whole_gain_attn.astype(jnp.float32),
        whole_shift_attn.astype(jnp.float32),
    )
    hidden_low = hidden.astype(jnp.bfloat16)
    up_value = jnp.dot(
        hidden_low, whole_up, preferred_element_type=jnp.float32
    ) + whole_up_bias.astype(jnp.float32)
    activated_low = jax.nn.gelu(up_value, approximate=False).astype(jnp.bfloat16)
    ffn_out = jnp.dot(
        activated_low, whole_down, preferred_element_type=jnp.float32
    ) + whole_down_bias.astype(jnp.float32)
    layer_out, normed_two, inverse_two = normalize(
        hidden + ffn_out, whole_gain_ffn.astype(jnp.float32), whole_shift_ffn.astype(jnp.float32)
    )
    back_qkv, back_out, back_up, back_down, back_gain_attn, back_gain_ffn = whole_qkv, whole_out, whole_up, whole_down, whole_gain_attn, whole_gain_ffn
    upstream = cotangent.astype(jnp.float32)
    grad_gain_ffn = jnp.sum(upstream * normed_two, axis=0)
    grad_shift_ffn = jnp.sum(upstream, axis=0)
    d_resid_two = normalize_back(
        upstream, normed_two, inverse_two, back_gain_ffn.astype(jnp.float32)
    )
    d_two_low = d_resid_two.astype(jnp.bfloat16)
    grad_down = contract_rows(activated_low, d_two_low)
    grad_down_bias = jnp.sum(d_resid_two, axis=0)
    d_activated = times_transposed(d_two_low, back_down)
    gelu_pullback = jax.vjp(partial(jax.nn.gelu, approximate=False), up_value)[1]
    d_up = gelu_pullback(d_activated)[0].astype(jnp.bfloat16)
    grad_up_bias = jnp.sum(d_up.astype(jnp.float32), axis=0)
    grad_up = contract_rows(hidden_low, d_up)
    d_hidden = d_resid_two + times_transposed(d_up, back_up)
    grad_gain_attn = jnp.sum(d_hidden * normed_one, axis=0)
    grad_shift_attn = jnp.sum(d_hidden, axis=0)
    d_resid_one = normalize_back(
        d_hidden, normed_one, inverse_one, back_gain_attn.astype(jnp.float32)
    )
    d_one_low = d_resid_one.astype(jnp.bfloat16)
    grad_out_bias = jnp.sum(d_resid_one, axis=0)
    grad_out = contract_rows(context, d_one_low)
    d_context = times_transposed(d_one_low, back_out).astype(jnp.bfloat16)
    d_context_heads = split_heads(d_context, row_count, seq_len)
    d_soft = jnp.einsum(
        "bqhc,bkhc->bhqk", d_context_heads, value_heads, preferred_element_type=jnp.float32
    )
    soft_again = jnp.exp(masked_scores(query_heads, key_heads, allowed) - log_total)
    d_values = (
        jnp.einsum(
            "bhqk,bqhc->bkhc",
            soft_again.astype(jnp.bfloat16),
            d_context_heads,
            preferred_element_type=jnp.float32,
        )
        .reshape(-1, D)
        .astype(jnp.bfloat16)
    )
    inner = jnp.sum(soft_again * d_soft, axis=-1, keepdims=True)
    d_scores = (soft_again * (d_soft - inner)).astype(jnp.bfloat16)
    d_queries = (
        (
            jnp.einsum("bhqk,bkhc->bqhc", d_scores, key_heads, preferred_element_type=jnp.float32)
            * HEAD_DIM ** (-0.5)
        )
        .reshape(-1, D)
        .astype(jnp.bfloat16)
    )
    d_keys = (
        (
            jnp.einsum("bhqk,bqhc->bkhc", d_scores, query_heads, preferred_element_type=jnp.float32)
            * HEAD_DIM ** (-0.5)
        )
        .reshape(-1, D)
        .astype(jnp.bfloat16)
    )
    d_projected = jnp.concatenate([d_queries, d_keys, d_values], axis=1)
    grad_query_bias = jnp.sum(d_queries.astype(jnp.float32), axis=0)
    grad_value_bias = jnp.sum(d_values.astype(jnp.float32), axis=0)
    grad_qkv = contract_rows(tokens, d_projected)
    grad_tokens = d_resid_one + times_transposed(d_projected, back_qkv)
    sums = jnp.concatenate(
        [
            jnp.stack(
                [grad_query_bias, grad_value_bias, grad_out_bias, grad_gain_attn, grad_shift_attn, grad_down_bias, grad_gain_ffn, grad_shift_ffn]
            ),
            grad_up_bias.reshape(4, 768),
            jnp.pad(local_tally.astype(F32).reshape(1, 48), ((0, 0), (0, 720))),
            jnp.zeros((3, 768), F32),
        ]
    )
    sqkv, sout, sup, sdown, sums = scatter_all(
        grad_qkv.astype(BF), grad_out.astype(BF), grad_up.astype(BF), grad_down.astype(BF), sums
    )
    index = lax.axis_index("dp") * 8 + lax.axis_index("fsdp")
    lines = lax.dynamic_slice(sums[:8], (0, index * 24), (8, 24))
    up_line = lax.dynamic_slice(sums[8:12].reshape(3072), (index * 96,), (96,))
    tallies = sums[12, :48].reshape(2, 24).astype(jnp.int32)
    return (
        layer_out.astype(jnp.bfloat16), grad_tokens, sqkv, lines[0], lines[1], sout, lines[2], lines[3], lines[4], sup, up_line, sdown,
        lines[5], lines[6], lines[7], tallies,
    )


def solution(mesh):
    in_specs = (
        P(("dp", "fsdp"), None),
        P(("dp", "fsdp"), None),
        P(("dp", "fsdp"), None),
        P(("dp", "fsdp"), None),
        P(("dp", "fsdp")),
        P(("dp", "fsdp")),
        P(("dp", "fsdp"), None),
        P(("dp", "fsdp")),
        P(("dp", "fsdp")),
        P(("dp", "fsdp"), None),
        P(("dp", "fsdp")),
        P(("dp", "fsdp")),
        P(("dp", "fsdp")),
        P(("dp", "fsdp"), None),
        P(("dp", "fsdp")),
        P(("dp", "fsdp"), None),
        P(("dp", "fsdp")),
        P(("dp", "fsdp")),
        P(("dp", "fsdp")),
    )
    out_specs = (
        P(("dp", "fsdp"), None),
        P(("dp", "fsdp"), None),
        P(("dp", "fsdp"), None),
        P(("dp", "fsdp")),
        P(("dp", "fsdp")),
        P(("dp", "fsdp"), None),
        P(("dp", "fsdp")),
        P(("dp", "fsdp")),
        P(("dp", "fsdp")),
        P(("dp", "fsdp"), None),
        P(("dp", "fsdp")),
        P(("dp", "fsdp"), None),
        P(("dp", "fsdp")),
        P(("dp", "fsdp")),
        P(("dp", "fsdp")),
        P(),
    )
    fast = tuple(mesh.shape.items()) == (("dp", 4), ("fsdp", 8))
    return jax.shard_map(
        fast_device if fast else plain_device, mesh=mesh, in_specs=in_specs, out_specs=out_specs, check_vma=False
    )
```

```python
from functools import partial

import jax
import jax.numpy as jnp
import numpy as np
from jax import lax
from jax.experimental import pallas as pl
from jax.experimental.pallas import tpu as pltpu
from jax.sharding import PartitionSpec as P

D = 768
HEADS = 12
HEAD_DIM = 64
CLASSES = 24


EPSILON = 1e-05


def normalize(operand, scale_vec, shift_vec):
    center = operand - jnp.mean(operand, axis=-1, keepdims=True)
    inverse = lax.rsqrt(jnp.mean(center * center, axis=-1, keepdims=True) + EPSILON)
    normed = center * inverse
    return (normed * scale_vec + shift_vec, normed, inverse)


def normalize_back(grad_out, normed, inverse, scale_vec):
    scaled = grad_out * scale_vec
    return inverse * (
        scaled
        - jnp.mean(scaled, axis=-1, keepdims=True)
        - normed * jnp.mean(scaled * normed, axis=-1, keepdims=True)
    )


def contract_rows(left, right):
    return lax.dot_general(
        left, right, (((0,), (0,)), ((), ())), preferred_element_type=jnp.float32
    )


def times_transposed(left, right):
    return lax.dot_general(
        left, right, (((1,), (1,)), ((), ())), preferred_element_type=jnp.float32
    )


def split_heads(matrix, row_count, seq_len):
    return matrix.reshape(row_count, seq_len, HEADS, HEAD_DIM)


def masked_scores(query_heads, key_heads, allowed):
    scores = jnp.einsum(
        "bqhc,bkhc->bhqk", query_heads, key_heads, preferred_element_type=jnp.float32
    ) * HEAD_DIM ** (-0.5)
    return jnp.where(allowed[:, None], scores, -1000000000.0)


MESH = pl.DeviceIdType.MESH
BF = jnp.bfloat16
F32 = jnp.float32
HALF = 384


def place():
    dp, fsdp = lax.axis_index("dp"), lax.axis_index("fsdp")
    return dp // 2, dp % 2, fsdp // 2, fsdp % 2


class Wires:
    def __init__(self, send_sems, recv_sems):
        self.y, self.x, self.z, self.core = place()
        self.plane = self.y * 2 + self.x
        self.chip = self.plane * 4 + self.z
        self.send_sems, self.recv_sems, self.used, self.open = send_sems, recv_sems, 0, []

    def device(self, y=None, x=None, z=None, core=None):
        y = self.y if y is None else y
        x = self.x if x is None else x
        z = self.z if z is None else z
        core = self.core if core is None else core
        return (y * 2 + x, z * 2 + core)

    def partner(self):
        return self.device(core=1 - self.core)

    def over_x(self):
        return self.device(x=1 - self.x)

    def over_y(self):
        return self.device(y=1 - self.y)

    def along_z(self, jump):
        return self.device(z=(self.z + jump) % 4)

    def barrier(self):
        semaphore = pltpu.get_barrier_semaphore()
        peers = [self.partner(), self.over_x(), self.over_y()] + [self.along_z(j) for j in (1, 2, 3)]
        for peer in peers:
            pl.semaphore_signal(semaphore, inc=1, device_id=peer, device_id_type=MESH)
        pl.semaphore_wait(semaphore, 6)

    def send(self, source, target, device):
        number = self.used
        self.used += 1
        copy = pltpu.make_async_remote_copy(
            src_ref=source,
            dst_ref=target,
            send_sem=self.send_sems.at[number],
            recv_sem=self.recv_sems.at[number],
            device_id=device,
            device_id_type=MESH,
        )
        copy.start()
        self.open.append(copy)
        return copy

    def drain(self):
        for copy in self.open:
            copy.wait_send()
        self.open = []


def arrived(copies):
    for copy in copies:
        copy.wait_recv()


def rows_at(start, count, slab):
    return pl.ds(pl.multiple_of(start * slab, 16), count * slab)


class Piece:
    at = 0

    def step(self):
        self.steps[self.at]()
        self.at += 1


class Gather(Piece):
    def __init__(self, wires, ref, slab, first, width, order):
        self.w, self.ref, self.slab, self.width, self.first = wires, ref, slab, width, first
        self.back = []
        self.steps = {
            "A": [self.z0, self.a1, self.a2, self.a3],
            "B": [self.z0, self.b1, self.b2, self.b3],
            "C": [self.c0, self.c1, self.c2, self.c3],
        }[order] + [self.done]

    def send(self, slabs, count, device):
        part = self.ref.at[rows_at(slabs, count, self.slab), pl.ds(pl.multiple_of(self.first, 128), self.width)]
        return self.w.send(part, part, device)

    def hand(self, slabs, count):
        self.back.append(self.send(slabs, count, self.w.partner()))

    def z0(self):
        self.into = [self.send(self.w.chip, 1, self.w.along_z(j)) for j in (1, 2, 3)]

    def a1(self):
        w = self.w
        arrived(self.into)
        self.into = [self.send(w.plane * 4, 4, w.over_x())]
        self.hand(w.plane * 4, 4)

    def a2(self):
        w = self.w
        arrived(self.into)
        self.into = [self.send(w.y * 8, 8, w.over_y())]
        self.hand((w.y * 2 + 1 - w.x) * 4, 4)

    def a3(self):
        arrived(self.into)
        self.hand((1 - self.w.y) * 8, 8)

    def b1(self):
        w = self.w
        arrived(self.into)
        self.into = [self.send(w.plane * 4, 4, w.over_y())]
        self.hand(w.plane * 4, 4)

    def b2(self):
        w = self.w
        arrived(self.into)
        other = ((1 - w.y) * 2 + w.x) * 4
        self.into = [self.send(w.plane * 4, 4, w.over_x()), self.send(other, 4, w.over_x())]
        self.hand(other, 4)

    def b3(self):
        w = self.w
        arrived(self.into)
        for y in (0, 1):
            self.hand((y * 2 + 1 - w.x) * 4, 4)

    def c0(self):
        self.into = [self.send(self.w.chip, 1, self.w.over_x())]

    def c1(self):
        w = self.w
        arrived(self.into)
        self.into = [self.send((w.y * 2 + x) * 4 + w.z, 1, w.over_y()) for x in (0, 1)]

    def c2(self):
        w = self.w
        arrived(self.into)
        self.into = [self.send(plane * 4 + w.z, 1, w.along_z(j)) for j in (1, 2, 3) for plane in range(4)]
        for plane in range(4):
            self.hand(plane * 4 + w.z, 1)

    def c3(self):
        w = self.w
        arrived(self.into)
        for j in (1, 2, 3):
            for plane in range(4):
                self.hand(plane * 4 + (w.z + j) % 4, 1)

    def done(self):
        arrived(self.back)


def add_rows(target, first, count, source, start):
    tile = 96

    def body(i, carry):
        there = pl.ds(pl.multiple_of(first + i * tile, 16), tile)
        target[there, :] = target[there, :] + source[pl.ds(pl.multiple_of(start + i * tile, 16), tile), :]
        return carry

    lax.fori_loop(0, count // tile, body, 0)


class Scatter(Piece):
    def __init__(self, wires, ref, slab, first, far, width, order, p, r1, r2, rz, whole, total, last, write, gate):
        self.w, self.ref, self.slab, self.first, self.far, self.width = wires, ref, slab, first, far, width
        self.p, self.r1, self.r2, self.rz, self.whole, self.total, self.last, self.write, self.gate = p, r1, r2, rz, whole, total, last, write, gate
        self.mine = ref.at[:, pl.ds(pl.multiple_of(first, 128), width)]
        self.steps = {
            "A": [self.p0, self.a1, self.a2, self.a3, self.z4],
            "B": [self.p0, self.b1, self.b2, self.b3, self.z4],
            "C": [self.p0, self.c1, self.c2, self.c3, self.c4],
        }[order] + [self.done]

    def rows(self, slabs, count):
        return self.ref.at[rows_at(slabs, count, self.slab), pl.ds(pl.multiple_of(self.first, 128), self.width)]

    def slot(self, buffer, slabs, count):
        return buffer.at[pl.ds(slabs * self.slab, count * self.slab), :]

    def add(self, slabs, count, source, start):
        add_rows(self.mine, slabs * self.slab, count * self.slab, source, start * self.slab)

    def p0(self):
        far = self.ref.at[:, pl.ds(pl.multiple_of(self.far, 128), self.width)]
        if self.ref.shape[0] != 16 * self.slab:
            far = self.ref.at[0 : 16 * self.slab, pl.ds(pl.multiple_of(self.far, 128), self.width)]
        self.into = [self.w.send(far, self.p, self.w.partner())]

    def a1(self):
        w = self.w
        self.gate()
        arrived(self.into)
        self.add((1 - w.y) * 8, 8, self.p, (1 - w.y) * 8)
        self.into = [w.send(self.rows((1 - w.y) * 8, 8), self.r1, w.over_y())]
        self.add(w.y * 8, 8, self.p, w.y * 8)

    def a2(self):
        w = self.w
        arrived(self.into)
        other = (w.y * 2 + 1 - w.x) * 4
        self.add(other, 4, self.r1, (1 - w.x) * 4)
        self.into = [w.send(self.rows(other, 4), self.r2, w.over_x())]
        self.add(w.plane * 4, 4, self.r1, w.x * 4)

    def a3(self):
        arrived(self.into)
        self.z3()

    def b1(self):
        w = self.w
        self.gate()
        arrived(self.into)
        self.into = []
        for y in (0, 1):
            slabs = (y * 2 + 1 - w.x) * 4
            self.add(slabs, 4, self.p, slabs)
            self.into.append(w.send(self.rows(slabs, 4), self.slot(self.r1, y * 4, 4), w.over_x()))
        for y in (0, 1):
            slabs = (y * 2 + w.x) * 4
            self.add(slabs, 4, self.p, slabs)

    def b2(self):
        w = self.w
        arrived(self.into)
        other = ((1 - w.y) * 2 + w.x) * 4
        self.add(other, 4, self.r1, (1 - w.y) * 4)
        self.into = [w.send(self.rows(other, 4), self.r2, w.over_y())]
        self.add(w.plane * 4, 4, self.r1, w.y * 4)

    def b3(self):
        arrived(self.into)
        self.z3()

    def z3(self):
        w = self.w
        self.add(w.plane * 4, 4, self.r2, 0)
        self.into = []
        for j in (1, 2, 3):
            there = (w.z + j) % 4
            self.into.append(w.send(self.rows(w.plane * 4 + there, 1), self.slot(self.rz, j - 1, 1), w.along_z(j)))

    def z4(self):
        arrived(self.into)
        self.close([self.slot(self.rz, j, 1) for j in range(3)])

    def c1(self):
        w = self.w
        self.gate()
        arrived(self.into)
        self.add(0, 16, self.p, 0)
        self.into = []
        for j in (1, 2, 3):
            for plane in range(4):
                there = self.rows(plane * 4 + (w.z + j) % 4, 1)
                self.into.append(w.send(there, self.slot(self.rz, (j - 1) * 4 + plane, 1), w.along_z(j)))

    def c2(self):
        w = self.w
        arrived(self.into)
        for plane in range(4):
            for j in range(3):
                self.add(plane * 4 + w.z, 1, self.rz, j * 4 + plane)
        self.into = []
        for x in (0, 1):
            there = self.rows(((1 - w.y) * 2 + x) * 4 + w.z, 1)
            self.into.append(w.send(there, self.slot(self.r1, x, 1), w.over_y()))

    def c3(self):
        w = self.w
        arrived(self.into)
        for x in (0, 1):
            self.add((w.y * 2 + x) * 4 + w.z, 1, self.r1, x)
        self.into = [w.send(self.rows((w.y * 2 + 1 - w.x) * 4 + w.z, 1), self.slot(self.r2, 0, 1), w.over_x())]

    def c4(self):
        arrived(self.into)
        self.close([self.slot(self.r2, 0, 1)])

    def close(self, others):
        w = self.w
        total = self.rows(w.chip, 1)[...].astype(F32)
        for other in others:
            total = total + other[...].astype(F32)
        self.whole[...] = total
        half = self.slab // 2
        self.total[...] = self.whole[pl.ds(pl.multiple_of((1 - w.core) * half, 8), half), :]
        self.into = [w.send(self.total, self.last, w.partner())]
        self.write(w.core, self.whole[pl.ds(pl.multiple_of(w.core * half, 8), half), :])

    def done(self):
        arrived(self.into)
        self.write(1 - self.w.core, self.last[...])


class Spread(Piece):
    def __init__(self, wires, tiles):
        self.w, self.tiles = wires, tiles
        self.steps = [self.s0, self.s1, self.s2, self.s3, self.s4]

    def send(self, start, count, device):
        part = self.tiles.at[pl.ds(pl.multiple_of(start * 8, 8), count * 8), :]
        return self.w.send(part, part, device)

    def s0(self):
        w = self.w
        self.into = [self.send(w.chip * 2 + w.core, 1, w.partner())]

    def s1(self):
        w = self.w
        arrived(self.into)
        self.into = [self.send(w.chip * 2, 2, w.along_z(j)) for j in (1, 2, 3)]

    def s2(self):
        arrived(self.into)
        self.into = [self.send(self.w.plane * 8, 8, self.w.over_x())]

    def s3(self):
        arrived(self.into)
        self.into = [self.send(self.w.y * 16, 16, self.w.over_y())]

    def s4(self):
        arrived(self.into)


class Sums(Piece):
    def __init__(self, wires, sums, stage, land, last):
        self.w, self.sums, self.stage, self.land, self.last = wires, sums, stage, land, last
        self.half = pl.ds(pl.multiple_of(wires.core * HALF, 128), HALF)
        self.steps = [self.s0, self.s1, self.s2, self.s3, self.s4, self.s5]

    def s0(self):
        far = pl.ds(pl.multiple_of((1 - self.w.core) * HALF, 128), HALF)
        self.into = [self.w.send(self.sums.at[:, far], self.land.at[0], self.w.partner())]

    def relay(self, value, at, device):
        self.stage[at] = value
        self.into = [self.w.send(self.stage.at[at], self.land.at[at + 1], device)]

    def s1(self):
        arrived(self.into)
        self.relay(self.sums[:, self.half] + self.land[0], 0, self.w.over_x())

    def s2(self):
        arrived(self.into)
        self.relay(self.stage[0] + self.land[1], 1, self.w.over_y())

    def s3(self):
        arrived(self.into)
        self.stage[2] = self.stage[1] + self.land[2]
        self.into = [self.w.send(self.stage.at[2], self.land.at[2 + j], self.w.along_z(j)) for j in (1, 2, 3)]

    def s4(self):
        arrived(self.into)
        self.stage[3] = self.stage[2] + self.land[3] + self.land[4] + self.land[5]
        self.last[:, self.half] = self.stage[3]
        self.into = [self.w.send(self.stage.at[3], self.last.at[:, self.half], self.w.partner())]

    def s5(self):
        arrived(self.into)


GATHER, SCATTER, SPREAD, SUMS, SEMAPHORES = 0, 20, 40, 41, 256
GATHER_ORDERS = "ABABABABABC"
SCATTER_ORDERS = "BABBABABCAB"
PLAN = (
    (),
    (40, 0),
    (1, 40, 2, 0, 40, 3, 1, 4, 40),
    (0, 2, 5, 1, 3, 6, 2, 4, 7, 0, 5, 8, 0),
    (),
    (1, 3, 6),
    (1,),
    (9, 4),
    (7,),
    (2, 10, 8, 2),
    (),
    (3, 5),
    (3,),
    (9,),
    (6, 10, 4, 4),
    (),
    (8, 7, 9, 5, 5),
    (),
    (6, 7, 6),
    (10, 7),
    (),
    (),
    (9, 8, 9, 8, 10, 10),
    (),
    (),
    (),
    (),
    (28,),
    (29,),
    (28, 29, 30),
    (),
    (),
    (30,),
    (),
    (24,),
    (25,),
    (24, 26, 29, 25),
    (26, 27),
    (30,),
    (27, 28, 24, 29),
    (),
    (),
    (23,),
    (25, 26),
    (23, 29),
    (),
    (20, 29, 30),
    (27, 28),
    (20,),
    (21, 24, 25),
    (),
    (),
    (21, 22, 26, 27, 30, 41),
    (24, 22, 30, 41),
    (23, 24, 25, 28),
    (),
    (25, 28, 26, 21, 26, 27, 20, 23, 27, 20, 22, 23, 41, 23, 21, 20, 22, 41, 20, 21, 21, 22, 22, 41, 41),
)


TOKENS = 1024
TILE = 256


def nn(left, right):
    return jnp.dot(left, right, preferred_element_type=F32)


def nt(left, right):
    return lax.dot_general(left, right, (((1,), (1,)), ((), ())), preferred_element_type=F32)


def tn(left, right):
    return lax.dot_general(left, right, (((0,), (0,)), ((), ())), preferred_element_type=F32)


def loop(start, stop, body):
    def step(i, carry):
        body(i)
        return carry

    lax.fori_loop(start, stop, step, 0)


def span(i, size):
    return slice(i * size, (i + 1) * size) if isinstance(i, int) else pl.ds(pl.multiple_of(i * size, size), size)


def row_sum(value):
    return jnp.sum(value, axis=0, keepdims=True)


def parts(value, size):
    return [(i, value[i : i + size]) for i in range(0, value.shape[0], size)]


def eight(value):
    return jnp.sum(value.reshape(value.shape[0] // 8, 8, value.shape[1]), axis=0)


def mean(value):
    return jnp.mean(value, axis=-1, keepdims=True)


def gelu_both(up):
    density = jnp.exp(up * up * -0.5)
    base = jnp.abs(up) * (0.3275911 * 0.5**0.5) + 1.0
    guess = pltpu.reciprocal(base, approx=True)
    t = guess * (2.0 - base * guess)
    poly = t * (0.127414796 + t * (-0.142248368 + t * (0.7107068705 + t * (-0.7265760135 + t * 0.5307027145))))
    tail = poly * density
    below = jnp.where(up >= 0, 1.0 - tail, tail)
    return up * below, below + up * density * 0.3989422804014327


class Layer:
    def __init__(self, **refs):
        self.__dict__.update(refs)

    def vectors(self):
        line = lambda i, n: self.lanes[i : i + 1, 0:n]
        place = lax.broadcasted_iota(jnp.int32, (128, 768), 0)
        hot = (place == line(0, 768)).astype(F32).astype(BF)
        spread = nn(self.vecs[...].astype(BF), hot).reshape(32, 8, 768)
        owner = lax.broadcasted_iota(jnp.int32, (32, 8, 768), 0)
        self.lines[...] = jnp.sum(jnp.where(owner == line(1, 768)[None], spread, 0.0), axis=0)
        nothing = jnp.zeros((1, 128), F32)
        for g in range(3):
            parts = []
            for p in (2 * g, 2 * g + 1):
                cols = slice(p * 128, (p + 1) * 128)
                parts += [self.lines[0:1, cols], nothing, self.lines[1:2, cols]]
            self.qkv_bias[g] = jnp.concatenate(parts, axis=1)
        firsts = self.vecs[pl.ds(0, 32, 8), :].astype(BF)
        for b in range(4):
            place = lax.broadcasted_iota(jnp.int32, (128, 768), 0)
            cols = slice(b * 768, (b + 1) * 768)
            hot = (place == self.lanes[2:3, cols] + 32).astype(F32).astype(BF)
            spread = nn(firsts, hot)
            owner = lax.broadcasted_iota(jnp.int32, (32, 768), 0)
            self.up_bias[b] = row_sum(jnp.where(owner == self.lanes[3:4, cols], spread, 0.0))

    def tally(self):
        which = lax.broadcasted_iota(jnp.int32, (128, 128), 0)
        total = jnp.zeros((128, 128), F32)
        for r in range(8):
            target, guess, live = (ref[r : r + 1, :] for ref in (self.targets, self.predicted, self.live))
            every = (which - 24 == target) & (live == 1)
            right = (which == target) & (live == 1) & (guess == target) & (which < 24)
            total += jnp.where(every | right, 1.0, 0.0)
        counts = nt(jnp.ones((8, 128), BF), total.astype(BF))
        self.sums[12:13, 0:128] = counts[0:1]

    def note(self, row, value, cols=slice(0, 768)):
        self.partial[8 * row : 8 * row + 8, cols] += value

    def fold(self):
        for row in range(12):
            self.sums[row : row + 1] = row_sum(self.partial[8 * row : 8 * row + 8])

    def project(self, g, i):
        rows = span(i, TILE)
        out = (nn(self.tokens[rows, :], self.wqkv[:, g * 768 : (g + 1) * 768]) + self.qkv_bias[g]).astype(BF)
        for h in (0, HALF):
            at = g * 768 + h
            self.qkv[rows, at : at + 128] = out[:, h : h + 128] * 0.125
            self.qkv[rows, at + 128 : at + HALF] = out[:, h + 128 : h + HALF]

    def halves(self, pair):
        left = lax.broadcasted_iota(jnp.int32, pair.shape, 1) < 64
        zero = jnp.zeros_like(pair)
        return jnp.concatenate([jnp.where(left, pair, zero), jnp.where(left, zero, pair)], axis=0)

    def chains(self, g, rows):
        return [(r, p, span(r, 128)) for r in rows for p in (2 * g, 2 * g + 1)]

    def part(self, p, rows, b):
        return self.qkv[rows, p * HALF + b * 128 : p * HALF + (b + 1) * 128]

    def attend(self, g, rows):
        eye = lax.broadcasted_iota(jnp.int32, (128, 128), 0) == lax.broadcasted_iota(jnp.int32, (128, 128), 1)
        allowed, probs = {}, []
        for r in rows:
            seg = jnp.broadcast_to(self.segments[r : r + 1, :].astype(F32), (128, 128))
            allowed[r] = (seg == seg.T) & ((self.live[r : r + 1, :] == 1) | eye)
        ones = jnp.ones((128, 128), BF)
        chains = self.chains(g, rows)
        scores = [nt(self.halves(self.part(p, where, 0)), self.part(p, where, 1)) for r, p, where in chains]
        for (r, p, where), score in zip(chains, scores):
            some = []
            for at, part in parts(score, 128):
                part = jnp.where(allowed[r], part, -1e9)
                raised = jnp.exp(part - jnp.max(part, axis=-1, keepdims=True))
                total = nn(raised.astype(BF), ones)
                guess = pltpu.reciprocal(total, approx=True)
                some.append((raised * (guess * (2.0 - total * guess))).astype(BF))
            self.probs[r, p * 256 : (p + 1) * 256, :] = jnp.concatenate(some, axis=0)
            probs.append(jnp.concatenate(some, axis=1))
        for (r, p, where), prob in zip(chains, probs):
            self.context[where, p * 128 : (p + 1) * 128] = nn(prob, self.halves(self.part(p, where, 2))).astype(BF)

    def out_project(self, i):
        rows = span(i, TILE)
        attended = nn(self.context[rows, :], self.wout[...])
        for at, part in parts(attended, 32):
            here = pl.ds(i * TILE + at, 32)
            resid = self.tokens[here, :].astype(F32) + (part + self.lines[2:3])
            center = resid - mean(resid)
            inverse = lax.rsqrt(mean(center * center) + EPSILON)
            normed = center * inverse
            self.normed[here, :] = normed.astype(BF)
            self.inverse[at : at + 32, i : i + 1] = inverse
            self.hidden[here, :] = (normed * self.lines[3:4] + self.lines[4:5]).astype(BF)

    def up(self, b, i, tile=512):
        rows = span(i, tile)
        for c in range(3):
            cols = slice(c * 256, (c + 1) * 256)
            up = nn(self.hidden[rows, :], self.wup[:, b * 768 + c * 256 : b * 768 + (c + 1) * 256])
            for at, part in parts(up, 32):
                here = pl.ds(i * tile + at, 32)
                act, slope = gelu_both(part + self.up_bias[b, :, cols])
                self.act[b, here, cols] = act.astype(BF)
                self.slope[b, here, cols] = slope.astype(BF)

    def down(self, i):
        rows = span(i, TILE)
        for c in range(3):
            cols = slice(c * 256, (c + 1) * 256)
            ffn = nn(self.act[0, rows, :], self.wdown[0:768, cols])
            for b in range(1, 4):
                ffn += nn(self.act[b, rows, :], self.wdown[b * 768 : (b + 1) * 768, cols])
            self.wide[rows, cols] = ffn
        totals = [jnp.zeros((8, 768), F32)] * 3
        for at in range(0, TILE, 32):
            here = pl.ds(i * TILE + at, 32)
            hidden = self.normed[here, :].astype(F32) * self.lines[3:4] + self.lines[4:5]
            resid = hidden + (self.wide[here, :] + self.lines[5:6])
            center = resid - mean(resid)
            inverse = lax.rsqrt(mean(center * center) + EPSILON)
            normed = center * inverse
            self.layer_out[here, :] = (normed * self.lines[6:7] + self.lines[7:8]).astype(BF)
            upstream = self.cotangent[here, :].astype(F32)
            scaled = upstream * self.lines[6:7]
            d_two = inverse * (scaled - mean(scaled) - normed * mean(scaled * normed))
            totals = [old + eight(new) for old, new in zip(totals, (d_two, upstream * normed, upstream))]
            self.wide[here, :] = d_two
            self.low[here, :] = d_two.astype(BF)
        for row, total in zip((5, 6, 7), totals):
            self.note(row, total)

    def grad_down(self, j):
        cols = slice(j * 256, (j + 1) * 256)
        for b in range(4):
            self.gdown[b * 768 : (b + 1) * 768, cols] = tn(self.act[b], self.low[:, cols]).astype(BF)

    def back_up(self, b, i, tile=512):
        rows = span(i, tile)
        for c in range(3):
            cols = slice(c * 256, (c + 1) * 256)
            d_act = nt(self.low[rows, :], self.wdown[b * 768 + c * 256 : b * 768 + (c + 1) * 256, :])
            total = jnp.zeros((8, 256), F32)
            for at, part in parts(d_act, 32):
                here = pl.ds(i * tile + at, 32)
                d_up = (part * self.slope[b, here, cols].astype(F32)).astype(BF)
                self.slope[b, here, cols] = d_up
                total += eight(d_up.astype(F32))
            self.note(8 + b, total, cols)

    def grad_up(self, b):
        for c in range(3):
            cols = slice(c * 256, (c + 1) * 256)
            self.act[b, 0:768, cols] = tn(self.hidden[...], self.slope[b, :, cols]).astype(BF)

    def back_hidden(self, i):
        rows = span(i, TILE)
        for c in range(3):
            cols = slice(c * 256, (c + 1) * 256)
            back = nt(self.slope[0, rows, :], self.wup[cols, 0:768])
            for b in range(1, 4):
                back += nt(self.slope[b, rows, :], self.wup[cols, b * 768 : (b + 1) * 768])
            self.wide[rows, cols] += back
        totals = [jnp.zeros((8, 768), F32)] * 3
        for at in range(0, TILE, 32):
            here = pl.ds(i * TILE + at, 32)
            d_hidden = self.wide[here, :]
            normed = self.normed[here, :].astype(F32)
            scaled = d_hidden * self.lines[3:4]
            d_one = self.inverse[at : at + 32, i : i + 1] * (scaled - mean(scaled) - normed * mean(scaled * normed))
            totals = [old + eight(new) for old, new in zip(totals, (d_one, d_hidden * normed, d_hidden))]
            self.wide[here, :] = d_one
            self.low[here, :] = d_one.astype(BF)
        for row, total in zip((2, 3, 4), totals):
            self.note(row, total)

    def grad_out(self):
        for c in range(3):
            cols = slice(c * 256, (c + 1) * 256)
            self.slope[3, 0:768, cols] = tn(self.context[...], self.low[:, cols]).astype(BF)

    def back_context(self, i):
        rows = span(i, TILE)
        self.context[rows, :] = nt(self.low[rows, :], self.wout[...]).astype(BF)

    def back_attend(self, g, rows):
        chains = self.chains(g, rows)
        qkv = [[self.part(p, where, b) for b in range(3)] for r, p, where in chains]
        probs = [self.probs[r, p * 256 : (p + 1) * 256, :] for r, p, where in chains]
        d_context = [self.halves(self.context[where, p * 128 : (p + 1) * 128]) for r, p, where in chains]
        d_probs = [nt(down, v) for down, (q, k, v) in zip(d_context, qkv)]
        d_values = [tn(prob, down).astype(BF) for prob, down in zip(probs, d_context)]
        d_scores = []
        for prob, d_prob in zip(probs, d_probs):
            some = []
            for at, part in parts(d_prob, 128):
                wide = prob[at : at + 128].astype(F32)
                inner = jnp.sum(wide * part, axis=-1, keepdims=True)
                some.append((wide * (part - inner)).astype(BF))
            d_scores.append(some)
        d_queries = [(nn(jnp.concatenate(some, axis=1), self.halves(k)) * 0.125).astype(BF) for some, (q, k, v) in zip(d_scores, qkv)]
        d_keys = [tn(jnp.concatenate(some, axis=0), self.halves(q)).astype(BF) for some, (q, k, v) in zip(d_scores, qkv)]
        totals = {}
        for i, (r, p, where) in enumerate(chains):
            for b, grad in enumerate((d_queries[i], d_keys[i], d_values[i])):
                self.qkv[where, p * HALF + b * 128 : p * HALF + (b + 1) * 128] = grad
                if b != 1:
                    totals[b, p] = totals.get((b, p), 0.0) + eight(grad.astype(F32))
        for (b, p), total in totals.items():
            self.note(b // 2, total, slice(p * 128, (p + 1) * 128))

    def grad_qkv(self, g):
        for c in range(3):
            cols = slice(c * 256, (c + 1) * 256)
            grad = self.qkv[:, g * 768 + c * 256 : g * 768 + (c + 1) * 256]
            self.slope[g, 0:768, cols] = tn(self.tokens[...], grad).astype(BF)

    def back_tokens(self, i):
        rows = span(i, TILE)
        grad = self.wide[rows, :]
        for g in range(3):
            cols = slice(g * 768, (g + 1) * 768)
            grad += nt(self.qkv[rows, cols], self.wqkv[:, cols])
        self.wide[rows, :] = grad


LANES = np.stack([np.arange(3072) % 24, np.arange(3072) // 24, np.arange(3072) % 96, np.arange(3072) // 96] + [np.zeros(3072)] * 4).astype(np.int32)


def layer_kernel(
    tokens, cotangent, segments, live, predicted, targets, lanes, sqkv, sout, sup, sdown, vec,
    layer_out, grad_tokens, oqkv, oout, oup, odown, osums,
    wqkv, wout, wup, wdown, vecs, lines, up_bias, qkv_bias, partial, qkv, probs, context, normed, inverse, hidden, act, slope, wide, low, gdown,
    sums, pdown, r1, r1_down, r1_c, r2, r2_down, r2_c, rz, rz_down, rz_c, whole, whole_down, totals, totals_down, lasts, lasts_down, stage, land,
    copies, sends, recvs, free, late,
):
    w = Wires(sends, recvs)
    core, chip = w.core, w.chip
    m = Layer(
        tokens=tokens, segments=segments, live=live, predicted=predicted, targets=targets, lanes=lanes, vecs=vecs,
        wqkv=wqkv, wout=wout, wup=wup, wdown=wdown, lines=lines, up_bias=up_bias, qkv_bias=qkv_bias, partial=partial, qkv=qkv, probs=probs,
        context=context, normed=normed, inverse=inverse, hidden=hidden, act=act, slope=slope, wide=wide, low=low, gdown=gdown,
        sums=sums, cotangent=gdown.at[0:1024], layer_out=gdown.at[1024:2048],
    )

    def block(b):
        return (wqkv, b * 768) if b < 3 else (wout, 0) if b < 4 else (wup, (b - 4) * 768)

    def shard(b, h):
        if b < 3:
            return jnp.concatenate([sqkv[:, i * 768 + (2 * b + h) * 128 : i * 768 + (2 * b + h + 1) * 128] for i in range(3)], axis=1)
        ref, at = (sout, 0) if b < 4 else (sup, (b - 4) * 768)
        return ref[:, at + h * HALF : at + (h + 1) * HALF]

    def packed(first, b, core_rows=0):
        rows = pl.ds(pl.multiple_of(first + core_rows + (b // 2) * 32, 16), 32)
        return rows, slice((b % 2) * HALF, (b % 2 + 1) * HALF)

    def exchange():
        for h in (0, 1):
            for b in range(8):
                rows, cols = packed(2048 + h * 128, b)
                gdown[rows, cols] = jnp.concatenate([shard(b, h).astype(F32), jnp.zeros((8, HALF), F32)], axis=0).astype(BF)
        w.barrier()
        there = w.partner()
        first = pl.ds(pl.multiple_of(2048 + (1 - core) * 128, 16), 64)
        second = pl.ds(pl.multiple_of(2112 + (1 - core) * 128, 16), 64)
        one = w.send(gdown.at[first, :], gdown.at[2304:2368, :], there)
        spread.step()
        two = w.send(gdown.at[second, :], gdown.at[2368:2432, :], there)
        three = []
        for j in range(3):
            cols = pl.ds(pl.multiple_of(j * 256 + (1 - core) * 128, 128), 128)
            three.append(w.send(sdown.at[:, cols], gdown.at[2432:2528, j * 128 : (j + 1) * 128], there))

        def merge(b):
            rows, cols = packed(2048, b, core * 128)
            own = gdown[rows, cols].astype(F32)[:24]
            rows, cols = packed(2304, b)
            got = gdown[rows, cols].astype(F32)[:24]
            low_rows, high_rows = jnp.where(core == 0, own, got), jnp.where(core == 0, got, own)
            ref, at = block(b)
            ref[rows_at(chip, 1, 48), pl.ds(pl.multiple_of(at + core * HALF, 128), HALF)] = jnp.concatenate(
                [low_rows, high_rows], axis=0
            ).astype(BF)

        one.wait_recv()
        for b in range(4):
            merge(b)
        return merge, two, three

    def exchange_rest(merge, two, three):
        two.wait_recv()
        for b in range(4, 8):
            merge(b)
        arrived(three)
        for j in range(3):
            cols = pl.ds(pl.multiple_of(j * 256 + core * 128, 128), 128)
            wdown[pl.ds(pl.multiple_of(chip * 192 + core * 96, 16), 96), cols] = sdown[:, cols]
            wdown[pl.ds(pl.multiple_of(chip * 192 + (1 - core) * 96, 16), 96), cols] = gdown[2432:2528, j * 128 : (j + 1) * 128]

    spread = Spread(w, vecs)
    gathers = {}
    for b in range(8):
        ref, at = block(b)
        gathers[b] = Gather(w, ref, 48, at + core * HALF, HALF, GATHER_ORDERS[b])
    for j in range(3):
        gathers[8 + j] = Gather(w, wdown, 192, j * 256 + core * 128, 128, GATHER_ORDERS[8 + j])
    pieces = {GATHER + i: piece for i, piece in gathers.items()}
    pieces[SPREAD] = spread

    def writer(b):
        def write(which, value):
            for i in range(3):
                if b < 3:
                    at = i * 768 + 2 * b * 128 + which * 128
                else:
                    at = max(b - 4, 0) * 768 + i * 128 + which * HALF
                ref = oqkv if b < 3 else oout if b < 4 else oup
                ref[:, pl.ds(pl.multiple_of(at, 128), 128)] = value[:, i * 128 : (i + 1) * 128]

        return write

    def writer_down(j):
        def write(which, value):
            odown[:, pl.ds(pl.multiple_of(j * 256 + which * 128, 128), 128)] = value

        return write

    waited = []

    def gate():
        if not waited:
            waited.append(True)
            pl.semaphore_wait(late, 5)

    def back_hidden(i):
        alone(m.back_hidden, i)
        if i == 3:
            for peer in [w.over_x(), w.over_y()] + [w.along_z(j) for j in (1, 2, 3)]:
                pl.semaphore_signal(late, inc=1, device_id=peer, device_id_type=MESH)

    for j in range(3):
        if SCATTER_ORDERS[8 + j] == "C":
            lands = (r1_c, r2_c, rz_c)
        else:
            lands = (r1_down.at[j - 1], r2_down.at[j - 1], rz_down.at[j - 1])
        pieces[SCATTER + 8 + j] = Scatter(
            w, gdown, 192, j * 256 + core * 128, j * 256 + (1 - core) * 128, 128, SCATTER_ORDERS[8 + j], pdown.at[j], *lands,
            whole_down, totals_down.at[j], lasts_down.at[j], writer_down(j), lambda: None,
        )
    for b in range(8):
        ref = slope.at[b, 0:768] if b < 3 else slope.at[3, 0:768] if b < 4 else act.at[b - 4, 0:768]
        p = wdown.at[(b // 2) * 768 : (b // 2 + 1) * 768, (b % 2) * HALF : (b % 2 + 1) * HALF]
        if b < 4:
            cols = slice(b * 768, b * 768 + HALF)
            lands = (wup.at[0:384, cols], wup.at[384:576, cols], wup.at[576:720, cols])
        else:
            lands = (r1.at[b - 4], r2.at[b - 4], rz.at[b - 4])
        pieces[SCATTER + b] = Scatter(
            w, ref, 48, core * HALF, (1 - core) * HALF, HALF, SCATTER_ORDERS[b], p, *lands,
            whole, totals.at[b], lasts.at[b], writer(b), gate if b < 4 else lambda: None,
        )
    pieces[SUMS] = Sums(w, sums, stage, land, osums)
    held = {}

    def local(source, target, i):
        held[i] = pltpu.make_async_copy(source, target, copies.at[i])
        held[i].start()

    def start():
        local(cotangent, gdown.at[0:1024], 0)
        vecs[pl.ds(pl.multiple_of((chip * 2 + core) * 8, 8), 8), :] = vec[...]
        sums[...] = jnp.zeros_like(sums)
        partial[...] = jnp.zeros_like(partial)
        held["rest"] = exchange()

    def first():
        alone(m.vectors)
        alone(m.tally)

    def down(i):
        if i == 0:
            held[0].wait()
        alone(m.down, i)
        rows = slice(i * TILE, (i + 1) * TILE)
        local(gdown.at[1024 + i * TILE : 1024 + (i + 1) * TILE], layer_out.at[rows], 1 + i)

    def grad_down(j):
        if j == 0:
            w.drain()
            for i in range(4):
                held[1 + i].wait()
        alone(m.grad_down, j)

    def back_up(b):
        alone(lambda: [m.back_up(b, i) for i in (0, 1)])
        if b == 3:
            pl.semaphore_signal(free, inc=1, device_id=w.partner(), device_id_type=MESH)

    def grad_up(b):
        alone(m.grad_up, b)
        if b == 0:
            pl.semaphore_wait(free, 1)

    def grad_qkv(g):
        alone(m.grad_qkv, g)
        if g == 2:
            alone(m.fold)

    def back_tokens(i):
        alone(m.back_tokens, i)
        rows = slice(i * TILE, (i + 1) * TILE)
        local(wide.at[rows], grad_tokens.at[rows], 5 + i)

    def alone(body, *args):
        @pl.when(core >= 0)
        def _():
            body(*args)

    def each(body, *items):
        return lambda: [body(i) for i in items]

    def apart(body, *items):
        return lambda: alone(lambda: [body(i) for i in items])

    work = [start, lambda: exchange_rest(*held["rest"]), first]
    for g in range(3):
        work.append(apart(lambda i, g=g: m.project(g, i), 0, 1, 2, 3))
        work += [apart(lambda r, g=g: m.attend(g, range(r, r + 4)), 4 * h) for h in (0, 1)]
    work += [apart(m.out_project, 0, 1), apart(m.out_project, 2, 3)]
    work += [apart(lambda i, b=b: m.up(b, i), i) for b in range(4) for i in (0, 1)]
    work += [each(down, i) for i in range(4)]
    work += [each(grad_down, j) for j in range(3)]
    work += [each(back_up, b) for b in range(4)]
    work += [each(grad_up, b) for b in range(4)]
    work += [each(back_hidden, i) for i in range(4)]
    work += [lambda: alone(m.grad_out), apart(m.back_context, 0, 1, 2, 3)]
    for g in range(3):
        work += [apart(lambda r, g=g: m.back_attend(g, range(r, r + 4)), 4 * h) for h in (0, 1)]
        work.append(each(grad_qkv, g))
    work += [each(back_tokens, i) for i in range(4)]
    work.append(lambda: None)
    assert len(work) == len(PLAN)
    for part, steps in zip(work, PLAN):
        for i in steps:
            pieces[i].step()
        part()
    for i in range(4):
        held[5 + i].wait()
    w.drain()
    assert w.used <= SEMAPHORES, w.used


def layer(tokens, cotangent, segment_ids, live_mask, predicted, targets, w_qkv, w_out, w_up, w_down, vec):
    V = pl.BlockSpec(memory_space=pltpu.VMEM)
    A = pl.BlockSpec(memory_space=pl.ANY)
    return pl.pallas_call(
        layer_kernel,
        out_shape=(
            jax.ShapeDtypeStruct((1024, 768), BF),
            jax.ShapeDtypeStruct((1024, 768), F32),
            jax.ShapeDtypeStruct((24, 2304), F32),
            jax.ShapeDtypeStruct((24, 768), F32),
            jax.ShapeDtypeStruct((24, 3072), F32),
            jax.ShapeDtypeStruct((96, 768), F32),
            jax.ShapeDtypeStruct((16, 768), F32),
        ),
        in_specs=[V, A] + [V] * 10,
        out_specs=[A] * 2 + [V] * 5,
        scratch_shapes=[
            pltpu.VMEM((768, 2304), BF),
            pltpu.VMEM((768, 768), BF),
            pltpu.VMEM((768, 3072), BF),
            pltpu.VMEM((3072, 768), BF),
            pltpu.VMEM((256, 128), F32),
            pltpu.VMEM((8, 768), F32),
            pltpu.VMEM((4, 1, 768), F32),
            pltpu.VMEM((3, 1, 768), F32),
            pltpu.VMEM((96, 768), F32),
            pltpu.VMEM((1024, 2304), BF),
            pltpu.VMEM((8, 1536, 128), BF),
            pltpu.VMEM((1024, 768), BF),
            pltpu.VMEM((1024, 768), BF),
            pltpu.VMEM((TILE, 128), F32),
            pltpu.VMEM((1024, 768), BF),
            pltpu.VMEM((4, 1024, 768), BF),
            pltpu.VMEM((4, 1024, 768), BF),
            pltpu.VMEM((1024, 768), F32),
            pltpu.VMEM((1024, 768), BF),
            pltpu.VMEM((3072, 768), BF),
            pltpu.VMEM((16, 768), F32),
            pltpu.VMEM((3, 3072, 128), BF),
            pltpu.VMEM((4, 384, HALF), BF),
            pltpu.VMEM((2, 1536, 128), BF),
            pltpu.VMEM((384, 128), BF),
            pltpu.VMEM((4, 192, HALF), BF),
            pltpu.VMEM((2, 768, 128), BF),
            pltpu.VMEM((192, 128), BF),
            pltpu.VMEM((4, 144, HALF), BF),
            pltpu.VMEM((2, 576, 128), BF),
            pltpu.VMEM((2304, 128), BF),
            pltpu.VMEM((48, HALF), F32),
            pltpu.VMEM((192, 128), F32),
            pltpu.VMEM((8, 24, HALF), F32),
            pltpu.VMEM((3, 96, 128), F32),
            pltpu.VMEM((8, 24, HALF), F32),
            pltpu.VMEM((3, 96, 128), F32),
            pltpu.VMEM((4, 16, HALF), F32),
            pltpu.VMEM((6, 16, HALF), F32),
            pltpu.SemaphoreType.DMA((9,)),
            pltpu.SemaphoreType.DMA((SEMAPHORES,)),
            pltpu.SemaphoreType.DMA((SEMAPHORES,)),
            pltpu.SemaphoreType.REGULAR,
            pltpu.SemaphoreType.REGULAR,
        ],
        compiler_params=pltpu.CompilerParams(collective_id=0, has_side_effects=True, vmem_limit_bytes=64 * 2**20 - 2**17),
    )(
        tokens, cotangent, segment_ids, live_mask, predicted.reshape(8, 128), targets.reshape(8, 128), jnp.asarray(LANES),
        w_qkv, w_out, w_up, w_down, vec,
    )


def plain_device(
    tokens,
    cotangent,
    segment_ids,
    live_mask,
    predicted,
    targets,
    w_qkv,
    bias_query,
    bias_value,
    w_out,
    bias_out,
    gain_attn,
    shift_attn,
    w_up,
    bias_up,
    w_down,
    bias_down,
    gain_ffn,
    shift_ffn,
):
    row_count, seq_len = segment_ids.shape
    classes = jnp.arange(CLASSES, dtype=jnp.int32)
    live_flat = live_mask.reshape(-1) == 1
    target_hits = (targets[:, None] == classes[None, :]) & live_flat[:, None]
    correct = target_hits & (predicted[:, None] == targets[:, None])
    local_tally = jnp.stack(
        [jnp.sum(correct, axis=0, dtype=jnp.int32), jnp.sum(target_hits, axis=0, dtype=jnp.int32)]
    )
    tallies = lax.psum(local_tally, ("dp", "fsdp"))
    (
        whole_qkv,
        whole_query_bias,
        whole_value_bias,
        whole_out,
        whole_out_bias,
        whole_gain_attn,
        whole_shift_attn,
        whole_up,
        whole_up_bias,
        whole_down,
        whole_down_bias,
        whole_gain_ffn,
        whole_shift_ffn,
    ) = (
        lax.all_gather(w_qkv, ("dp", "fsdp"), axis=0, tiled=True),
        lax.all_gather(bias_query, ("dp", "fsdp"), axis=0, tiled=True),
        lax.all_gather(bias_value, ("dp", "fsdp"), axis=0, tiled=True),
        lax.all_gather(w_out, ("dp", "fsdp"), axis=0, tiled=True),
        lax.all_gather(bias_out, ("dp", "fsdp"), axis=0, tiled=True),
        lax.all_gather(gain_attn, ("dp", "fsdp"), axis=0, tiled=True),
        lax.all_gather(shift_attn, ("dp", "fsdp"), axis=0, tiled=True),
        lax.all_gather(w_up, ("dp", "fsdp"), axis=0, tiled=True),
        lax.all_gather(bias_up, ("dp", "fsdp"), axis=0, tiled=True),
        lax.all_gather(w_down, ("dp", "fsdp"), axis=0, tiled=True),
        lax.all_gather(bias_down, ("dp", "fsdp"), axis=0, tiled=True),
        lax.all_gather(gain_ffn, ("dp", "fsdp"), axis=0, tiled=True),
        lax.all_gather(shift_ffn, ("dp", "fsdp"), axis=0, tiled=True),
    )
    projected = jnp.dot(tokens, whole_qkv, preferred_element_type=jnp.float32)
    queries = (projected[:, :D] + whole_query_bias.astype(jnp.float32)).astype(jnp.bfloat16)
    keys_part = projected[:, D : 2 * D].astype(jnp.bfloat16)
    values = (projected[:, 2 * D :] + whole_value_bias.astype(jnp.float32)).astype(jnp.bfloat16)
    query_heads = split_heads(queries, row_count, seq_len)
    key_heads = split_heads(keys_part, row_count, seq_len)
    value_heads = split_heads(values, row_count, seq_len)
    diagonal = jnp.eye(seq_len, dtype=bool)
    allowed = (segment_ids[:, :, None] == segment_ids[:, None, :]) & (
        (live_mask[:, None, :] == 1) | diagonal[None]
    )
    scores = masked_scores(query_heads, key_heads, allowed)
    highest = jnp.max(scores, axis=-1, keepdims=True)
    raised = jnp.exp(scores - highest)
    total = jnp.sum(raised, axis=-1, keepdims=True)
    soft_weights = raised / total
    log_total = highest + jnp.log(total)
    context = (
        jnp.einsum(
            "bhqk,bkhc->bqhc",
            soft_weights.astype(jnp.bfloat16),
            value_heads,
            preferred_element_type=jnp.float32,
        )
        .reshape(-1, D)
        .astype(jnp.bfloat16)
    )
    attended = jnp.dot(
        context, whole_out, preferred_element_type=jnp.float32
    ) + whole_out_bias.astype(jnp.float32)
    hidden, normed_one, inverse_one = normalize(
        tokens.astype(jnp.float32) + attended,
        whole_gain_attn.astype(jnp.float32),
        whole_shift_attn.astype(jnp.float32),
    )
    hidden_low = hidden.astype(jnp.bfloat16)
    up_value = jnp.dot(
        hidden_low, whole_up, preferred_element_type=jnp.float32
    ) + whole_up_bias.astype(jnp.float32)
    activated_low = jax.nn.gelu(up_value, approximate=False).astype(jnp.bfloat16)
    ffn_out = jnp.dot(
        activated_low, whole_down, preferred_element_type=jnp.float32
    ) + whole_down_bias.astype(jnp.float32)
    layer_out, normed_two, inverse_two = normalize(
        hidden + ffn_out, whole_gain_ffn.astype(jnp.float32), whole_shift_ffn.astype(jnp.float32)
    )
    back_qkv, back_out, back_up, back_down, back_gain_attn, back_gain_ffn = (
        lax.all_gather(w_qkv, ("dp", "fsdp"), axis=0, tiled=True),
        lax.all_gather(w_out, ("dp", "fsdp"), axis=0, tiled=True),
        lax.all_gather(w_up, ("dp", "fsdp"), axis=0, tiled=True),
        lax.all_gather(w_down, ("dp", "fsdp"), axis=0, tiled=True),
        lax.all_gather(gain_attn, ("dp", "fsdp"), axis=0, tiled=True),
        lax.all_gather(gain_ffn, ("dp", "fsdp"), axis=0, tiled=True),
    )
    upstream = cotangent.astype(jnp.float32)
    grad_gain_ffn = jnp.sum(upstream * normed_two, axis=0)
    grad_shift_ffn = jnp.sum(upstream, axis=0)
    d_resid_two = normalize_back(
        upstream, normed_two, inverse_two, back_gain_ffn.astype(jnp.float32)
    )
    d_two_low = d_resid_two.astype(jnp.bfloat16)
    grad_down = contract_rows(activated_low, d_two_low)
    grad_down_bias = jnp.sum(d_resid_two, axis=0)
    d_activated = times_transposed(d_two_low, back_down)
    gelu_pullback = jax.vjp(partial(jax.nn.gelu, approximate=False), up_value)[1]
    d_up = gelu_pullback(d_activated)[0].astype(jnp.bfloat16)
    grad_up_bias = jnp.sum(d_up.astype(jnp.float32), axis=0)
    grad_up = contract_rows(hidden_low, d_up)
    d_hidden = d_resid_two + times_transposed(d_up, back_up)
    grad_gain_attn = jnp.sum(d_hidden * normed_one, axis=0)
    grad_shift_attn = jnp.sum(d_hidden, axis=0)
    d_resid_one = normalize_back(
        d_hidden, normed_one, inverse_one, back_gain_attn.astype(jnp.float32)
    )
    d_one_low = d_resid_one.astype(jnp.bfloat16)
    grad_out_bias = jnp.sum(d_resid_one, axis=0)
    grad_out = contract_rows(context, d_one_low)
    d_context = times_transposed(d_one_low, back_out).astype(jnp.bfloat16)
    d_context_heads = split_heads(d_context, row_count, seq_len)
    d_soft = jnp.einsum(
        "bqhc,bkhc->bhqk", d_context_heads, value_heads, preferred_element_type=jnp.float32
    )
    soft_again = jnp.exp(masked_scores(query_heads, key_heads, allowed) - log_total)
    d_values = (
        jnp.einsum(
            "bhqk,bqhc->bkhc",
            soft_again.astype(jnp.bfloat16),
            d_context_heads,
            preferred_element_type=jnp.float32,
        )
        .reshape(-1, D)
        .astype(jnp.bfloat16)
    )
    inner = jnp.sum(soft_again * d_soft, axis=-1, keepdims=True)
    d_scores = (soft_again * (d_soft - inner)).astype(jnp.bfloat16)
    d_queries = (
        (
            jnp.einsum("bhqk,bkhc->bqhc", d_scores, key_heads, preferred_element_type=jnp.float32)
            * HEAD_DIM ** (-0.5)
        )
        .reshape(-1, D)
        .astype(jnp.bfloat16)
    )
    d_keys = (
        (
            jnp.einsum("bhqk,bqhc->bkhc", d_scores, query_heads, preferred_element_type=jnp.float32)
            * HEAD_DIM ** (-0.5)
        )
        .reshape(-1, D)
        .astype(jnp.bfloat16)
    )
    d_projected = jnp.concatenate([d_queries, d_keys, d_values], axis=1)
    grad_query_bias = jnp.sum(d_queries.astype(jnp.float32), axis=0)
    grad_value_bias = jnp.sum(d_values.astype(jnp.float32), axis=0)
    grad_qkv = contract_rows(tokens, d_projected)
    grad_tokens = d_resid_one + times_transposed(d_projected, back_qkv)
    summed = tuple(
        (
            lax.psum_scatter(grad_qkv, ("dp", "fsdp"), scatter_dimension=0, tiled=True),
            lax.psum_scatter(grad_query_bias, ("dp", "fsdp"), scatter_dimension=0, tiled=True),
            lax.psum_scatter(grad_value_bias, ("dp", "fsdp"), scatter_dimension=0, tiled=True),
            lax.psum_scatter(grad_out, ("dp", "fsdp"), scatter_dimension=0, tiled=True),
            lax.psum_scatter(grad_out_bias, ("dp", "fsdp"), scatter_dimension=0, tiled=True),
            lax.psum_scatter(grad_gain_attn, ("dp", "fsdp"), scatter_dimension=0, tiled=True),
            lax.psum_scatter(grad_shift_attn, ("dp", "fsdp"), scatter_dimension=0, tiled=True),
            lax.psum_scatter(grad_up, ("dp", "fsdp"), scatter_dimension=0, tiled=True),
            lax.psum_scatter(grad_up_bias, ("dp", "fsdp"), scatter_dimension=0, tiled=True),
            lax.psum_scatter(grad_down, ("dp", "fsdp"), scatter_dimension=0, tiled=True),
            lax.psum_scatter(grad_down_bias, ("dp", "fsdp"), scatter_dimension=0, tiled=True),
            lax.psum_scatter(grad_gain_ffn, ("dp", "fsdp"), scatter_dimension=0, tiled=True),
            lax.psum_scatter(grad_shift_ffn, ("dp", "fsdp"), scatter_dimension=0, tiled=True),
        )
    )
    return (layer_out.astype(jnp.bfloat16), grad_tokens) + summed + (tallies,)


def fast_device(
    tokens,
    cotangent,
    segment_ids,
    live_mask,
    predicted,
    targets,
    w_qkv,
    bias_query,
    bias_value,
    w_out,
    bias_out,
    gain_attn,
    shift_attn,
    w_up,
    bias_up,
    w_down,
    bias_down,
    gain_ffn,
    shift_ffn,
):
    small = jnp.stack([bias_query, bias_value, bias_out, gain_attn, shift_attn, bias_down, gain_ffn, shift_ffn]).astype(F32)
    vec = jnp.concatenate([small, jnp.zeros((8, 8), F32), jnp.pad(bias_up.astype(F32)[None], ((0, 7), (0, 0)))], axis=1)
    layer_out, grad_tokens, sqkv, sout, sup, sdown, sums = layer(
        tokens, cotangent, segment_ids, live_mask, predicted, targets, w_qkv, w_out, w_up, w_down, vec
    )
    index = lax.axis_index("dp") * 8 + lax.axis_index("fsdp")
    lines = lax.dynamic_slice(sums[:8], (0, index * 24), (8, 24))
    up_line = lax.dynamic_slice(sums[8:12].reshape(3072), (index * 96,), (96,))
    tallies = sums[12, :48].reshape(2, 24).astype(jnp.int32)
    return (
        layer_out, grad_tokens, sqkv, lines[0], lines[1], sout, lines[2], lines[3], lines[4], sup, up_line, sdown,
        lines[5], lines[6], lines[7], tallies,
    )


def solution(mesh):
    in_specs = (
        P(("dp", "fsdp"), None),
        P(("dp", "fsdp"), None),
        P(("dp", "fsdp"), None),
        P(("dp", "fsdp"), None),
        P(("dp", "fsdp")),
        P(("dp", "fsdp")),
        P(("dp", "fsdp"), None),
        P(("dp", "fsdp")),
        P(("dp", "fsdp")),
        P(("dp", "fsdp"), None),
        P(("dp", "fsdp")),
        P(("dp", "fsdp")),
        P(("dp", "fsdp")),
        P(("dp", "fsdp"), None),
        P(("dp", "fsdp")),
        P(("dp", "fsdp"), None),
        P(("dp", "fsdp")),
        P(("dp", "fsdp")),
        P(("dp", "fsdp")),
    )
    out_specs = (
        P(("dp", "fsdp"), None),
        P(("dp", "fsdp"), None),
        P(("dp", "fsdp"), None),
        P(("dp", "fsdp")),
        P(("dp", "fsdp")),
        P(("dp", "fsdp"), None),
        P(("dp", "fsdp")),
        P(("dp", "fsdp")),
        P(("dp", "fsdp")),
        P(("dp", "fsdp"), None),
        P(("dp", "fsdp")),
        P(("dp", "fsdp"), None),
        P(("dp", "fsdp")),
        P(("dp", "fsdp")),
        P(("dp", "fsdp")),
        P(),
    )
    fast = tuple(mesh.shape.items()) == (("dp", 4), ("fsdp", 8))
    return jax.shard_map(
        fast_device if fast else plain_device, mesh=mesh, in_specs=in_specs, out_specs=out_specs, check_vma=False
    )
```

```python
import functools
from functools import partial

import jax
import jax.numpy as jnp
import numpy as np
from jax import lax
from jax.experimental import pallas as pl
from jax.experimental.pallas import tpu as pltpu
from jax.sharding import PartitionSpec as P

D = 768
HEADS = 12
HEAD_DIM = 64
CLASSES = 24


EPSILON = 1e-05


def normalize(operand, scale_vec, shift_vec):
    center = operand - jnp.mean(operand, axis=-1, keepdims=True)
    inverse = lax.rsqrt(jnp.mean(center * center, axis=-1, keepdims=True) + EPSILON)
    normed = center * inverse
    return (normed * scale_vec + shift_vec, normed, inverse)


def normalize_back(grad_out, normed, inverse, scale_vec):
    scaled = grad_out * scale_vec
    return inverse * (
        scaled
        - jnp.mean(scaled, axis=-1, keepdims=True)
        - normed * jnp.mean(scaled * normed, axis=-1, keepdims=True)
    )


def contract_rows(left, right):
    return lax.dot_general(
        left, right, (((0,), (0,)), ((), ())), preferred_element_type=jnp.float32
    )


def times_transposed(left, right):
    return lax.dot_general(
        left, right, (((1,), (1,)), ((), ())), preferred_element_type=jnp.float32
    )


def split_heads(matrix, row_count, seq_len):
    return matrix.reshape(row_count, seq_len, HEADS, HEAD_DIM)


def masked_scores(query_heads, key_heads, allowed):
    scores = jnp.einsum(
        "bqhc,bkhc->bhqk", query_heads, key_heads, preferred_element_type=jnp.float32
    ) * HEAD_DIM ** (-0.5)
    return jnp.where(allowed[:, None], scores, -1000000000.0)


MESH = pl.DeviceIdType.MESH
BF = jnp.bfloat16
F32 = jnp.float32
HALF = 384


def place():
    dp, fsdp = lax.axis_index("dp"), lax.axis_index("fsdp")
    return dp // 2, dp % 2, fsdp // 2, fsdp % 2


class Wires:
    def __init__(self, send_sems, recv_sems):
        self.y, self.x, self.z, self.core = place()
        self.plane = self.y * 2 + self.x
        self.chip = self.plane * 4 + self.z
        self.send_sems, self.recv_sems, self.used, self.open = send_sems, recv_sems, 0, []

    def device(self, y=None, x=None, z=None, core=None):
        y = self.y if y is None else y
        x = self.x if x is None else x
        z = self.z if z is None else z
        core = self.core if core is None else core
        return (y * 2 + x, z * 2 + core)

    def partner(self):
        return self.device(core=1 - self.core)

    def over_x(self):
        return self.device(x=1 - self.x)

    def over_y(self):
        return self.device(y=1 - self.y)

    def along_z(self, jump):
        return self.device(z=(self.z + jump) % 4)

    def barrier(self):
        semaphore = pltpu.get_barrier_semaphore()
        peers = [self.partner(), self.over_x(), self.over_y()] + [self.along_z(j) for j in (1, 2, 3)]
        for peer in peers:
            pl.semaphore_signal(semaphore, inc=1, device_id=peer, device_id_type=MESH)
        pl.semaphore_wait(semaphore, 6)

    def send(self, source, target, device):
        number = self.used
        self.used += 1
        copy = pltpu.make_async_remote_copy(
            src_ref=source,
            dst_ref=target,
            send_sem=self.send_sems.at[number],
            recv_sem=self.recv_sems.at[number],
            device_id=device,
            device_id_type=MESH,
        )
        copy.start()
        self.open.append(copy)
        return copy

    def drain(self):
        for copy in self.open:
            copy.wait_send()
        self.open = []


def arrived(copies):
    for copy in copies:
        copy.wait_recv()


def rows_at(start, count, slab):
    return pl.ds(pl.multiple_of(start * slab, 16), count * slab)


class Piece:
    at = 0

    def step(self):
        self.steps[self.at]()
        self.at += 1


class Gather(Piece):
    def __init__(self, wires, ref, slab, first, width, order):
        self.w, self.ref, self.slab, self.width, self.first = wires, ref, slab, width, first
        self.back = []
        self.steps = {
            "A": [self.z0, self.a1, self.a2, self.a3],
            "B": [self.z0, self.b1, self.b2, self.b3],
            "C": [self.c0, self.c1, self.c2, self.c3],
        }[order] + [self.done]

    def send(self, slabs, count, device):
        part = self.ref.at[rows_at(slabs, count, self.slab), pl.ds(pl.multiple_of(self.first, 128), self.width)]
        return self.w.send(part, part, device)

    def hand(self, slabs, count):
        self.back.append(self.send(slabs, count, self.w.partner()))

    def z0(self):
        self.into = [self.send(self.w.chip, 1, self.w.along_z(j)) for j in (1, 2, 3)]

    def a1(self):
        w = self.w
        arrived(self.into)
        self.into = [self.send(w.plane * 4, 4, w.over_x())]
        self.hand(w.plane * 4, 4)

    def a2(self):
        w = self.w
        arrived(self.into)
        self.into = [self.send(w.y * 8, 8, w.over_y())]
        self.hand((w.y * 2 + 1 - w.x) * 4, 4)

    def a3(self):
        arrived(self.into)
        self.hand((1 - self.w.y) * 8, 8)

    def b1(self):
        w = self.w
        arrived(self.into)
        self.into = [self.send(w.plane * 4, 4, w.over_y())]
        self.hand(w.plane * 4, 4)

    def b2(self):
        w = self.w
        arrived(self.into)
        other = ((1 - w.y) * 2 + w.x) * 4
        self.into = [self.send(w.plane * 4, 4, w.over_x()), self.send(other, 4, w.over_x())]
        self.hand(other, 4)

    def b3(self):
        w = self.w
        arrived(self.into)
        for y in (0, 1):
            self.hand((y * 2 + 1 - w.x) * 4, 4)

    def c0(self):
        self.into = [self.send(self.w.chip, 1, self.w.over_x())]

    def c1(self):
        w = self.w
        arrived(self.into)
        self.into = [self.send((w.y * 2 + x) * 4 + w.z, 1, w.over_y()) for x in (0, 1)]

    def c2(self):
        w = self.w
        arrived(self.into)
        self.into = [self.send(plane * 4 + w.z, 1, w.along_z(j)) for j in (1, 2, 3) for plane in range(4)]
        for plane in range(4):
            self.hand(plane * 4 + w.z, 1)

    def c3(self):
        w = self.w
        arrived(self.into)
        for j in (1, 2, 3):
            for plane in range(4):
                self.hand(plane * 4 + (w.z + j) % 4, 1)

    def done(self):
        arrived(self.back)


def add_rows(target, first, count, source, start):
    tile = 96 if count % 96 == 0 else 48

    def body(i, carry):
        there = pl.ds(pl.multiple_of(first + i * tile, 16), tile)
        target[there, :] = target[there, :] + source[pl.ds(pl.multiple_of(start + i * tile, 16), tile), :]
        return carry

    lax.fori_loop(0, count // tile, body, 0)


SIZES = {"A": (8, 4, 3), "B": (8, 4, 3), "C": (2, 1, 12)}


class Scatter(Piece):
    def __init__(self, wires, ref, slab, first, far, width, order, p, land, whole, total, last, write, ready, gate):
        self.w, self.ref, self.slab, self.first, self.far, self.width = wires, ref, slab, first, far, width
        self.p, self.whole, self.total, self.last = p, whole, total, last
        self.write, self.ready, self.gate = write, ready, gate
        self.mine = ref.at[:, pl.ds(pl.multiple_of(first, 128), width)]
        one, two, three = (12, 14, 0) if order == "C" else (0, 8, 12)
        self.r1, self.r2, self.rz = (land.at[at * slab : (at + size) * slab, :] for at, size in zip((one, two, three), SIZES[order]))
        self.steps = {
            "A": [self.p0, self.a1, self.a2, self.a3, self.z4],
            "B": [self.p0, self.b1, self.b2, self.b3, self.z4],
            "C": [self.p0, self.c1, self.c2, self.c3, self.c4],
        }[order] + [self.done]

    def rows(self, slabs, count):
        return self.ref.at[rows_at(slabs, count, self.slab), pl.ds(pl.multiple_of(self.first, 128), self.width)]

    def slot(self, buffer, slabs, count):
        return buffer.at[pl.ds(slabs * self.slab, count * self.slab), :]

    def add(self, slabs, count, source, start):
        add_rows(self.mine, slabs * self.slab, count * self.slab, source, start * self.slab)

    def p0(self):
        self.ready()
        far = self.ref.at[:, pl.ds(pl.multiple_of(self.far, 128), self.width)]
        self.into = [self.w.send(far, self.p, self.w.partner())]

    def a1(self):
        w = self.w
        self.gate()
        arrived(self.into)
        self.add((1 - w.y) * 8, 8, self.p, (1 - w.y) * 8)
        self.into = [w.send(self.rows((1 - w.y) * 8, 8), self.r1, w.over_y())]
        self.add(w.y * 8, 8, self.p, w.y * 8)

    def a2(self):
        w = self.w
        arrived(self.into)
        other = (w.y * 2 + 1 - w.x) * 4
        self.add(other, 4, self.r1, (1 - w.x) * 4)
        self.into = [w.send(self.rows(other, 4), self.r2, w.over_x())]
        self.add(w.plane * 4, 4, self.r1, w.x * 4)

    def a3(self):
        arrived(self.into)
        self.z3()

    def b1(self):
        w = self.w
        self.gate()
        arrived(self.into)
        self.into = []
        for y in (0, 1):
            slabs = (y * 2 + 1 - w.x) * 4
            self.add(slabs, 4, self.p, slabs)
            self.into.append(w.send(self.rows(slabs, 4), self.slot(self.r1, y * 4, 4), w.over_x()))
        for y in (0, 1):
            slabs = (y * 2 + w.x) * 4
            self.add(slabs, 4, self.p, slabs)

    def b2(self):
        w = self.w
        arrived(self.into)
        other = ((1 - w.y) * 2 + w.x) * 4
        self.add(other, 4, self.r1, (1 - w.y) * 4)
        self.into = [w.send(self.rows(other, 4), self.r2, w.over_y())]
        self.add(w.plane * 4, 4, self.r1, w.y * 4)

    def b3(self):
        arrived(self.into)
        self.z3()

    def z3(self):
        w = self.w
        self.add(w.plane * 4, 4, self.r2, 0)
        self.into = []
        for j in (1, 2, 3):
            there = (w.z + j) % 4
            self.into.append(w.send(self.rows(w.plane * 4 + there, 1), self.slot(self.rz, j - 1, 1), w.along_z(j)))

    def z4(self):
        arrived(self.into)
        self.close([self.slot(self.rz, j, 1) for j in range(3)])

    def c1(self):
        w = self.w
        self.gate()
        arrived(self.into)
        self.add(0, 16, self.p, 0)
        self.into = []
        for j in (1, 2, 3):
            for plane in range(4):
                there = self.rows(plane * 4 + (w.z + j) % 4, 1)
                self.into.append(w.send(there, self.slot(self.rz, (j - 1) * 4 + plane, 1), w.along_z(j)))

    def c2(self):
        w = self.w
        arrived(self.into)
        for plane in range(4):
            for j in range(3):
                self.add(plane * 4 + w.z, 1, self.rz, j * 4 + plane)
        self.into = []
        for x in (0, 1):
            there = self.rows(((1 - w.y) * 2 + x) * 4 + w.z, 1)
            self.into.append(w.send(there, self.slot(self.r1, x, 1), w.over_y()))

    def c3(self):
        w = self.w
        arrived(self.into)
        for x in (0, 1):
            self.add((w.y * 2 + x) * 4 + w.z, 1, self.r1, x)
        self.into = [w.send(self.rows((w.y * 2 + 1 - w.x) * 4 + w.z, 1), self.slot(self.r2, 0, 1), w.over_x())]

    def c4(self):
        arrived(self.into)
        self.close([self.slot(self.r2, 0, 1)])

    def close(self, others):
        w = self.w
        total = self.rows(w.chip, 1)[...].astype(F32)
        for other in others:
            total = total + other[...].astype(F32)
        self.whole[...] = total
        half = self.slab // 2
        self.total[...] = self.whole[pl.ds(pl.multiple_of((1 - w.core) * half, 8), half), :]
        self.into = [w.send(self.total, self.last, w.partner())]
        self.write(w.core, self.whole[pl.ds(pl.multiple_of(w.core * half, 8), half), :])

    def done(self):
        arrived(self.into)
        self.write(1 - self.w.core, self.last[...])


class Spread(Piece):
    def __init__(self, wires, tiles):
        self.w, self.tiles = wires, tiles
        self.steps = [self.s0, self.s1, self.s2, self.s3, self.s4]

    def send(self, start, count, device):
        part = self.tiles.at[pl.ds(pl.multiple_of(start * 8, 8), count * 8), :]
        return self.w.send(part, part, device)

    def s0(self):
        w = self.w
        self.into = [self.send(w.chip * 2 + w.core, 1, w.partner())]

    def s1(self):
        w = self.w
        arrived(self.into)
        self.into = [self.send(w.chip * 2, 2, w.along_z(j)) for j in (1, 2, 3)]

    def s2(self):
        arrived(self.into)
        self.into = [self.send(self.w.plane * 8, 8, self.w.over_x())]

    def s3(self):
        arrived(self.into)
        self.into = [self.send(self.w.y * 16, 16, self.w.over_y())]

    def s4(self):
        arrived(self.into)


class Sums(Piece):
    def __init__(self, wires, sums, stage, land, last):
        self.w, self.sums, self.stage, self.land, self.last = wires, sums, stage, land, last
        self.half = pl.ds(pl.multiple_of(wires.core * HALF, 128), HALF)
        self.steps = [self.s0, self.s1, self.s2, self.s3, self.s4, self.s5]

    def s0(self):
        far = pl.ds(pl.multiple_of((1 - self.w.core) * HALF, 128), HALF)
        self.into = [self.w.send(self.sums.at[:, far], self.land.at[0], self.w.partner())]

    def relay(self, value, at, device):
        self.stage[at] = value
        self.into = [self.w.send(self.stage.at[at], self.land.at[at + 1], device)]

    def s1(self):
        arrived(self.into)
        self.relay(self.sums[:, self.half] + self.land[0], 0, self.w.over_x())

    def s2(self):
        arrived(self.into)
        self.relay(self.stage[0] + self.land[1], 1, self.w.over_y())

    def s3(self):
        arrived(self.into)
        self.stage[2] = self.stage[1] + self.land[2]
        self.into = [self.w.send(self.stage.at[2], self.land.at[2 + j], self.w.along_z(j)) for j in (1, 2, 3)]

    def s4(self):
        arrived(self.into)
        self.stage[3] = self.stage[2] + self.land[3] + self.land[4] + self.land[5]
        self.last[:, self.half] = self.stage[3]
        self.into = [self.w.send(self.stage.at[3], self.last.at[:, self.half], self.w.partner())]

    def s5(self):
        arrived(self.into)


GATHER, SCATTER, SPREAD, SUMS, SEMAPHORES = 0, 40, 80, 81, 400
GATHERS = (
    (0, 0, 384, "B"),
    (1, 0, 384, "B"),
    (2, 0, 384, "A"),
    (3, 0, 384, "A"),
    (4, 0, 256, "B"),
    (4, 256, 128, "A"),
    (5, 0, 256, "A"),
    (5, 256, 128, "A"),
    (6, 0, 256, "B"),
    (6, 256, 128, "B"),
    (7, 0, 256, "C"),
    (7, 256, 128, "A"),
    (8, 0, 128, "B"),
    (9, 0, 128, "A"),
    (10, 0, 128, "C"),
)
SCATTERS = (
    (8, 0, 128, "A"),
    (9, 0, 128, "A"),
    (10, 0, 128, "B"),
    (4, 0, 384, "B"),
    (5, 0, 384, "A"),
    (6, 0, 384, "C"),
    (7, 0, 384, "A"),
    (3, 0, 384, "B"),
    (0, 0, 384, "A"),
    (1, 0, 256, "A"),
    (1, 256, 128, "B"),
    (2, 0, 128, "A"),
    (2, 128, 128, "B"),
    (2, 256, 128, "B"),
)
PLAN = (
    ("start", ()),
    ("rest", (80, 0)),
    ("first", (5, 2, 1, 80, 8, 0, 80, 5, 3, 2, 7, 10, 5, 6, 0, 1, 80)),
    ("proj0", (4, 8, 9, 2, 5, 10, 11, 13, 14, 5, 3, 7, 1, 6, 8, 12, 0, 4, 14, 9, 0)),
    ("att00", (11,)),
    ("att01", (3, 2)),
    ("proj1", (10, 13, 7, 2, 4, 14, 12, 9, 1, 6, 1)),
    ("att10", ()),
    ("att11", ()),
    ("proj2", ()),
    ("att20", (3, 11, 8)),
    ("att21", (10, 3, 8, 7)),
    ("out0", ()),
    ("out1", (13, 10, 7)),
    ("up00", (12, 4, 6, 4)),
    ("up01", (9, 11, 6)),
    ("up10", ()),
    ("up11", (9, 11)),
    ("up20", ()),
    ("up21", ()),
    ("up30", ()),
    ("up31", ()),
    ("down0", (14, 12, 13, 14, 12, 13)),
    ("down1", ()),
    ("down2", ()),
    ("down3", ()),
    ("gd0", ()),
    ("bu0", (40,)),
    ("bu3", ()),
    ("gd1", (40,)),
    ("gd2", (41,)),
    ("bu1", (42,)),
    ("bu2", (41,)),
    ("bh0", (42,)),
    ("gu1", ()),
    ("gu2", (40, 44)),
    ("bh3", (45,)),
    ("gu0", (44, 45)),
    ("bh2", (43,)),
    ("gu3", (42, 41, 43)),
    ("bh1", (40, 46)),
    ("go", (44,)),
    ("bc", (47, 46, 41)),
    ("ba01", (47, 42)),
    ("ba00", ()),
    ("gq0", (45,)),
    ("ba11", (48, 43)),
    ("ba20", ()),
    ("ba10", (40, 48, 46, 44, 40, 45)),
    ("gq1", ()),
    ("ba21", (49, 50, 41, 43)),
    ("gq2", (47, 81, 49, 50, 42, 81, 41)),
    ("bt0", (42, 53, 48, 46, 52, 44, 51, 45, 53)),
    ("bt2", (47, 81, 52, 44, 51, 50, 45, 43)),
    ("bt1", (48, 43)),
    ("bt3", (81, 49, 53, 46)),
    ("end", (51, 52, 47, 46, 50, 47, 53, 49, 48, 51, 52, 48, 81, 50, 81, 53, 50, 53, 49, 51, 49, 52, 51, 52)),
)


TOKENS = 1024
TILE = 256


def nn(left, right):
    return jnp.dot(left, right, preferred_element_type=F32)


def nt(left, right):
    return lax.dot_general(left, right, (((1,), (1,)), ((), ())), preferred_element_type=F32)


def tn(left, right):
    return lax.dot_general(left, right, (((0,), (0,)), ((), ())), preferred_element_type=F32)


def loop(start, stop, body):
    def step(i, carry):
        body(i)
        return carry

    lax.fori_loop(start, stop, step, 0)


def span(i, size):
    return slice(i * size, (i + 1) * size) if isinstance(i, int) else pl.ds(pl.multiple_of(i * size, size), size)


def row_sum(value):
    return jnp.sum(value, axis=0, keepdims=True)


def parts(value, size):
    return [(i, value[i : i + size]) for i in range(0, value.shape[0], size)]


def eight(value):
    return jnp.sum(value.reshape(value.shape[0] // 8, 8, value.shape[1]), axis=0)


def mean(value):
    return jnp.mean(value, axis=-1, keepdims=True)


def gelu_both(up):
    density = jnp.exp(up * up * -0.5)
    base = jnp.abs(up) * (0.3275911 * 0.5**0.5) + 1.0
    guess = pltpu.reciprocal(base, approx=True)
    t = guess * (2.0 - base * guess)
    poly = t * (0.127414796 + t * (-0.142248368 + t * (0.7107068705 + t * (-0.7265760135 + t * 0.5307027145))))
    tail = poly * density
    below = jnp.where(up >= 0, 1.0 - tail, tail)
    return up * below, below + up * density * 0.3989422804014327


class Layer:
    def __init__(self, **refs):
        self.__dict__.update(refs)

    def vectors(self):
        line = lambda i, n: self.lanes[i : i + 1, 0:n]
        place = lax.broadcasted_iota(jnp.int32, (128, 768), 0)
        hot = (place == line(0, 768)).astype(F32).astype(BF)
        spread = nn(self.vecs[...].astype(BF), hot).reshape(32, 8, 768)
        owner = lax.broadcasted_iota(jnp.int32, (32, 8, 768), 0)
        self.lines[...] = jnp.sum(jnp.where(owner == line(1, 768)[None], spread, 0.0), axis=0)
        nothing = jnp.zeros((1, 128), F32)
        for g in range(3):
            parts = []
            for p in (2 * g, 2 * g + 1):
                cols = slice(p * 128, (p + 1) * 128)
                parts += [self.lines[0:1, cols], nothing, self.lines[1:2, cols]]
            self.qkv_bias[g] = jnp.concatenate(parts, axis=1)
        firsts = self.vecs[pl.ds(0, 32, 8), :].astype(BF)
        for b in range(4):
            place = lax.broadcasted_iota(jnp.int32, (128, 768), 0)
            cols = slice(b * 768, (b + 1) * 768)
            hot = (place == self.lanes[2:3, cols] + 32).astype(F32).astype(BF)
            spread = nn(firsts, hot)
            owner = lax.broadcasted_iota(jnp.int32, (32, 768), 0)
            self.up_bias[b] = row_sum(jnp.where(owner == self.lanes[3:4, cols], spread, 0.0))

    def tally(self):
        which = lax.broadcasted_iota(jnp.int32, (128, 128), 0)
        right, every = jnp.zeros((128, 128), F32), jnp.zeros((128, 128), F32)
        for r in range(8):
            target, guess, live = (ref[r : r + 1, :] for ref in (self.targets, self.predicted, self.live))
            hit = (which == target) & (live == 1)
            every += jnp.where(hit, 1.0, 0.0)
            right += jnp.where(hit & (guess == target), 1.0, 0.0)
        for row, total in ((12, right), (13, every)):
            self.sums[row : row + 1, 0:128] = nt(jnp.ones((8, 128), BF), total.astype(BF))[0:1]

    def note(self, row, value, cols=slice(0, 768)):
        self.partial[8 * row : 8 * row + 8, cols] += value

    def fold(self):
        for row in range(12):
            self.sums[row : row + 1] = row_sum(self.partial[8 * row : 8 * row + 8])

    def project(self, g, i):
        rows = span(i, TILE)
        out = (nn(self.tokens[rows, :], self.wqkv[:, g * 768 : (g + 1) * 768]) + self.qkv_bias[g]).astype(BF)
        for h in (0, HALF):
            at = g * 768 + h
            self.qkv[rows, at : at + 128] = out[:, h : h + 128] * 0.125
            self.qkv[rows, at + 128 : at + HALF] = out[:, h + 128 : h + HALF]

    def halves(self, pair):
        left = lax.broadcasted_iota(jnp.int32, pair.shape, 1) < 64
        zero = jnp.zeros_like(pair)
        return jnp.concatenate([jnp.where(left, pair, zero), jnp.where(left, zero, pair)], axis=0)

    def chains(self, g, rows):
        return [(r, p, span(r, 128)) for r in rows for p in (2 * g, 2 * g + 1)]

    def part(self, p, rows, b):
        return self.qkv[rows, p * HALF + b * 128 : p * HALF + (b + 1) * 128]

    def attend(self, g, rows):
        eye = lax.broadcasted_iota(jnp.int32, (128, 128), 0) == lax.broadcasted_iota(jnp.int32, (128, 128), 1)
        allowed, probs = {}, []
        for r in rows:
            seg = jnp.broadcast_to(self.segments[r : r + 1, :].astype(F32), (128, 128))
            allowed[r] = (seg == seg.T) & ((self.live[r : r + 1, :] == 1) | eye)
        ones = jnp.ones((128, 128), BF)
        chains = self.chains(g, rows)
        scores = [nt(self.halves(self.part(p, where, 0)), self.part(p, where, 1)) for r, p, where in chains]
        for (r, p, where), score in zip(chains, scores):
            some = []
            for at, part in parts(score, 128):
                part = jnp.where(allowed[r], part, -1e9)
                raised = jnp.exp(part - jnp.max(part, axis=-1, keepdims=True))
                total = nn(raised.astype(BF), ones)
                guess = pltpu.reciprocal(total, approx=True)
                some.append((raised * (guess * (2.0 - total * guess))).astype(BF))
            self.probs[r, p * 256 : (p + 1) * 256, :] = jnp.concatenate(some, axis=0)
            probs.append(jnp.concatenate(some, axis=1))
        for (r, p, where), prob in zip(chains, probs):
            self.context[where, p * 128 : (p + 1) * 128] = nn(prob, self.halves(self.part(p, where, 2))).astype(BF)

    def out_project(self, i):
        rows = span(i, TILE)
        attended = nn(self.context[rows, :], self.wout[...])
        for at, part in parts(attended, 32):
            here = pl.ds(i * TILE + at, 32)
            resid = self.tokens[here, :].astype(F32) + (part + self.lines[2:3])
            center = resid - mean(resid)
            inverse = lax.rsqrt(mean(center * center) + EPSILON)
            normed = center * inverse
            self.normed[here, :] = normed.astype(BF)
            self.inverse[at : at + 32, i : i + 1] = inverse
            self.hidden[here, :] = (normed * self.lines[3:4] + self.lines[4:5]).astype(BF)

    def up(self, b, i, tile=512):
        rows = span(i, tile)
        for c in range(3):
            cols = slice(c * 256, (c + 1) * 256)
            up = nn(self.hidden[rows, :], self.wup[:, b * 768 + c * 256 : b * 768 + (c + 1) * 256])
            for at, part in parts(up, 32):
                here = pl.ds(i * tile + at, 32)
                act, slope = gelu_both(part + self.up_bias[b, :, cols])
                self.act[b, here, cols] = act.astype(BF)
                self.slope[b, here, cols] = slope.astype(BF)

    def down(self, i):
        rows = span(i, TILE)
        for c in range(3):
            cols = slice(c * 256, (c + 1) * 256)
            ffn = nn(self.act[0, rows, :], self.wdown[0:768, cols])
            for b in range(1, 4):
                ffn += nn(self.act[b, rows, :], self.wdown[b * 768 : (b + 1) * 768, cols])
            self.wide[rows, cols] = ffn
        totals = [jnp.zeros((8, 768), F32)] * 3
        for at in range(0, TILE, 32):
            here = pl.ds(i * TILE + at, 32)
            hidden = self.normed[here, :].astype(F32) * self.lines[3:4] + self.lines[4:5]
            resid = hidden + (self.wide[here, :] + self.lines[5:6])
            center = resid - mean(resid)
            inverse = lax.rsqrt(mean(center * center) + EPSILON)
            normed = center * inverse
            self.layer_out[here, :] = (normed * self.lines[6:7] + self.lines[7:8]).astype(BF)
            upstream = self.cotangent[here, :].astype(F32)
            scaled = upstream * self.lines[6:7]
            d_two = inverse * (scaled - mean(scaled) - normed * mean(scaled * normed))
            totals = [old + eight(new) for old, new in zip(totals, (d_two, upstream * normed, upstream))]
            self.wide[here, :] = d_two
            self.low[here, :] = d_two.astype(BF)
        for row, total in zip((5, 6, 7), totals):
            self.note(row, total)

    def grad_down(self, j):
        cols = slice(j * 256, (j + 1) * 256)
        for b in range(4):
            self.gdown[b * 768 : (b + 1) * 768, cols] = tn(self.act[b], self.low[:, cols]).astype(BF)

    def back_up(self, b, i, tile=512):
        rows = span(i, tile)
        for c in range(3):
            cols = slice(c * 256, (c + 1) * 256)
            d_act = nt(self.low[rows, :], self.wdown[b * 768 + c * 256 : b * 768 + (c + 1) * 256, :])
            total = jnp.zeros((8, 256), F32)
            for at, part in parts(d_act, 32):
                here = pl.ds(i * tile + at, 32)
                d_up = (part * self.slope[b, here, cols].astype(F32)).astype(BF)
                self.slope[b, here, cols] = d_up
                total += eight(d_up.astype(F32))
            self.note(8 + b, total, cols)

    def grad_up(self, b):
        for c in range(3):
            cols = slice(c * 256, (c + 1) * 256)
            self.act[b, 0:768, cols] = tn(self.hidden[...], self.slope[b, :, cols]).astype(BF)

    def back_hidden(self, i):
        rows = span(i, TILE)
        for c in range(3):
            cols = slice(c * 256, (c + 1) * 256)
            back = nt(self.slope[0, rows, :], self.wup[cols, 0:768])
            for b in range(1, 4):
                back += nt(self.slope[b, rows, :], self.wup[cols, b * 768 : (b + 1) * 768])
            self.wide[rows, cols] += back
        totals = [jnp.zeros((8, 768), F32)] * 3
        for at in range(0, TILE, 32):
            here = pl.ds(i * TILE + at, 32)
            d_hidden = self.wide[here, :]
            normed = self.normed[here, :].astype(F32)
            scaled = d_hidden * self.lines[3:4]
            d_one = self.inverse[at : at + 32, i : i + 1] * (scaled - mean(scaled) - normed * mean(scaled * normed))
            totals = [old + eight(new) for old, new in zip(totals, (d_one, d_hidden * normed, d_hidden))]
            self.wide[here, :] = d_one
            self.low[here, :] = d_one.astype(BF)
        for row, total in zip((2, 3, 4), totals):
            self.note(row, total)

    def grad_out(self):
        for c in range(3):
            cols = slice(c * 256, (c + 1) * 256)
            self.slope[3, 0:768, cols] = tn(self.context[...], self.low[:, cols]).astype(BF)

    def back_context(self, i):
        rows = span(i, TILE)
        self.context[rows, :] = nt(self.low[rows, :], self.wout[...]).astype(BF)

    def back_attend(self, g, rows):
        chains = self.chains(g, rows)
        qkv = [[self.part(p, where, b) for b in range(3)] for r, p, where in chains]
        probs = [self.probs[r, p * 256 : (p + 1) * 256, :] for r, p, where in chains]
        d_context = [self.halves(self.context[where, p * 128 : (p + 1) * 128]) for r, p, where in chains]
        d_probs = [nt(down, v) for down, (q, k, v) in zip(d_context, qkv)]
        d_values = [tn(prob, down).astype(BF) for prob, down in zip(probs, d_context)]
        d_scores = []
        for prob, d_prob in zip(probs, d_probs):
            some = []
            for at, part in parts(d_prob, 128):
                wide = prob[at : at + 128].astype(F32)
                inner = jnp.sum(wide * part, axis=-1, keepdims=True)
                some.append((wide * (part - inner)).astype(BF))
            d_scores.append(some)
        d_queries = [(nn(jnp.concatenate(some, axis=1), self.halves(k)) * 0.125).astype(BF) for some, (q, k, v) in zip(d_scores, qkv)]
        d_keys = [tn(jnp.concatenate(some, axis=0), self.halves(q)).astype(BF) for some, (q, k, v) in zip(d_scores, qkv)]
        totals = {}
        for i, (r, p, where) in enumerate(chains):
            for b, grad in enumerate((d_queries[i], d_keys[i], d_values[i])):
                self.qkv[where, p * HALF + b * 128 : p * HALF + (b + 1) * 128] = grad
                if b != 1:
                    totals[b, p] = totals.get((b, p), 0.0) + eight(grad.astype(F32))
        for (b, p), total in totals.items():
            self.note(b // 2, total, slice(p * 128, (p + 1) * 128))

    def grad_qkv(self, g):
        for c in range(3):
            cols = slice(c * 256, (c + 1) * 256)
            grad = self.qkv[:, g * 768 + c * 256 : g * 768 + (c + 1) * 256]
            self.slope[g, 0:768, cols] = tn(self.tokens[...], grad).astype(BF)

    def back_tokens(self, i):
        rows = span(i, TILE)
        grad = self.wide[rows, :]
        for g in range(3):
            cols = slice(g * 768, (g + 1) * 768)
            grad += nt(self.qkv[rows, cols], self.wqkv[:, cols])
        self.wide[rows, :] = grad


LANES = np.stack([np.arange(3072) % 24, np.arange(3072) // 24, np.arange(3072) % 96, np.arange(3072) // 96] + [np.zeros(3072)] * 4).astype(np.int32)


def layer_kernel(
    tokens, cotangent, segments, live, predicted, targets, lanes, sqkv, sout, sup, sdown, vec,
    layer_out, grad_tokens, oqkv, oout, oup, odown, osums,
    wqkv, wout, wup, wdown, vecs, lines, up_bias, qkv_bias, partial, qkv, probs, context, normed, inverse, hidden, act, slope, wide, low, gdown,
    sums, pdown, land_up, land_down, whole, whole_down, totals, totals_down, lasts, lasts_down, stage, land,
    copies, sends, recvs, free, late,
):
    w = Wires(sends, recvs)
    core, chip = w.core, w.chip
    m = Layer(
        tokens=tokens, segments=segments, live=live, predicted=predicted, targets=targets, lanes=lanes, vecs=vecs,
        wqkv=wqkv, wout=wout, wup=wup, wdown=wdown, lines=lines, up_bias=up_bias, qkv_bias=qkv_bias, partial=partial, qkv=qkv, probs=probs,
        context=context, normed=normed, inverse=inverse, hidden=hidden, act=act, slope=slope, wide=wide, low=low, gdown=gdown,
        sums=sums, cotangent=gdown.at[0:1024], layer_out=gdown.at[1024:2048],
    )

    def block(b):
        return (wqkv, b * 768) if b < 3 else (wout, 0) if b < 4 else (wup, (b - 4) * 768)

    def shard(b, h):
        if b < 3:
            return jnp.concatenate([sqkv[:, i * 768 + (2 * b + h) * 128 : i * 768 + (2 * b + h + 1) * 128] for i in range(3)], axis=1)
        ref, at = (sout, 0) if b < 4 else (sup, (b - 4) * 768)
        return ref[:, at + h * HALF : at + (h + 1) * HALF]

    def packed(first, b, core_rows=0):
        rows = pl.ds(pl.multiple_of(first + core_rows + (b // 2) * 32, 16), 32)
        return rows, slice((b % 2) * HALF, (b % 2 + 1) * HALF)

    def exchange():
        for h in (0, 1):
            for b in range(8):
                rows, cols = packed(2048 + h * 128, b)
                gdown[rows, cols] = jnp.concatenate([shard(b, h).astype(F32), jnp.zeros((8, HALF), F32)], axis=0).astype(BF)
        w.barrier()
        there = w.partner()
        first = pl.ds(pl.multiple_of(2048 + (1 - core) * 128, 16), 64)
        second = pl.ds(pl.multiple_of(2112 + (1 - core) * 128, 16), 64)
        one = w.send(gdown.at[first, :], gdown.at[2304:2368, :], there)
        spread.step()
        two = w.send(gdown.at[second, :], gdown.at[2368:2432, :], there)
        three = []
        for j in range(3):
            cols = pl.ds(pl.multiple_of(j * 256 + (1 - core) * 128, 128), 128)
            three.append(w.send(sdown.at[:, cols], gdown.at[2432:2528, j * 128 : (j + 1) * 128], there))

        def merge(b):
            rows, cols = packed(2048, b, core * 128)
            own = gdown[rows, cols].astype(F32)[:24]
            rows, cols = packed(2304, b)
            got = gdown[rows, cols].astype(F32)[:24]
            low_rows, high_rows = jnp.where(core == 0, own, got), jnp.where(core == 0, got, own)
            ref, at = block(b)
            ref[rows_at(chip, 1, 48), pl.ds(pl.multiple_of(at + core * HALF, 128), HALF)] = jnp.concatenate(
                [low_rows, high_rows], axis=0
            ).astype(BF)

        one.wait_recv()
        for b in range(4):
            merge(b)
        return merge, two, three

    def exchange_rest(merge, two, three):
        two.wait_recv()
        for b in range(4, 8):
            merge(b)
        arrived(three)
        for j in range(3):
            cols = pl.ds(pl.multiple_of(j * 256 + core * 128, 128), 128)
            wdown[pl.ds(pl.multiple_of(chip * 192 + core * 96, 16), 96), cols] = sdown[:, cols]
            wdown[pl.ds(pl.multiple_of(chip * 192 + (1 - core) * 96, 16), 96), cols] = gdown[2432:2528, j * 128 : (j + 1) * 128]

    spread = Spread(w, vecs)
    pieces = {SPREAD: spread}
    for i, (b, offset, width, order) in enumerate(GATHERS):
        if b < 8:
            ref, at = block(b)
            pieces[GATHER + i] = Gather(w, ref, 48, at + core * HALF + offset, width, order)
        else:
            pieces[GATHER + i] = Gather(w, wdown, 192, (b - 8) * 256 + core * 128, 128, order)

    def writer(b, offset, width):
        def write(which, value):
            for i in range(width // 128):
                part = i + offset // 128
                if b < 3:
                    ref, at = oqkv, part * 768 + 2 * b * 128 + which * 128
                elif b < 8:
                    ref, at = (oout if b < 4 else oup), max(b - 4, 0) * 768 + part * 128 + which * HALF
                else:
                    ref, at = odown, (b - 8) * 256 + which * 128
                ref[:, pl.ds(pl.multiple_of(at, 128), 128)] = value[:, i * 128 : (i + 1) * 128]

        return write

    def alone(body, *args):
        @pl.when(core >= 0)
        def _():
            body(*args)

    class Gate:
        def __init__(self, semaphore, count):
            self.semaphore, self.count, self.passed = semaphore, count, False

        def __call__(self):
            if not self.passed:
                pl.semaphore_wait(self.semaphore, self.count)
                self.passed = True

    ready, gate, always = Gate(free, 1), Gate(late, 5), lambda: None
    finished = {"back_up": 0, "back_hidden": 0, "grad_down": 0, "back_attend": 0}

    def last_of(name, count):
        finished[name] += 1
        return finished[name] == count

    def back_hidden(i):
        alone(m.back_hidden, i)
        if last_of("back_hidden", 4):
            for peer in [w.over_x(), w.over_y()] + [w.along_z(j) for j in (1, 2, 3)]:
                pl.semaphore_signal(late, inc=1, device_id=peer, device_id_type=MESH)

    for i, (b, offset, width, order) in enumerate(SCATTERS):
        cols = slice(offset, offset + width)
        if b < 8:
            ref = slope.at[b, 0:768] if b < 3 else slope.at[3, 0:768] if b < 4 else act.at[b - 4, 0:768]
            p = wdown.at[(b // 2) * 768 : (b // 2 + 1) * 768, (b % 2) * HALF + offset : (b % 2) * HALF + offset + width]
            land_at = wup.at[0:720, b * 768 + offset : b * 768 + offset + width] if b < 4 else land_up.at[b - 4, :, cols]
            pieces[SCATTER + i] = Scatter(
                w, ref, 48, core * HALF + offset, (1 - core) * HALF + offset, width, order, p, land_at, whole.at[:, cols],
                totals.at[b, :, cols], lasts.at[b, :, cols], writer(b, offset, width), ready, gate if b < 4 else always,
            )
        else:
            j = b - 8
            pieces[SCATTER + i] = Scatter(
                w, gdown, 192, j * 256 + core * 128, j * 256 + (1 - core) * 128, 128, order, pdown.at[j], land_down.at[j], whole_down,
                totals_down.at[j], lasts_down.at[j], writer(b, 0, 128), always, always,
            )
    pieces[SUMS] = Sums(w, sums, stage, land, osums)
    held = {}

    def local(source, target, i):
        held[i] = pltpu.make_async_copy(source, target, copies.at[i])
        held[i].start()

    def start():
        local(cotangent, gdown.at[0:1024], 0)
        vecs[pl.ds(pl.multiple_of((chip * 2 + core) * 8, 8), 8), :] = vec[...]
        sums[...] = jnp.zeros_like(sums)
        partial[...] = jnp.zeros_like(partial)
        held["rest"] = exchange()

    def first():
        alone(m.vectors)
        alone(m.tally)

    def down(i):
        if i == 0:
            held[0].wait()
        alone(m.down, i)
        rows = slice(i * TILE, (i + 1) * TILE)
        local(gdown.at[1024 + i * TILE : 1024 + (i + 1) * TILE], layer_out.at[rows], 1 + i)

    def grad_down(j):
        if last_of("grad_down", 1):
            w.drain()
            for i in range(4):
                held[1 + i].wait()
        alone(m.grad_down, j)

    def back_up(b):
        alone(lambda: [m.back_up(b, i) for i in (0, 1)])
        if last_of("back_up", 4):
            pl.semaphore_signal(free, inc=1, device_id=w.partner(), device_id_type=MESH)

    def grad_up(b):
        alone(m.grad_up, b)

    def back_attend(g, h):
        alone(m.back_attend, g, range(4 * h, 4 * h + 4))
        if last_of("back_attend", 6):
            alone(m.fold)

    def back_tokens(i):
        alone(m.back_tokens, i)
        rows = slice(i * TILE, (i + 1) * TILE)
        local(wide.at[rows], grad_tokens.at[rows], 5 + i)

    parts_of_work = {"start": start, "rest": lambda: exchange_rest(*held["rest"]), "first": first}

    def add(name, body, *args):
        parts_of_work[name] = functools.partial(body, *args)

    for g in range(3):
        add(f"proj{g}", alone, lambda g=g: [m.project(g, i) for i in range(4)])
        add(f"gq{g}", alone, m.grad_qkv, g)
        for h in (0, 1):
            add(f"att{g}{h}", alone, m.attend, g, range(4 * h, 4 * h + 4))
            add(f"ba{g}{h}", back_attend, g, h)
    for h in (0, 1):
        add(f"out{h}", alone, lambda h=h: [m.out_project(i) for i in (2 * h, 2 * h + 1)])
    for j in range(3):
        add(f"gd{j}", grad_down, j)
    for i in range(4):
        add(f"up{i}0", alone, m.up, i, 0)
        add(f"up{i}1", alone, m.up, i, 1)
        add(f"down{i}", down, i)
        add(f"bu{i}", back_up, i)
        add(f"gu{i}", grad_up, i)
        add(f"bh{i}", back_hidden, i)
        add(f"bt{i}", back_tokens, i)
    add("go", alone, m.grad_out)
    add("bc", alone, lambda: [m.back_context(i) for i in range(4)])
    add("end", always)
    assert len(PLAN) == len(parts_of_work)
    for name, steps in PLAN:
        for i in steps:
            pieces[i].step()
        parts_of_work[name]()
    for i in range(4):
        held[5 + i].wait()
    w.drain()
    assert w.used <= SEMAPHORES, w.used


def layer(tokens, cotangent, segment_ids, live_mask, predicted, targets, w_qkv, w_out, w_up, w_down, vec):
    V = pl.BlockSpec(memory_space=pltpu.VMEM)
    A = pl.BlockSpec(memory_space=pl.ANY)
    return pl.pallas_call(
        layer_kernel,
        out_shape=(
            jax.ShapeDtypeStruct((1024, 768), BF),
            jax.ShapeDtypeStruct((1024, 768), F32),
            jax.ShapeDtypeStruct((24, 2304), F32),
            jax.ShapeDtypeStruct((24, 768), F32),
            jax.ShapeDtypeStruct((24, 3072), F32),
            jax.ShapeDtypeStruct((96, 768), F32),
            jax.ShapeDtypeStruct((16, 768), F32),
        ),
        in_specs=[V, A] + [V] * 10,
        out_specs=[A] * 2 + [V] * 5,
        scratch_shapes=[
            pltpu.VMEM((768, 2304), BF),
            pltpu.VMEM((768, 768), BF),
            pltpu.VMEM((768, 3072), BF),
            pltpu.VMEM((3072, 768), BF),
            pltpu.VMEM((256, 128), F32),
            pltpu.VMEM((8, 768), F32),
            pltpu.VMEM((4, 1, 768), F32),
            pltpu.VMEM((3, 1, 768), F32),
            pltpu.VMEM((96, 768), F32),
            pltpu.VMEM((1024, 2304), BF),
            pltpu.VMEM((8, 1536, 128), BF),
            pltpu.VMEM((1024, 768), BF),
            pltpu.VMEM((1024, 768), BF),
            pltpu.VMEM((TILE, 128), F32),
            pltpu.VMEM((1024, 768), BF),
            pltpu.VMEM((4, 1024, 768), BF),
            pltpu.VMEM((4, 1024, 768), BF),
            pltpu.VMEM((1024, 768), F32),
            pltpu.VMEM((1024, 768), BF),
            pltpu.VMEM((3072, 768), BF),
            pltpu.VMEM((16, 768), F32),
            pltpu.VMEM((3, 3072, 128), BF),
            pltpu.VMEM((4, 720, HALF), BF),
            pltpu.VMEM((3, 2880, 128), BF),
            pltpu.VMEM((48, HALF), F32),
            pltpu.VMEM((192, 128), F32),
            pltpu.VMEM((8, 24, HALF), F32),
            pltpu.VMEM((3, 96, 128), F32),
            pltpu.VMEM((8, 24, HALF), F32),
            pltpu.VMEM((3, 96, 128), F32),
            pltpu.VMEM((4, 16, HALF), F32),
            pltpu.VMEM((6, 16, HALF), F32),
            pltpu.SemaphoreType.DMA((9,)),
            pltpu.SemaphoreType.DMA((SEMAPHORES,)),
            pltpu.SemaphoreType.DMA((SEMAPHORES,)),
            pltpu.SemaphoreType.REGULAR,
            pltpu.SemaphoreType.REGULAR,
        ],
        compiler_params=pltpu.CompilerParams(collective_id=0, has_side_effects=True, vmem_limit_bytes=64 * 2**20 - 2**17),
    )(
        tokens, cotangent, segment_ids, live_mask, predicted.reshape(8, 128), targets.reshape(8, 128), jnp.asarray(LANES),
        w_qkv, w_out, w_up, w_down, vec,
    )


def finish_kernel(a, b, c, d, e, f, sums, oa, ob, oc, od, oe, of, *rest):
    vectors, up_vector, tallies, buffers, semaphores = rest[:8], rest[8], rest[9], rest[10:16], rest[16]
    copies = []
    for old, new, buffer, cuts in zip((a, b, c, d, e, f), (oa, ob, oc, od, oe, of), buffers, (2, 4, 1, 1, 1, 1)):
        size = old.shape[0] // cuts
        for i in range(cuts):
            rows = pl.ds(i * size, size)
            number = len(copies)
            copies.append(
                (
                    pltpu.make_async_copy(old.at[rows], buffer.at[rows], semaphores.at[2 * number]),
                    pltpu.make_async_copy(buffer.at[rows], new.at[rows], semaphores.at[2 * number + 1]),
                )
            )
            copies[-1][0].start()
    device = lax.axis_index("dp") * 8 + lax.axis_index("fsdp")
    place = lax.broadcasted_iota(jnp.int32, (768, 128), 0)
    lane = lax.broadcasted_iota(jnp.int32, (768, 128), 1)

    def pick(value, first):
        hot = jnp.where(place == lane + first, 1.0, 0.0)
        return lax.dot_general(
            value, hot, (((1,), (0,)), ((), ())), precision=lax.Precision.HIGHEST, preferred_element_type=F32
        )

    own = pick(sums[0:8, :], device * 24)
    for i, out in enumerate(vectors):
        out[...] = own[i : i + 1, 0:24]
    row = sums[pl.ds(8 + device // 8, 1), :]
    up_vector[...] = pick(jnp.broadcast_to(row, (8, 768)), device % 8 * 96)[0:1, 0:96]
    tallies[...] = sums[12:14, 0:24].astype(jnp.int32)
    for copy_in, copy_out in copies:
        copy_in.wait()
        copy_out.start()
    for copy_in, copy_out in copies:
        copy_out.wait()


def finish(layer_out, grad_tokens, gqkv, gout, gup, gdown, sums):
    V = pl.BlockSpec(memory_space=pltpu.VMEM)
    A = pl.BlockSpec(memory_space=pl.ANY)
    arrays = (layer_out, grad_tokens, gqkv, gout, gup, gdown)
    return pl.pallas_call(
        finish_kernel,
        out_shape=tuple(jax.ShapeDtypeStruct(x.shape, x.dtype) for x in arrays)
        + (jax.ShapeDtypeStruct((1, 24), F32),) * 8
        + (jax.ShapeDtypeStruct((1, 96), F32), jax.ShapeDtypeStruct((2, 24), jnp.int32)),
        in_specs=[A] * 6 + [V],
        out_specs=[A] * 6 + [V] * 10,
        scratch_shapes=[pltpu.VMEM(x.shape, x.dtype) for x in arrays] + [pltpu.SemaphoreType.DMA((20,))],
        compiler_params=pltpu.CompilerParams(vmem_limit_bytes=63 * 2**20),
    )(*arrays, sums)


def plain_device(
    tokens,
    cotangent,
    segment_ids,
    live_mask,
    predicted,
    targets,
    w_qkv,
    bias_query,
    bias_value,
    w_out,
    bias_out,
    gain_attn,
    shift_attn,
    w_up,
    bias_up,
    w_down,
    bias_down,
    gain_ffn,
    shift_ffn,
):
    row_count, seq_len = segment_ids.shape
    classes = jnp.arange(CLASSES, dtype=jnp.int32)
    live_flat = live_mask.reshape(-1) == 1
    target_hits = (targets[:, None] == classes[None, :]) & live_flat[:, None]
    correct = target_hits & (predicted[:, None] == targets[:, None])
    local_tally = jnp.stack(
        [jnp.sum(correct, axis=0, dtype=jnp.int32), jnp.sum(target_hits, axis=0, dtype=jnp.int32)]
    )
    tallies = lax.psum(local_tally, ("dp", "fsdp"))
    (
        whole_qkv,
        whole_query_bias,
        whole_value_bias,
        whole_out,
        whole_out_bias,
        whole_gain_attn,
        whole_shift_attn,
        whole_up,
        whole_up_bias,
        whole_down,
        whole_down_bias,
        whole_gain_ffn,
        whole_shift_ffn,
    ) = (
        lax.all_gather(w_qkv, ("dp", "fsdp"), axis=0, tiled=True),
        lax.all_gather(bias_query, ("dp", "fsdp"), axis=0, tiled=True),
        lax.all_gather(bias_value, ("dp", "fsdp"), axis=0, tiled=True),
        lax.all_gather(w_out, ("dp", "fsdp"), axis=0, tiled=True),
        lax.all_gather(bias_out, ("dp", "fsdp"), axis=0, tiled=True),
        lax.all_gather(gain_attn, ("dp", "fsdp"), axis=0, tiled=True),
        lax.all_gather(shift_attn, ("dp", "fsdp"), axis=0, tiled=True),
        lax.all_gather(w_up, ("dp", "fsdp"), axis=0, tiled=True),
        lax.all_gather(bias_up, ("dp", "fsdp"), axis=0, tiled=True),
        lax.all_gather(w_down, ("dp", "fsdp"), axis=0, tiled=True),
        lax.all_gather(bias_down, ("dp", "fsdp"), axis=0, tiled=True),
        lax.all_gather(gain_ffn, ("dp", "fsdp"), axis=0, tiled=True),
        lax.all_gather(shift_ffn, ("dp", "fsdp"), axis=0, tiled=True),
    )
    projected = jnp.dot(tokens, whole_qkv, preferred_element_type=jnp.float32)
    queries = (projected[:, :D] + whole_query_bias.astype(jnp.float32)).astype(jnp.bfloat16)
    keys_part = projected[:, D : 2 * D].astype(jnp.bfloat16)
    values = (projected[:, 2 * D :] + whole_value_bias.astype(jnp.float32)).astype(jnp.bfloat16)
    query_heads = split_heads(queries, row_count, seq_len)
    key_heads = split_heads(keys_part, row_count, seq_len)
    value_heads = split_heads(values, row_count, seq_len)
    diagonal = jnp.eye(seq_len, dtype=bool)
    allowed = (segment_ids[:, :, None] == segment_ids[:, None, :]) & (
        (live_mask[:, None, :] == 1) | diagonal[None]
    )
    scores = masked_scores(query_heads, key_heads, allowed)
    highest = jnp.max(scores, axis=-1, keepdims=True)
    raised = jnp.exp(scores - highest)
    total = jnp.sum(raised, axis=-1, keepdims=True)
    soft_weights = raised / total
    log_total = highest + jnp.log(total)
    context = (
        jnp.einsum(
            "bhqk,bkhc->bqhc",
            soft_weights.astype(jnp.bfloat16),
            value_heads,
            preferred_element_type=jnp.float32,
        )
        .reshape(-1, D)
        .astype(jnp.bfloat16)
    )
    attended = jnp.dot(
        context, whole_out, preferred_element_type=jnp.float32
    ) + whole_out_bias.astype(jnp.float32)
    hidden, normed_one, inverse_one = normalize(
        tokens.astype(jnp.float32) + attended,
        whole_gain_attn.astype(jnp.float32),
        whole_shift_attn.astype(jnp.float32),
    )
    hidden_low = hidden.astype(jnp.bfloat16)
    up_value = jnp.dot(
        hidden_low, whole_up, preferred_element_type=jnp.float32
    ) + whole_up_bias.astype(jnp.float32)
    activated_low = jax.nn.gelu(up_value, approximate=False).astype(jnp.bfloat16)
    ffn_out = jnp.dot(
        activated_low, whole_down, preferred_element_type=jnp.float32
    ) + whole_down_bias.astype(jnp.float32)
    layer_out, normed_two, inverse_two = normalize(
        hidden + ffn_out, whole_gain_ffn.astype(jnp.float32), whole_shift_ffn.astype(jnp.float32)
    )
    back_qkv, back_out, back_up, back_down, back_gain_attn, back_gain_ffn = (
        lax.all_gather(w_qkv, ("dp", "fsdp"), axis=0, tiled=True),
        lax.all_gather(w_out, ("dp", "fsdp"), axis=0, tiled=True),
        lax.all_gather(w_up, ("dp", "fsdp"), axis=0, tiled=True),
        lax.all_gather(w_down, ("dp", "fsdp"), axis=0, tiled=True),
        lax.all_gather(gain_attn, ("dp", "fsdp"), axis=0, tiled=True),
        lax.all_gather(gain_ffn, ("dp", "fsdp"), axis=0, tiled=True),
    )
    upstream = cotangent.astype(jnp.float32)
    grad_gain_ffn = jnp.sum(upstream * normed_two, axis=0)
    grad_shift_ffn = jnp.sum(upstream, axis=0)
    d_resid_two = normalize_back(
        upstream, normed_two, inverse_two, back_gain_ffn.astype(jnp.float32)
    )
    d_two_low = d_resid_two.astype(jnp.bfloat16)
    grad_down = contract_rows(activated_low, d_two_low)
    grad_down_bias = jnp.sum(d_resid_two, axis=0)
    d_activated = times_transposed(d_two_low, back_down)
    gelu_pullback = jax.vjp(partial(jax.nn.gelu, approximate=False), up_value)[1]
    d_up = gelu_pullback(d_activated)[0].astype(jnp.bfloat16)
    grad_up_bias = jnp.sum(d_up.astype(jnp.float32), axis=0)
    grad_up = contract_rows(hidden_low, d_up)
    d_hidden = d_resid_two + times_transposed(d_up, back_up)
    grad_gain_attn = jnp.sum(d_hidden * normed_one, axis=0)
    grad_shift_attn = jnp.sum(d_hidden, axis=0)
    d_resid_one = normalize_back(
        d_hidden, normed_one, inverse_one, back_gain_attn.astype(jnp.float32)
    )
    d_one_low = d_resid_one.astype(jnp.bfloat16)
    grad_out_bias = jnp.sum(d_resid_one, axis=0)
    grad_out = contract_rows(context, d_one_low)
    d_context = times_transposed(d_one_low, back_out).astype(jnp.bfloat16)
    d_context_heads = split_heads(d_context, row_count, seq_len)
    d_soft = jnp.einsum(
        "bqhc,bkhc->bhqk", d_context_heads, value_heads, preferred_element_type=jnp.float32
    )
    soft_again = jnp.exp(masked_scores(query_heads, key_heads, allowed) - log_total)
    d_values = (
        jnp.einsum(
            "bhqk,bqhc->bkhc",
            soft_again.astype(jnp.bfloat16),
            d_context_heads,
            preferred_element_type=jnp.float32,
        )
        .reshape(-1, D)
        .astype(jnp.bfloat16)
    )
    inner = jnp.sum(soft_again * d_soft, axis=-1, keepdims=True)
    d_scores = (soft_again * (d_soft - inner)).astype(jnp.bfloat16)
    d_queries = (
        (
            jnp.einsum("bhqk,bkhc->bqhc", d_scores, key_heads, preferred_element_type=jnp.float32)
            * HEAD_DIM ** (-0.5)
        )
        .reshape(-1, D)
        .astype(jnp.bfloat16)
    )
    d_keys = (
        (
            jnp.einsum("bhqk,bqhc->bkhc", d_scores, query_heads, preferred_element_type=jnp.float32)
            * HEAD_DIM ** (-0.5)
        )
        .reshape(-1, D)
        .astype(jnp.bfloat16)
    )
    d_projected = jnp.concatenate([d_queries, d_keys, d_values], axis=1)
    grad_query_bias = jnp.sum(d_queries.astype(jnp.float32), axis=0)
    grad_value_bias = jnp.sum(d_values.astype(jnp.float32), axis=0)
    grad_qkv = contract_rows(tokens, d_projected)
    grad_tokens = d_resid_one + times_transposed(d_projected, back_qkv)
    summed = tuple(
        (
            lax.psum_scatter(grad_qkv, ("dp", "fsdp"), scatter_dimension=0, tiled=True),
            lax.psum_scatter(grad_query_bias, ("dp", "fsdp"), scatter_dimension=0, tiled=True),
            lax.psum_scatter(grad_value_bias, ("dp", "fsdp"), scatter_dimension=0, tiled=True),
            lax.psum_scatter(grad_out, ("dp", "fsdp"), scatter_dimension=0, tiled=True),
            lax.psum_scatter(grad_out_bias, ("dp", "fsdp"), scatter_dimension=0, tiled=True),
            lax.psum_scatter(grad_gain_attn, ("dp", "fsdp"), scatter_dimension=0, tiled=True),
            lax.psum_scatter(grad_shift_attn, ("dp", "fsdp"), scatter_dimension=0, tiled=True),
            lax.psum_scatter(grad_up, ("dp", "fsdp"), scatter_dimension=0, tiled=True),
            lax.psum_scatter(grad_up_bias, ("dp", "fsdp"), scatter_dimension=0, tiled=True),
            lax.psum_scatter(grad_down, ("dp", "fsdp"), scatter_dimension=0, tiled=True),
            lax.psum_scatter(grad_down_bias, ("dp", "fsdp"), scatter_dimension=0, tiled=True),
            lax.psum_scatter(grad_gain_ffn, ("dp", "fsdp"), scatter_dimension=0, tiled=True),
            lax.psum_scatter(grad_shift_ffn, ("dp", "fsdp"), scatter_dimension=0, tiled=True),
        )
    )
    return (layer_out.astype(jnp.bfloat16), grad_tokens) + summed + (tallies,)


def fast_device(
    tokens,
    cotangent,
    segment_ids,
    live_mask,
    predicted,
    targets,
    w_qkv,
    bias_query,
    bias_value,
    w_out,
    bias_out,
    gain_attn,
    shift_attn,
    w_up,
    bias_up,
    w_down,
    bias_down,
    gain_ffn,
    shift_ffn,
):

    small = jnp.stack([bias_query, bias_value, bias_out, gain_attn, shift_attn, bias_down, gain_ffn, shift_ffn]).astype(F32)
    vec = jnp.concatenate([small, jnp.zeros((8, 8), F32), jnp.pad(bias_up.astype(F32)[None], ((0, 7), (0, 0)))], axis=1)
    results = finish(
        *layer(tokens, cotangent, segment_ids, live_mask, predicted, targets, w_qkv, w_out, w_up, w_down, vec)
    )
    layer_out, grad_tokens, gqkv, gout, gup, gdown = results[:6]
    lines = [line.reshape(24) for line in results[6:14]]
    return (
        layer_out, grad_tokens, gqkv, lines[0], lines[1], gout, lines[2], lines[3], lines[4], gup, results[14].reshape(96), gdown,
        lines[5], lines[6], lines[7], results[15],
    )


def solution(mesh):
    in_specs = (
        P(("dp", "fsdp"), None),
        P(("dp", "fsdp"), None),
        P(("dp", "fsdp"), None),
        P(("dp", "fsdp"), None),
        P(("dp", "fsdp")),
        P(("dp", "fsdp")),
        P(("dp", "fsdp"), None),
        P(("dp", "fsdp")),
        P(("dp", "fsdp")),
        P(("dp", "fsdp"), None),
        P(("dp", "fsdp")),
        P(("dp", "fsdp")),
        P(("dp", "fsdp")),
        P(("dp", "fsdp"), None),
        P(("dp", "fsdp")),
        P(("dp", "fsdp"), None),
        P(("dp", "fsdp")),
        P(("dp", "fsdp")),
        P(("dp", "fsdp")),
    )
    out_specs = (
        P(("dp", "fsdp"), None),
        P(("dp", "fsdp"), None),
        P(("dp", "fsdp"), None),
        P(("dp", "fsdp")),
        P(("dp", "fsdp")),
        P(("dp", "fsdp"), None),
        P(("dp", "fsdp")),
        P(("dp", "fsdp")),
        P(("dp", "fsdp")),
        P(("dp", "fsdp"), None),
        P(("dp", "fsdp")),
        P(("dp", "fsdp"), None),
        P(("dp", "fsdp")),
        P(("dp", "fsdp")),
        P(("dp", "fsdp")),
        P(),
    )
    fast = tuple(mesh.shape.items()) == (("dp", 4), ("fsdp", 8))
    return jax.shard_map(
        fast_device if fast else plain_device, mesh=mesh, in_specs=in_specs, out_specs=out_specs, check_vma=False
    )
```

```python
import functools
from functools import partial

import jax
import jax.numpy as jnp
import numpy as np
from jax import lax
from jax.experimental import pallas as pl
from jax.experimental.pallas import tpu as pltpu
from jax.sharding import PartitionSpec as P

D = 768
HEADS = 12
HEAD_DIM = 64
CLASSES = 24


EPSILON = 1e-05


def normalize(operand, scale_vec, shift_vec):
    center = operand - jnp.mean(operand, axis=-1, keepdims=True)
    inverse = lax.rsqrt(jnp.mean(center * center, axis=-1, keepdims=True) + EPSILON)
    normed = center * inverse
    return (normed * scale_vec + shift_vec, normed, inverse)


def normalize_back(grad_out, normed, inverse, scale_vec):
    scaled = grad_out * scale_vec
    return inverse * (
        scaled
        - jnp.mean(scaled, axis=-1, keepdims=True)
        - normed * jnp.mean(scaled * normed, axis=-1, keepdims=True)
    )


def contract_rows(left, right):
    return lax.dot_general(
        left, right, (((0,), (0,)), ((), ())), preferred_element_type=jnp.float32
    )


def times_transposed(left, right):
    return lax.dot_general(
        left, right, (((1,), (1,)), ((), ())), preferred_element_type=jnp.float32
    )


def split_heads(matrix, row_count, seq_len):
    return matrix.reshape(row_count, seq_len, HEADS, HEAD_DIM)


def masked_scores(query_heads, key_heads, allowed):
    scores = jnp.einsum(
        "bqhc,bkhc->bhqk", query_heads, key_heads, preferred_element_type=jnp.float32
    ) * HEAD_DIM ** (-0.5)
    return jnp.where(allowed[:, None], scores, -1000000000.0)


MESH = pl.DeviceIdType.MESH
BF = jnp.bfloat16
F32 = jnp.float32
HALF = 384


def place():
    dp, fsdp = lax.axis_index("dp"), lax.axis_index("fsdp")
    return dp // 2, dp % 2, fsdp // 2, fsdp % 2


class Wires:
    def __init__(self, send_sems, recv_sems):
        self.y, self.x, self.z, self.core = place()
        self.plane = self.y * 2 + self.x
        self.chip = self.plane * 4 + self.z
        self.send_sems, self.recv_sems, self.used, self.open = send_sems, recv_sems, 0, []

    def device(self, y=None, x=None, z=None, core=None):
        y = self.y if y is None else y
        x = self.x if x is None else x
        z = self.z if z is None else z
        core = self.core if core is None else core
        return (y * 2 + x, z * 2 + core)

    def partner(self):
        return self.device(core=1 - self.core)

    def over_x(self):
        return self.device(x=1 - self.x)

    def over_y(self):
        return self.device(y=1 - self.y)

    def along_z(self, jump):
        return self.device(z=(self.z + jump) % 4)

    def greet(self):
        semaphore = pltpu.get_barrier_semaphore()
        peers = [self.partner(), self.over_x(), self.over_y()] + [self.along_z(j) for j in (1, 2, 3)]
        for peer in peers:
            pl.semaphore_signal(semaphore, inc=1, device_id=peer, device_id_type=MESH)

    def meet(self):
        pl.semaphore_wait(pltpu.get_barrier_semaphore(), 6)

    def send(self, source, target, device):
        number = self.used
        self.used += 1
        copy = pltpu.make_async_remote_copy(
            src_ref=source,
            dst_ref=target,
            send_sem=self.send_sems.at[number],
            recv_sem=self.recv_sems.at[number],
            device_id=device,
            device_id_type=MESH,
        )
        copy.start()
        self.open.append(copy)
        return copy

    def drain(self):
        for copy in self.open:
            copy.wait_send()
        self.open = []


def arrived(copies):
    for copy in copies:
        copy.wait_recv()


def rows_at(start, count, slab):
    return pl.ds(pl.multiple_of(start * slab, 16), count * slab)


class Piece:
    at = 0

    def step(self):
        self.steps[self.at]()
        self.at += 1


class Gather(Piece):
    def __init__(self, wires, ref, slab, first, width, order):
        self.w, self.ref, self.slab, self.width, self.first = wires, ref, slab, width, first
        self.back = []
        self.steps = {
            "A": [self.z0, self.a1, self.a2, self.a3],
            "B": [self.z0, self.b1, self.b2, self.b3],
            "C": [self.c0, self.c1, self.c2, self.c3],
        }[order] + [self.done]

    def send(self, slabs, count, device):
        part = self.ref.at[rows_at(slabs, count, self.slab), pl.ds(pl.multiple_of(self.first, 128), self.width)]
        return self.w.send(part, part, device)

    def hand(self, slabs, count):
        self.back.append(self.send(slabs, count, self.w.partner()))

    def z0(self):
        self.into = [self.send(self.w.chip, 1, self.w.along_z(j)) for j in (1, 2, 3)]

    def a1(self):
        w = self.w
        arrived(self.into)
        self.into = [self.send(w.plane * 4, 4, w.over_x())]
        self.hand(w.plane * 4, 4)

    def a2(self):
        w = self.w
        arrived(self.into)
        self.into = [self.send(w.y * 8, 8, w.over_y())]
        self.hand((w.y * 2 + 1 - w.x) * 4, 4)

    def a3(self):
        arrived(self.into)
        self.hand((1 - self.w.y) * 8, 8)

    def b1(self):
        w = self.w
        arrived(self.into)
        self.into = [self.send(w.plane * 4, 4, w.over_y())]
        self.hand(w.plane * 4, 4)

    def b2(self):
        w = self.w
        arrived(self.into)
        other = ((1 - w.y) * 2 + w.x) * 4
        self.into = [self.send(w.plane * 4, 4, w.over_x()), self.send(other, 4, w.over_x())]
        self.hand(other, 4)

    def b3(self):
        w = self.w
        arrived(self.into)
        for y in (0, 1):
            self.hand((y * 2 + 1 - w.x) * 4, 4)

    def c0(self):
        self.into = [self.send(self.w.chip, 1, self.w.over_x())]

    def c1(self):
        w = self.w
        arrived(self.into)
        self.into = [self.send((w.y * 2 + x) * 4 + w.z, 1, w.over_y()) for x in (0, 1)]

    def c2(self):
        w = self.w
        arrived(self.into)
        self.into = [self.send(plane * 4 + w.z, 1, w.along_z(j)) for j in (1, 2, 3) for plane in range(4)]
        for plane in range(4):
            self.hand(plane * 4 + w.z, 1)

    def c3(self):
        w = self.w
        arrived(self.into)
        for j in (1, 2, 3):
            for plane in range(4):
                self.hand(plane * 4 + (w.z + j) % 4, 1)

    def done(self):
        arrived(self.back)


def add_rows(target, first, count, source, start):
    tile = 96 if count % 96 == 0 else 48

    def body(i, carry):
        there = pl.ds(pl.multiple_of(first + i * tile, 16), tile)
        target[there, :] = target[there, :] + source[pl.ds(pl.multiple_of(start + i * tile, 16), tile), :]
        return carry

    lax.fori_loop(0, count // tile, body, 0)


SIZES = {"A": (8, 4, 3), "B": (8, 4, 3), "C": (2, 1, 12)}


class Scatter(Piece):
    def __init__(self, wires, ref, slab, first, far, width, order, p, land, whole, total, last, write, ready, gate):
        self.w, self.ref, self.slab, self.first, self.far, self.width = wires, ref, slab, first, far, width
        self.p, self.whole, self.total, self.last = p, whole, total, last
        self.write, self.ready, self.gate = write, ready, gate
        self.mine = ref.at[:, pl.ds(pl.multiple_of(first, 128), width)]
        one, two, three = (12, 14, 0) if order == "C" else (0, 8, 12)
        self.r1, self.r2, self.rz = (land.at[at * slab : (at + size) * slab, :] for at, size in zip((one, two, three), SIZES[order]))
        self.steps = {
            "A": [self.p0, self.a1, self.a2, self.a3, self.z4],
            "B": [self.p0, self.b1, self.b2, self.b3, self.z4],
            "C": [self.p0, self.c1, self.c2, self.c3, self.c4],
        }[order] + [self.done]

    def rows(self, slabs, count):
        return self.ref.at[rows_at(slabs, count, self.slab), pl.ds(pl.multiple_of(self.first, 128), self.width)]

    def slot(self, buffer, slabs, count):
        return buffer.at[pl.ds(slabs * self.slab, count * self.slab), :]

    def add(self, slabs, count, source, start):
        add_rows(self.mine, slabs * self.slab, count * self.slab, source, start * self.slab)

    def p0(self):
        self.ready()
        far = self.ref.at[:, pl.ds(pl.multiple_of(self.far, 128), self.width)]
        self.into = [self.w.send(far, self.p, self.w.partner())]

    def a1(self):
        w = self.w
        self.gate()
        arrived(self.into)
        self.add((1 - w.y) * 8, 8, self.p, (1 - w.y) * 8)
        self.into = [w.send(self.rows((1 - w.y) * 8, 8), self.r1, w.over_y())]
        self.add(w.y * 8, 8, self.p, w.y * 8)

    def a2(self):
        w = self.w
        arrived(self.into)
        other = (w.y * 2 + 1 - w.x) * 4
        self.add(other, 4, self.r1, (1 - w.x) * 4)
        self.into = [w.send(self.rows(other, 4), self.r2, w.over_x())]
        self.add(w.plane * 4, 4, self.r1, w.x * 4)

    def a3(self):
        arrived(self.into)
        self.z3()

    def b1(self):
        w = self.w
        self.gate()
        arrived(self.into)
        self.into = []
        for y in (0, 1):
            slabs = (y * 2 + 1 - w.x) * 4
            self.add(slabs, 4, self.p, slabs)
            self.into.append(w.send(self.rows(slabs, 4), self.slot(self.r1, y * 4, 4), w.over_x()))
        for y in (0, 1):
            slabs = (y * 2 + w.x) * 4
            self.add(slabs, 4, self.p, slabs)

    def b2(self):
        w = self.w
        arrived(self.into)
        other = ((1 - w.y) * 2 + w.x) * 4
        self.add(other, 4, self.r1, (1 - w.y) * 4)
        self.into = [w.send(self.rows(other, 4), self.r2, w.over_y())]
        self.add(w.plane * 4, 4, self.r1, w.y * 4)

    def b3(self):
        arrived(self.into)
        self.z3()

    def z3(self):
        w = self.w
        self.add(w.plane * 4, 4, self.r2, 0)
        self.into = []
        for j in (1, 2, 3):
            there = (w.z + j) % 4
            self.into.append(w.send(self.rows(w.plane * 4 + there, 1), self.slot(self.rz, j - 1, 1), w.along_z(j)))

    def z4(self):
        arrived(self.into)
        self.close([self.slot(self.rz, j, 1) for j in range(3)])

    def c1(self):
        w = self.w
        self.gate()
        arrived(self.into)
        self.add(0, 16, self.p, 0)
        self.into = []
        for j in (1, 2, 3):
            for plane in range(4):
                there = self.rows(plane * 4 + (w.z + j) % 4, 1)
                self.into.append(w.send(there, self.slot(self.rz, (j - 1) * 4 + plane, 1), w.along_z(j)))

    def c2(self):
        w = self.w
        arrived(self.into)
        for plane in range(4):
            for j in range(3):
                self.add(plane * 4 + w.z, 1, self.rz, j * 4 + plane)
        self.into = []
        for x in (0, 1):
            there = self.rows(((1 - w.y) * 2 + x) * 4 + w.z, 1)
            self.into.append(w.send(there, self.slot(self.r1, x, 1), w.over_y()))

    def c3(self):
        w = self.w
        arrived(self.into)
        for x in (0, 1):
            self.add((w.y * 2 + x) * 4 + w.z, 1, self.r1, x)
        self.into = [w.send(self.rows((w.y * 2 + 1 - w.x) * 4 + w.z, 1), self.slot(self.r2, 0, 1), w.over_x())]

    def c4(self):
        arrived(self.into)
        self.close([self.slot(self.r2, 0, 1)])

    def close(self, others):
        w = self.w
        total = self.rows(w.chip, 1)[...].astype(F32)
        for other in others:
            total = total + other[...].astype(F32)
        self.whole[...] = total
        half = self.slab // 2
        self.total[...] = self.whole[pl.ds(pl.multiple_of((1 - w.core) * half, 8), half), :]
        self.into = [w.send(self.total, self.last, w.partner())]
        self.write(w.core, self.whole[pl.ds(pl.multiple_of(w.core * half, 8), half), :])

    def done(self):
        arrived(self.into)
        self.write(1 - self.w.core, self.last[...])


class Spread(Piece):
    def __init__(self, wires, tiles):
        self.w, self.tiles = wires, tiles
        self.steps = [self.s0, self.s1, self.s2, self.s3, self.s4]

    def send(self, start, count, device):
        part = self.tiles.at[pl.ds(pl.multiple_of(start * 8, 8), count * 8), :]
        return self.w.send(part, part, device)

    def s0(self):
        w = self.w
        self.into = [self.send(w.chip * 2 + w.core, 1, w.partner())]

    def s1(self):
        w = self.w
        arrived(self.into)
        self.into = [self.send(w.chip * 2, 2, w.along_z(j)) for j in (1, 2, 3)]

    def s2(self):
        arrived(self.into)
        self.into = [self.send(self.w.plane * 8, 8, self.w.over_x())]

    def s3(self):
        arrived(self.into)
        self.into = [self.send(self.w.y * 16, 16, self.w.over_y())]

    def s4(self):
        arrived(self.into)


class Sums(Piece):
    def __init__(self, wires, sums, stage, land, last):
        self.w, self.sums, self.stage, self.land, self.last = wires, sums, stage, land, last
        self.half = pl.ds(pl.multiple_of(wires.core * HALF, 128), HALF)
        self.steps = [self.s0, self.s1, self.s2, self.s3, self.s4, self.s5]

    def s0(self):
        far = pl.ds(pl.multiple_of((1 - self.w.core) * HALF, 128), HALF)
        self.into = [self.w.send(self.sums.at[:, far], self.land.at[0], self.w.partner())]

    def relay(self, value, at, device):
        self.stage[at] = value
        self.into = [self.w.send(self.stage.at[at], self.land.at[at + 1], device)]

    def s1(self):
        arrived(self.into)
        self.relay(self.sums[:, self.half] + self.land[0], 0, self.w.over_x())

    def s2(self):
        arrived(self.into)
        self.relay(self.stage[0] + self.land[1], 1, self.w.over_y())

    def s3(self):
        arrived(self.into)
        self.stage[2] = self.stage[1] + self.land[2]
        self.into = [self.w.send(self.stage.at[2], self.land.at[2 + j], self.w.along_z(j)) for j in (1, 2, 3)]

    def s4(self):
        arrived(self.into)
        self.stage[3] = self.stage[2] + self.land[3] + self.land[4] + self.land[5]
        self.last[:, self.half] = self.stage[3]
        self.into = [self.w.send(self.stage.at[3], self.last.at[:, self.half], self.w.partner())]

    def s5(self):
        arrived(self.into)


GATHER, SCATTER, SPREAD, SUMS, SEMAPHORES = 0, 40, 80, 81, 400
GATHERS = (
    (0, 0, 128, "B"),
    (0, 128, 128, "B"),
    (0, 256, 128, "A"),
    (1, 0, 384, "A"),
    (2, 0, 384, "B"),
    (3, 0, 384, "C"),
    (4, 0, 384, "B"),
    (5, 0, 384, "B"),
    (6, 0, 384, "A"),
    (7, 0, 384, "B"),
    (8, 0, 128, "A"),
    (9, 0, 128, "B"),
    (10, 0, 128, "C"),
)
SCATTERS = (
    (8, 0, 128, "A"),
    (9, 0, 128, "A"),
    (10, 0, 128, "B"),
    (4, 0, 384, "B"),
    (5, 0, 384, "A"),
    (6, 0, 384, "B"),
    (7, 0, 384, "C"),
    (3, 0, 384, "A"),
    (0, 0, 384, "B"),
    (1, 0, 256, "A"),
    (1, 256, 128, "B"),
    (2, 0, 128, "B"),
    (2, 128, 128, "A"),
    (2, 256, 128, "B"),
)
PLAN = (
    ("start", ()),
    ("rest", (0, 80)),
    ("first", (1, 2, 4, 0, 3, 80, 1, 2, 7, 0, 80, 4, 6, 5, 1, 2, 3, 8, 80)),
    ("proj0", (0, 7, 5, 12, 10, 1, 4, 0, 6, 2, 9, 1, 3, 8, 12, 2)),
    ("att00", (11, 7, 5)),
    ("att01", (10,)),
    ("proj1", (6, 4, 9, 8, 4, 11, 3, 12, 3)),
    ("att10", (7, 9)),
    ("att11", ()),
    ("proj2", ()),
    ("att20", (7, 10)),
    ("att21", ()),
    ("out0", (8, 5, 6, 8, 11, 5)),
    ("out1", ()),
    ("up00", (6,)),
    ("up01", ()),
    ("up10", ()),
    ("up11", (9,)),
    ("up20", ()),
    ("up21", ()),
    ("up30", (10, 9)),
    ("up31", ()),
    ("dm0", (10,)),
    ("dm1", (11, 12, 11)),
    ("dm2", (12,)),
    ("de0", ()),
    ("de1", ()),
    ("de2", ()),
    ("de3", ()),
    ("gd0", ()),
    ("gd2", (40,)),
    ("bu3", (42,)),
    ("gd1", (40,)),
    ("bu1", (41, 42)),
    ("bu2", ()),
    ("bu0", (41,)),
    ("gu0", ()),
    ("gu3", (43,)),
    ("bh3", (46,)),
    ("gu1", (40, 43)),
    ("gu2", (46, 44, 42)),
    ("bh2", (45,)),
    ("bh1", (44,)),
    ("bh0", (45, 40, 41)),
    ("go", ()),
    ("bc", (47, 42)),
    ("ba01", (43,)),
    ("ba00", (47,)),
    ("gq0", ()),
    ("ba20", (44, 48)),
    ("ba10", (46, 45)),
    ("ba21", ()),
    ("ba11", (48, 43)),
    ("gq1", (40, 41, 81)),
    ("bt0", (49, 50)),
    ("bt3", (44, 40, 81, 47, 42)),
    ("gq2", (46, 49, 50)),
    ("bt2", (52, 53, 51, 42, 43)),
    ("bt1", (45, 81, 48)),
    ("end", (52, 53, 41, 51, 43, 47, 46, 49, 44, 41, 81, 50, 46, 44, 45, 48, 53, 52, 51, 45, 50, 47, 49, 81, 53, 47, 52, 51, 81, 48, 50, 48, 49, 50, 53, 52, 49, 51, 53, 52, 51)),
)


TOKENS = 1024
TILE = 256


def nn(left, right):
    return jnp.dot(left, right, preferred_element_type=F32)


def nt(left, right):
    return lax.dot_general(left, right, (((1,), (1,)), ((), ())), preferred_element_type=F32)


def tn(left, right):
    return lax.dot_general(left, right, (((0,), (0,)), ((), ())), preferred_element_type=F32)


def loop(start, stop, body):
    def step(i, carry):
        body(i)
        return carry

    lax.fori_loop(start, stop, step, 0)


def span(i, size):
    return slice(i * size, (i + 1) * size) if isinstance(i, int) else pl.ds(pl.multiple_of(i * size, size), size)


def row_sum(value):
    return jnp.sum(value, axis=0, keepdims=True)


def parts(value, size):
    return [(i, value[i : i + size]) for i in range(0, value.shape[0], size)]


def eight(value):
    return jnp.sum(value.reshape(value.shape[0] // 8, 8, value.shape[1]), axis=0)


def mean(value):
    return jnp.mean(value, axis=-1, keepdims=True)


def gelu_both(up):
    density = jnp.exp(up * up * -0.5)
    base = jnp.abs(up) * (0.3275911 * 0.5**0.5) + 1.0
    guess = pltpu.reciprocal(base, approx=True)
    t = guess * (2.0 - base * guess)
    poly = t * (0.127414796 + t * (-0.142248368 + t * (0.7107068705 + t * (-0.7265760135 + t * 0.5307027145))))
    tail = poly * density
    below = jnp.where(up >= 0, 1.0 - tail, tail)
    return up * below, below + up * density * 0.3989422804014327


class Layer:
    def __init__(self, **refs):
        self.__dict__.update(refs)

    def vectors(self):
        line = lambda i, n: self.lanes[i : i + 1, 0:n]
        place = lax.broadcasted_iota(jnp.int32, (128, 768), 0)
        hot = (place == line(0, 768)).astype(F32).astype(BF)
        spread = nn(self.vecs[...].astype(BF), hot).reshape(32, 8, 768)
        owner = lax.broadcasted_iota(jnp.int32, (32, 8, 768), 0)
        self.lines[...] = jnp.sum(jnp.where(owner == line(1, 768)[None], spread, 0.0), axis=0)
        nothing = jnp.zeros((1, 128), F32)
        for g in range(3):
            parts = []
            for p in (2 * g, 2 * g + 1):
                cols = slice(p * 128, (p + 1) * 128)
                parts += [self.lines[0:1, cols], nothing, self.lines[1:2, cols]]
            self.qkv_bias[g] = jnp.concatenate(parts, axis=1)
        firsts = self.vecs[pl.ds(0, 32, 8), :].astype(BF)
        for b in range(4):
            place = lax.broadcasted_iota(jnp.int32, (128, 768), 0)
            cols = slice(b * 768, (b + 1) * 768)
            hot = (place == self.lanes[2:3, cols] + 32).astype(F32).astype(BF)
            spread = nn(firsts, hot)
            owner = lax.broadcasted_iota(jnp.int32, (32, 768), 0)
            self.up_bias[b] = row_sum(jnp.where(owner == self.lanes[3:4, cols], spread, 0.0))

    def tally(self):
        which = lax.broadcasted_iota(jnp.int32, (128, 128), 0)
        right, every = jnp.zeros((128, 128), F32), jnp.zeros((128, 128), F32)
        for r in range(8):
            target, guess, live = (ref[r : r + 1, :] for ref in (self.targets, self.predicted, self.live))
            hit = (which == target) & (live == 1)
            every += jnp.where(hit, 1.0, 0.0)
            right += jnp.where(hit & (guess == target), 1.0, 0.0)
        for row, total in ((12, right), (13, every)):
            self.sums[row : row + 1, 0:128] = nt(jnp.ones((8, 128), BF), total.astype(BF))[0:1]

    def note(self, row, value, cols=slice(0, 768)):
        self.partial[8 * row : 8 * row + 8, cols] += value

    def fold(self):
        for row in range(12):
            self.sums[row : row + 1] = row_sum(self.partial[8 * row : 8 * row + 8])

    def project(self, g, i):
        rows = span(i, TILE)
        out = (nn(self.tokens[rows, :], self.wqkv[:, g * 768 : (g + 1) * 768]) + self.qkv_bias[g]).astype(BF)
        for h in (0, HALF):
            at = g * 768 + h
            self.qkv[rows, at : at + 128] = out[:, h : h + 128] * 0.125
            self.qkv[rows, at + 128 : at + HALF] = out[:, h + 128 : h + HALF]

    def halves(self, pair):
        left = lax.broadcasted_iota(jnp.int32, pair.shape, 1) < 64
        zero = jnp.zeros_like(pair)
        return jnp.concatenate([jnp.where(left, pair, zero), jnp.where(left, zero, pair)], axis=0)

    def chains(self, g, rows):
        return [(r, p, span(r, 128)) for r in rows for p in (2 * g, 2 * g + 1)]

    def part(self, p, rows, b):
        return self.qkv[rows, p * HALF + b * 128 : p * HALF + (b + 1) * 128]

    def attend(self, g, rows):
        eye = lax.broadcasted_iota(jnp.int32, (128, 128), 0) == lax.broadcasted_iota(jnp.int32, (128, 128), 1)
        allowed, probs = {}, []
        for r in rows:
            seg = jnp.broadcast_to(self.segments[r : r + 1, :].astype(F32), (128, 128))
            allowed[r] = (seg == seg.T) & ((self.live[r : r + 1, :] == 1) | eye)
        ones = jnp.ones((128, 128), BF)
        chains = self.chains(g, rows)
        scores = [nt(self.halves(self.part(p, where, 0)), self.part(p, where, 1)) for r, p, where in chains]
        for (r, p, where), score in zip(chains, scores):
            some = []
            for at, part in parts(score, 128):
                part = jnp.where(allowed[r], part, -1e9)
                raised = jnp.exp(part - jnp.max(part, axis=-1, keepdims=True))
                total = nn(raised.astype(BF), ones)
                guess = pltpu.reciprocal(total, approx=True)
                some.append((raised * (guess * (2.0 - total * guess))).astype(BF))
            self.probs[r, p * 256 : (p + 1) * 256, :] = jnp.concatenate(some, axis=0)
            probs.append(jnp.concatenate(some, axis=1))
        for (r, p, where), prob in zip(chains, probs):
            self.context[where, p * 128 : (p + 1) * 128] = nn(prob, self.halves(self.part(p, where, 2))).astype(BF)

    def out_project(self, i):
        rows = span(i, TILE)
        attended = nn(self.context[rows, :], self.wout[...])
        for at, part in parts(attended, 32):
            here = pl.ds(i * TILE + at, 32)
            resid = self.tokens[here, :].astype(F32) + (part + self.lines[2:3])
            center = resid - mean(resid)
            inverse = lax.rsqrt(mean(center * center) + EPSILON)
            normed = center * inverse
            self.normed[here, :] = normed.astype(BF)
            self.inverse[at : at + 32, i : i + 1] = inverse
            self.hidden[here, :] = (normed * self.lines[3:4] + self.lines[4:5]).astype(BF)

    def up(self, b, i, tile=512):
        rows = span(i, tile)
        for c in range(3):
            cols = slice(c * 256, (c + 1) * 256)
            up = nn(self.hidden[rows, :], self.wup[:, b * 768 + c * 256 : b * 768 + (c + 1) * 256])
            for at, part in parts(up, 32):
                here = pl.ds(i * tile + at, 32)
                act, slope = gelu_both(part + self.up_bias[b, :, cols])
                self.act[b, here, cols] = act.astype(BF)
                self.slope[b, here, cols] = slope.astype(BF)

    def down_product(self, j):
        cols = slice(j * 256, (j + 1) * 256)
        for i in range(4):
            rows = span(i, TILE)
            ffn = nn(self.act[0, rows, :], self.wdown[0:768, cols])
            for b in range(1, 4):
                ffn += nn(self.act[b, rows, :], self.wdown[b * 768 : (b + 1) * 768, cols])
            self.wide[rows, cols] = ffn

    def down_norm(self, i):
        totals = [jnp.zeros((8, 768), F32)] * 3
        for at in range(0, TILE, 32):
            here = pl.ds(i * TILE + at, 32)
            hidden = self.normed[here, :].astype(F32) * self.lines[3:4] + self.lines[4:5]
            resid = hidden + (self.wide[here, :] + self.lines[5:6])
            center = resid - mean(resid)
            inverse = lax.rsqrt(mean(center * center) + EPSILON)
            normed = center * inverse
            self.layer_out[here, :] = (normed * self.lines[6:7] + self.lines[7:8]).astype(BF)
            upstream = self.cotangent[here, :].astype(F32)
            scaled = upstream * self.lines[6:7]
            d_two = inverse * (scaled - mean(scaled) - normed * mean(scaled * normed))
            totals = [old + eight(new) for old, new in zip(totals, (d_two, upstream * normed, upstream))]
            self.wide[here, :] = d_two
            self.low[here, :] = d_two.astype(BF)
        for row, total in zip((5, 6, 7), totals):
            self.note(row, total)

    def grad_down(self, j):
        cols = slice(j * 256, (j + 1) * 256)
        for b in range(4):
            self.gdown[b * 768 : (b + 1) * 768, cols] = tn(self.act[b], self.low[:, cols]).astype(BF)

    def back_up(self, b, i, tile=512):
        rows = span(i, tile)
        for c in range(3):
            cols = slice(c * 256, (c + 1) * 256)
            d_act = nt(self.low[rows, :], self.wdown[b * 768 + c * 256 : b * 768 + (c + 1) * 256, :])
            total = jnp.zeros((8, 256), F32)
            for at, part in parts(d_act, 32):
                here = pl.ds(i * tile + at, 32)
                d_up = (part * self.slope[b, here, cols].astype(F32)).astype(BF)
                self.slope[b, here, cols] = d_up
                total += eight(d_up.astype(F32))
            self.note(8 + b, total, cols)

    def grad_up(self, b):
        for c in range(3):
            cols = slice(c * 256, (c + 1) * 256)
            self.act[b, 0:768, cols] = tn(self.hidden[...], self.slope[b, :, cols]).astype(BF)

    def back_hidden(self, i):
        rows = span(i, TILE)
        for c in range(3):
            cols = slice(c * 256, (c + 1) * 256)
            back = nt(self.slope[0, rows, :], self.wup[cols, 0:768])
            for b in range(1, 4):
                back += nt(self.slope[b, rows, :], self.wup[cols, b * 768 : (b + 1) * 768])
            self.wide[rows, cols] += back
        totals = [jnp.zeros((8, 768), F32)] * 3
        for at in range(0, TILE, 32):
            here = pl.ds(i * TILE + at, 32)
            d_hidden = self.wide[here, :]
            normed = self.normed[here, :].astype(F32)
            scaled = d_hidden * self.lines[3:4]
            d_one = self.inverse[at : at + 32, i : i + 1] * (scaled - mean(scaled) - normed * mean(scaled * normed))
            totals = [old + eight(new) for old, new in zip(totals, (d_one, d_hidden * normed, d_hidden))]
            self.wide[here, :] = d_one
            self.low[here, :] = d_one.astype(BF)
        for row, total in zip((2, 3, 4), totals):
            self.note(row, total)

    def grad_out(self):
        for c in range(3):
            cols = slice(c * 256, (c + 1) * 256)
            self.slope[3, 0:768, cols] = tn(self.context[...], self.low[:, cols]).astype(BF)

    def back_context(self, i):
        rows = span(i, TILE)
        self.context[rows, :] = nt(self.low[rows, :], self.wout[...]).astype(BF)

    def back_attend(self, g, rows):
        chains = self.chains(g, rows)
        qkv = [[self.part(p, where, b) for b in range(3)] for r, p, where in chains]
        probs = [self.probs[r, p * 256 : (p + 1) * 256, :] for r, p, where in chains]
        d_context = [self.halves(self.context[where, p * 128 : (p + 1) * 128]) for r, p, where in chains]
        d_probs = [nt(down, v) for down, (q, k, v) in zip(d_context, qkv)]
        d_values = [tn(prob, down).astype(BF) for prob, down in zip(probs, d_context)]
        d_scores = []
        for prob, d_prob in zip(probs, d_probs):
            some = []
            for at, part in parts(d_prob, 128):
                wide = prob[at : at + 128].astype(F32)
                inner = jnp.sum(wide * part, axis=-1, keepdims=True)
                some.append((wide * (part - inner)).astype(BF))
            d_scores.append(some)
        d_queries = [(nn(jnp.concatenate(some, axis=1), self.halves(k)) * 0.125).astype(BF) for some, (q, k, v) in zip(d_scores, qkv)]
        d_keys = [tn(jnp.concatenate(some, axis=0), self.halves(q)).astype(BF) for some, (q, k, v) in zip(d_scores, qkv)]
        totals = {}
        for i, (r, p, where) in enumerate(chains):
            for b, grad in enumerate((d_queries[i], d_keys[i], d_values[i])):
                self.qkv[where, p * HALF + b * 128 : p * HALF + (b + 1) * 128] = grad
                if b != 1:
                    totals[b, p] = totals.get((b, p), 0.0) + eight(grad.astype(F32))
        for (b, p), total in totals.items():
            self.note(b // 2, total, slice(p * 128, (p + 1) * 128))

    def grad_qkv(self, g):
        for c in range(3):
            cols = slice(c * 256, (c + 1) * 256)
            grad = self.qkv[:, g * 768 + c * 256 : g * 768 + (c + 1) * 256]
            self.slope[g, 0:768, cols] = tn(self.tokens[...], grad).astype(BF)

    def back_tokens(self, i):
        rows = span(i, TILE)
        grad = self.wide[rows, :]
        for g in range(3):
            cols = slice(g * 768, (g + 1) * 768)
            grad += nt(self.qkv[rows, cols], self.wqkv[:, cols])
        self.wide[rows, :] = grad


LANES = np.stack([np.arange(3072) % 24, np.arange(3072) // 24, np.arange(3072) % 96, np.arange(3072) // 96] + [np.zeros(3072)] * 4).astype(np.int32)


def layer_kernel(
    token_rows, cotangent, segments, live, predicted, targets, lanes, sqkv, sout, sup, sdown, small, up_small,
    layer_out, grad_tokens, oqkv, oout, oup, odown, osums,
    tokens, wqkv, wout, wup, wdown, vecs, lines, up_bias, qkv_bias, partial, qkv, probs, context, normed, inverse, hidden, act, slope, wide, low, gdown,
    sums, pdown, land_up, land_down, whole, whole_down, totals, totals_down, lasts, lasts_down, stage, land,
    copies, sends, recvs, free, late,
):
    w = Wires(sends, recvs)
    core, chip = w.core, w.chip
    m = Layer(
        tokens=tokens, segments=segments, live=live, predicted=predicted, targets=targets, lanes=lanes, vecs=vecs,
        wqkv=wqkv, wout=wout, wup=wup, wdown=wdown, lines=lines, up_bias=up_bias, qkv_bias=qkv_bias, partial=partial, qkv=qkv, probs=probs,
        context=context, normed=normed, inverse=inverse, hidden=hidden, act=act, slope=slope, wide=wide, low=low, gdown=gdown,
        sums=sums, cotangent=gdown.at[0:1024], layer_out=gdown.at[1024:2048],
    )

    def block(b):
        return (wqkv, b * 768) if b < 3 else (wout, 0) if b < 4 else (wup, (b - 4) * 768)

    def shard(b, h):
        if b < 3:
            return jnp.concatenate([sqkv[:, i * 768 + (2 * b + h) * 128 : i * 768 + (2 * b + h + 1) * 128] for i in range(3)], axis=1)
        ref, at = (sout, 0) if b < 4 else (sup, (b - 4) * 768)
        return ref[:, at + h * HALF : at + (h + 1) * HALF]

    def packed(first, b, core_rows=0):
        rows = pl.ds(pl.multiple_of(first + core_rows + (b // 2) * 32, 16), 32)
        return rows, slice((b % 2) * HALF, (b % 2 + 1) * HALF)

    def exchange():
        for h in (0, 1):
            for b in range(8):
                rows, cols = packed(2048 + h * 128, b)
                gdown[rows, cols] = jnp.concatenate([shard(b, h).astype(F32), jnp.zeros((8, HALF), F32)], axis=0).astype(BF)
        w.meet()
        there = w.partner()
        first = pl.ds(pl.multiple_of(2048 + (1 - core) * 128, 16), 64)
        second = pl.ds(pl.multiple_of(2112 + (1 - core) * 128, 16), 64)
        one = w.send(gdown.at[first, :], gdown.at[2304:2368, :], there)
        spread.step()
        two = w.send(gdown.at[second, :], gdown.at[2368:2432, :], there)
        three = []
        for j in range(3):
            cols = pl.ds(pl.multiple_of(j * 256 + (1 - core) * 128, 128), 128)
            three.append(w.send(sdown.at[:, cols], gdown.at[2432:2528, j * 128 : (j + 1) * 128], there))

        def merge(b):
            rows, cols = packed(2048, b, core * 128)
            own = gdown[rows, cols].astype(F32)[:24]
            rows, cols = packed(2304, b)
            got = gdown[rows, cols].astype(F32)[:24]
            low_rows, high_rows = jnp.where(core == 0, own, got), jnp.where(core == 0, got, own)
            ref, at = block(b)
            ref[rows_at(chip, 1, 48), pl.ds(pl.multiple_of(at + core * HALF, 128), HALF)] = jnp.concatenate(
                [low_rows, high_rows], axis=0
            ).astype(BF)

        one.wait_recv()
        for b in range(4):
            merge(b)
        return merge, two, three

    def exchange_rest(merge, two, three):
        two.wait_recv()
        for b in range(4, 8):
            merge(b)
        arrived(three)
        for j in range(3):
            cols = pl.ds(pl.multiple_of(j * 256 + core * 128, 128), 128)
            wdown[pl.ds(pl.multiple_of(chip * 192 + core * 96, 16), 96), cols] = sdown[:, cols]
            wdown[pl.ds(pl.multiple_of(chip * 192 + (1 - core) * 96, 16), 96), cols] = gdown[2432:2528, j * 128 : (j + 1) * 128]

    spread = Spread(w, vecs)
    pieces = {SPREAD: spread}
    for i, (b, offset, width, order) in enumerate(GATHERS):
        if b < 8:
            ref, at = block(b)
            pieces[GATHER + i] = Gather(w, ref, 48, at + core * HALF + offset, width, order)
        else:
            pieces[GATHER + i] = Gather(w, wdown, 192, (b - 8) * 256 + core * 128, 128, order)

    def writer(b, offset, width):
        def write(which, value):
            for i in range(width // 128):
                part = i + offset // 128
                if b < 3:
                    ref, at = oqkv, part * 768 + 2 * b * 128 + which * 128
                elif b < 8:
                    ref, at = (oout if b < 4 else oup), max(b - 4, 0) * 768 + part * 128 + which * HALF
                else:
                    ref, at = odown, (b - 8) * 256 + which * 128
                ref[:, pl.ds(pl.multiple_of(at, 128), 128)] = value[:, i * 128 : (i + 1) * 128]

        return write

    def alone(body, *args):
        @pl.when(core >= 0)
        def _():
            body(*args)

    class Gate:
        def __init__(self, semaphore, count):
            self.semaphore, self.count, self.passed = semaphore, count, False

        def __call__(self):
            if not self.passed:
                pl.semaphore_wait(self.semaphore, self.count)
                self.passed = True

    ready, gate, always = Gate(free, 1), Gate(late, 5), lambda: None
    finished = {"back_up": 0, "back_hidden": 0, "grad_down": 0, "back_attend": 0}

    def last_of(name, count):
        finished[name] += 1
        return finished[name] == count

    def back_hidden(i):
        alone(m.back_hidden, i)
        if last_of("back_hidden", 4):
            for peer in [w.over_x(), w.over_y()] + [w.along_z(j) for j in (1, 2, 3)]:
                pl.semaphore_signal(late, inc=1, device_id=peer, device_id_type=MESH)

    for i, (b, offset, width, order) in enumerate(SCATTERS):
        cols = slice(offset, offset + width)
        if b < 8:
            ref = slope.at[b, 0:768] if b < 3 else slope.at[3, 0:768] if b < 4 else act.at[b - 4, 0:768]
            p = wdown.at[(b // 2) * 768 : (b // 2 + 1) * 768, (b % 2) * HALF + offset : (b % 2) * HALF + offset + width]
            land_at = wup.at[0:720, b * 768 + offset : b * 768 + offset + width] if b < 4 else land_up.at[b - 4, :, cols]
            pieces[SCATTER + i] = Scatter(
                w, ref, 48, core * HALF + offset, (1 - core) * HALF + offset, width, order, p, land_at, whole.at[:, cols],
                totals.at[b, :, cols], lasts.at[b, :, cols], writer(b, offset, width), ready, gate if b < 4 else always,
            )
        else:
            j = b - 8
            pieces[SCATTER + i] = Scatter(
                w, gdown, 192, j * 256 + core * 128, j * 256 + (1 - core) * 128, 128, order, pdown.at[j], land_down.at[j], whole_down,
                totals_down.at[j], lasts_down.at[j], writer(b, 0, 128), always, always,
            )
    pieces[SUMS] = Sums(w, sums, stage, land, osums)
    held = {}

    def local(source, target, i):
        held[i] = pltpu.make_async_copy(source, target, copies.at[i])
        held[i].start()

    def start():
        w.greet()
        local(token_rows, tokens, 9)
        local(cotangent, gdown.at[0:1024], 0)
        lasts[0, 0:8, 0:128] = jnp.zeros((8, 128), F32)
        lasts[0, 0:8, 0:24] = small[...].astype(F32)
        lasts[0, 0:1, 32:128] = up_small[...].astype(F32)
        vecs[pl.ds(pl.multiple_of((chip * 2 + core) * 8, 8), 8), :] = lasts[0, 0:8, 0:128]
        sums[...] = jnp.zeros_like(sums)
        partial[...] = jnp.zeros_like(partial)
        held["rest"] = exchange()

    def first():
        held[9].wait()
        alone(m.vectors)
        alone(m.tally)

    def down(i):
        if i == 0:
            held[0].wait()
        alone(m.down_norm, i)
        rows = slice(i * TILE, (i + 1) * TILE)
        local(gdown.at[1024 + i * TILE : 1024 + (i + 1) * TILE], layer_out.at[rows], 1 + i)

    def grad_down(j):
        if last_of("grad_down", 1):
            w.drain()
            for i in range(4):
                held[1 + i].wait()
        alone(m.grad_down, j)

    def back_up(b):
        alone(lambda: [m.back_up(b, i) for i in (0, 1)])
        if last_of("back_up", 4):
            pl.semaphore_signal(free, inc=1, device_id=w.partner(), device_id_type=MESH)

    def grad_up(b):
        alone(m.grad_up, b)

    def back_attend(g, h):
        alone(m.back_attend, g, range(4 * h, 4 * h + 4))
        if last_of("back_attend", 6):
            alone(m.fold)

    def back_tokens(i):
        alone(m.back_tokens, i)
        rows = slice(i * TILE, (i + 1) * TILE)
        local(wide.at[rows], grad_tokens.at[rows], 5 + i)

    parts_of_work = {"start": start, "rest": lambda: exchange_rest(*held["rest"]), "first": first}

    def add(name, body, *args):
        parts_of_work[name] = functools.partial(body, *args)

    for g in range(3):
        add(f"proj{g}", alone, lambda g=g: [m.project(g, i) for i in range(4)])
        add(f"gq{g}", alone, m.grad_qkv, g)
        for h in (0, 1):
            add(f"att{g}{h}", alone, m.attend, g, range(4 * h, 4 * h + 4))
            add(f"ba{g}{h}", back_attend, g, h)
    for h in (0, 1):
        add(f"out{h}", alone, lambda h=h: [m.out_project(i) for i in (2 * h, 2 * h + 1)])
    for j in range(3):
        add(f"gd{j}", grad_down, j)
        add(f"dm{j}", alone, m.down_product, j)
    for i in range(4):
        add(f"up{i}0", alone, m.up, i, 0)
        add(f"up{i}1", alone, m.up, i, 1)
        add(f"de{i}", down, i)
        add(f"bu{i}", back_up, i)
        add(f"gu{i}", grad_up, i)
        add(f"bh{i}", back_hidden, i)
        add(f"bt{i}", back_tokens, i)
    add("go", alone, m.grad_out)
    add("bc", alone, lambda: [m.back_context(i) for i in range(4)])
    add("end", always)
    assert len(PLAN) == len(parts_of_work)
    for name, steps in PLAN:
        for i in steps:
            pieces[i].step()
        parts_of_work[name]()
    for i in range(4):
        held[5 + i].wait()
    w.drain()
    assert w.used <= SEMAPHORES, w.used


def layer(tokens, cotangent, segment_ids, live_mask, predicted, targets, w_qkv, w_out, w_up, w_down, small, up_small):
    V = pl.BlockSpec(memory_space=pltpu.VMEM)
    A = pl.BlockSpec(memory_space=pl.ANY)
    return pl.pallas_call(
        layer_kernel,
        out_shape=(
            jax.ShapeDtypeStruct((1024, 768), BF),
            jax.ShapeDtypeStruct((1024, 768), F32),
            jax.ShapeDtypeStruct((24, 2304), F32),
            jax.ShapeDtypeStruct((24, 768), F32),
            jax.ShapeDtypeStruct((24, 3072), F32),
            jax.ShapeDtypeStruct((96, 768), F32),
            jax.ShapeDtypeStruct((16, 768), F32),
        ),
        in_specs=[A, A] + [V] * 11,
        out_specs=[A] * 2 + [V] * 5,
        scratch_shapes=[
            pltpu.VMEM((1024, 768), BF),
            pltpu.VMEM((768, 2304), BF),
            pltpu.VMEM((768, 768), BF),
            pltpu.VMEM((768, 3072), BF),
            pltpu.VMEM((3072, 768), BF),
            pltpu.VMEM((256, 128), F32),
            pltpu.VMEM((8, 768), F32),
            pltpu.VMEM((4, 1, 768), F32),
            pltpu.VMEM((3, 1, 768), F32),
            pltpu.VMEM((96, 768), F32),
            pltpu.VMEM((1024, 2304), BF),
            pltpu.VMEM((8, 1536, 128), BF),
            pltpu.VMEM((1024, 768), BF),
            pltpu.VMEM((1024, 768), BF),
            pltpu.VMEM((TILE, 128), F32),
            pltpu.VMEM((1024, 768), BF),
            pltpu.VMEM((4, 1024, 768), BF),
            pltpu.VMEM((4, 1024, 768), BF),
            pltpu.VMEM((1024, 768), F32),
            pltpu.VMEM((1024, 768), BF),
            pltpu.VMEM((3072, 768), BF),
            pltpu.VMEM((16, 768), F32),
            pltpu.VMEM((3, 3072, 128), BF),
            pltpu.VMEM((4, 720, HALF), BF),
            pltpu.VMEM((3, 2880, 128), BF),
            pltpu.VMEM((48, HALF), F32),
            pltpu.VMEM((192, 128), F32),
            pltpu.VMEM((8, 24, HALF), F32),
            pltpu.VMEM((3, 96, 128), F32),
            pltpu.VMEM((8, 24, HALF), F32),
            pltpu.VMEM((3, 96, 128), F32),
            pltpu.VMEM((4, 16, HALF), F32),
            pltpu.VMEM((6, 16, HALF), F32),
            pltpu.SemaphoreType.DMA((10,)),
            pltpu.SemaphoreType.DMA((SEMAPHORES,)),
            pltpu.SemaphoreType.DMA((SEMAPHORES,)),
            pltpu.SemaphoreType.REGULAR,
            pltpu.SemaphoreType.REGULAR,
        ],
        compiler_params=pltpu.CompilerParams(collective_id=0, has_side_effects=True, vmem_limit_bytes=64 * 2**20 - 2**17),
    )(
        tokens, cotangent, segment_ids, live_mask, predicted.reshape(8, 128), targets.reshape(8, 128), jnp.asarray(LANES),
        w_qkv, w_out, w_up, w_down, small, up_small,
    )


def finish_kernel(a, b, c, d, e, f, sums, oa, ob, oc, od, oe, of, *rest):
    vectors, up_vector, tallies, buffers, semaphores = rest[:8], rest[8], rest[9], rest[10:16], rest[16]
    copies = []
    for old, new, buffer, cuts in zip((a, b, c, d, e, f), (oa, ob, oc, od, oe, of), buffers, (4, 8, 1, 1, 1, 2)):
        size = old.shape[0] // cuts
        for i in range(cuts):
            rows = pl.ds(i * size, size)
            number = len(copies)
            copies.append(
                (
                    pltpu.make_async_copy(old.at[rows], buffer.at[rows], semaphores.at[2 * number]),
                    pltpu.make_async_copy(buffer.at[rows], new.at[rows], semaphores.at[2 * number + 1]),
                )
            )
            copies[-1][0].start()
    device = lax.axis_index("dp") * 8 + lax.axis_index("fsdp")
    place = lax.broadcasted_iota(jnp.int32, (768, 128), 0)
    lane = lax.broadcasted_iota(jnp.int32, (768, 128), 1)

    def pick(value, first):
        hot = jnp.where(place == lane + first, 1.0, 0.0)
        return lax.dot_general(
            value, hot, (((1,), (0,)), ((), ())), precision=lax.Precision.HIGHEST, preferred_element_type=F32
        )

    own = pick(sums[0:8, :], device * 24)
    for i, out in enumerate(vectors):
        out[...] = own[i : i + 1, 0:24]
    row = sums[pl.ds(8 + device // 8, 1), :]
    up_vector[...] = pick(jnp.broadcast_to(row, (8, 768)), device % 8 * 96)[0:1, 0:96]
    tallies[...] = sums[12:14, 0:24].astype(jnp.int32)
    for copy_in, copy_out in copies:
        copy_in.wait()
        copy_out.start()
    for copy_in, copy_out in copies:
        copy_out.wait()


def finish(layer_out, grad_tokens, gqkv, gout, gup, gdown, sums):
    V = pl.BlockSpec(memory_space=pltpu.VMEM)
    A = pl.BlockSpec(memory_space=pl.ANY)
    arrays = (layer_out, grad_tokens, gqkv, gout, gup, gdown)
    return pl.pallas_call(
        finish_kernel,
        out_shape=tuple(jax.ShapeDtypeStruct(x.shape, x.dtype) for x in arrays)
        + (jax.ShapeDtypeStruct((1, 24), F32),) * 8
        + (jax.ShapeDtypeStruct((1, 96), F32), jax.ShapeDtypeStruct((2, 24), jnp.int32)),
        in_specs=[A] * 6 + [V],
        out_specs=[A] * 6 + [V] * 10,
        scratch_shapes=[pltpu.VMEM(x.shape, x.dtype) for x in arrays] + [pltpu.SemaphoreType.DMA((34,))],
        compiler_params=pltpu.CompilerParams(vmem_limit_bytes=63 * 2**20),
    )(*arrays, sums)


def plain_device(
    tokens,
    cotangent,
    segment_ids,
    live_mask,
    predicted,
    targets,
    w_qkv,
    bias_query,
    bias_value,
    w_out,
    bias_out,
    gain_attn,
    shift_attn,
    w_up,
    bias_up,
    w_down,
    bias_down,
    gain_ffn,
    shift_ffn,
):
    row_count, seq_len = segment_ids.shape
    classes = jnp.arange(CLASSES, dtype=jnp.int32)
    live_flat = live_mask.reshape(-1) == 1
    target_hits = (targets[:, None] == classes[None, :]) & live_flat[:, None]
    correct = target_hits & (predicted[:, None] == targets[:, None])
    local_tally = jnp.stack(
        [jnp.sum(correct, axis=0, dtype=jnp.int32), jnp.sum(target_hits, axis=0, dtype=jnp.int32)]
    )
    tallies = lax.psum(local_tally, ("dp", "fsdp"))
    (
        whole_qkv,
        whole_query_bias,
        whole_value_bias,
        whole_out,
        whole_out_bias,
        whole_gain_attn,
        whole_shift_attn,
        whole_up,
        whole_up_bias,
        whole_down,
        whole_down_bias,
        whole_gain_ffn,
        whole_shift_ffn,
    ) = (
        lax.all_gather(w_qkv, ("dp", "fsdp"), axis=0, tiled=True),
        lax.all_gather(bias_query, ("dp", "fsdp"), axis=0, tiled=True),
        lax.all_gather(bias_value, ("dp", "fsdp"), axis=0, tiled=True),
        lax.all_gather(w_out, ("dp", "fsdp"), axis=0, tiled=True),
        lax.all_gather(bias_out, ("dp", "fsdp"), axis=0, tiled=True),
        lax.all_gather(gain_attn, ("dp", "fsdp"), axis=0, tiled=True),
        lax.all_gather(shift_attn, ("dp", "fsdp"), axis=0, tiled=True),
        lax.all_gather(w_up, ("dp", "fsdp"), axis=0, tiled=True),
        lax.all_gather(bias_up, ("dp", "fsdp"), axis=0, tiled=True),
        lax.all_gather(w_down, ("dp", "fsdp"), axis=0, tiled=True),
        lax.all_gather(bias_down, ("dp", "fsdp"), axis=0, tiled=True),
        lax.all_gather(gain_ffn, ("dp", "fsdp"), axis=0, tiled=True),
        lax.all_gather(shift_ffn, ("dp", "fsdp"), axis=0, tiled=True),
    )
    projected = jnp.dot(tokens, whole_qkv, preferred_element_type=jnp.float32)
    queries = (projected[:, :D] + whole_query_bias.astype(jnp.float32)).astype(jnp.bfloat16)
    keys_part = projected[:, D : 2 * D].astype(jnp.bfloat16)
    values = (projected[:, 2 * D :] + whole_value_bias.astype(jnp.float32)).astype(jnp.bfloat16)
    query_heads = split_heads(queries, row_count, seq_len)
    key_heads = split_heads(keys_part, row_count, seq_len)
    value_heads = split_heads(values, row_count, seq_len)
    diagonal = jnp.eye(seq_len, dtype=bool)
    allowed = (segment_ids[:, :, None] == segment_ids[:, None, :]) & (
        (live_mask[:, None, :] == 1) | diagonal[None]
    )
    scores = masked_scores(query_heads, key_heads, allowed)
    highest = jnp.max(scores, axis=-1, keepdims=True)
    raised = jnp.exp(scores - highest)
    total = jnp.sum(raised, axis=-1, keepdims=True)
    soft_weights = raised / total
    log_total = highest + jnp.log(total)
    context = (
        jnp.einsum(
            "bhqk,bkhc->bqhc",
            soft_weights.astype(jnp.bfloat16),
            value_heads,
            preferred_element_type=jnp.float32,
        )
        .reshape(-1, D)
        .astype(jnp.bfloat16)
    )
    attended = jnp.dot(
        context, whole_out, preferred_element_type=jnp.float32
    ) + whole_out_bias.astype(jnp.float32)
    hidden, normed_one, inverse_one = normalize(
        tokens.astype(jnp.float32) + attended,
        whole_gain_attn.astype(jnp.float32),
        whole_shift_attn.astype(jnp.float32),
    )
    hidden_low = hidden.astype(jnp.bfloat16)
    up_value = jnp.dot(
        hidden_low, whole_up, preferred_element_type=jnp.float32
    ) + whole_up_bias.astype(jnp.float32)
    activated_low = jax.nn.gelu(up_value, approximate=False).astype(jnp.bfloat16)
    ffn_out = jnp.dot(
        activated_low, whole_down, preferred_element_type=jnp.float32
    ) + whole_down_bias.astype(jnp.float32)
    layer_out, normed_two, inverse_two = normalize(
        hidden + ffn_out, whole_gain_ffn.astype(jnp.float32), whole_shift_ffn.astype(jnp.float32)
    )
    back_qkv, back_out, back_up, back_down, back_gain_attn, back_gain_ffn = (
        lax.all_gather(w_qkv, ("dp", "fsdp"), axis=0, tiled=True),
        lax.all_gather(w_out, ("dp", "fsdp"), axis=0, tiled=True),
        lax.all_gather(w_up, ("dp", "fsdp"), axis=0, tiled=True),
        lax.all_gather(w_down, ("dp", "fsdp"), axis=0, tiled=True),
        lax.all_gather(gain_attn, ("dp", "fsdp"), axis=0, tiled=True),
        lax.all_gather(gain_ffn, ("dp", "fsdp"), axis=0, tiled=True),
    )
    upstream = cotangent.astype(jnp.float32)
    grad_gain_ffn = jnp.sum(upstream * normed_two, axis=0)
    grad_shift_ffn = jnp.sum(upstream, axis=0)
    d_resid_two = normalize_back(
        upstream, normed_two, inverse_two, back_gain_ffn.astype(jnp.float32)
    )
    d_two_low = d_resid_two.astype(jnp.bfloat16)
    grad_down = contract_rows(activated_low, d_two_low)
    grad_down_bias = jnp.sum(d_resid_two, axis=0)
    d_activated = times_transposed(d_two_low, back_down)
    gelu_pullback = jax.vjp(partial(jax.nn.gelu, approximate=False), up_value)[1]
    d_up = gelu_pullback(d_activated)[0].astype(jnp.bfloat16)
    grad_up_bias = jnp.sum(d_up.astype(jnp.float32), axis=0)
    grad_up = contract_rows(hidden_low, d_up)
    d_hidden = d_resid_two + times_transposed(d_up, back_up)
    grad_gain_attn = jnp.sum(d_hidden * normed_one, axis=0)
    grad_shift_attn = jnp.sum(d_hidden, axis=0)
    d_resid_one = normalize_back(
        d_hidden, normed_one, inverse_one, back_gain_attn.astype(jnp.float32)
    )
    d_one_low = d_resid_one.astype(jnp.bfloat16)
    grad_out_bias = jnp.sum(d_resid_one, axis=0)
    grad_out = contract_rows(context, d_one_low)
    d_context = times_transposed(d_one_low, back_out).astype(jnp.bfloat16)
    d_context_heads = split_heads(d_context, row_count, seq_len)
    d_soft = jnp.einsum(
        "bqhc,bkhc->bhqk", d_context_heads, value_heads, preferred_element_type=jnp.float32
    )
    soft_again = jnp.exp(masked_scores(query_heads, key_heads, allowed) - log_total)
    d_values = (
        jnp.einsum(
            "bhqk,bqhc->bkhc",
            soft_again.astype(jnp.bfloat16),
            d_context_heads,
            preferred_element_type=jnp.float32,
        )
        .reshape(-1, D)
        .astype(jnp.bfloat16)
    )
    inner = jnp.sum(soft_again * d_soft, axis=-1, keepdims=True)
    d_scores = (soft_again * (d_soft - inner)).astype(jnp.bfloat16)
    d_queries = (
        (
            jnp.einsum("bhqk,bkhc->bqhc", d_scores, key_heads, preferred_element_type=jnp.float32)
            * HEAD_DIM ** (-0.5)
        )
        .reshape(-1, D)
        .astype(jnp.bfloat16)
    )
    d_keys = (
        (
            jnp.einsum("bhqk,bqhc->bkhc", d_scores, query_heads, preferred_element_type=jnp.float32)
            * HEAD_DIM ** (-0.5)
        )
        .reshape(-1, D)
        .astype(jnp.bfloat16)
    )
    d_projected = jnp.concatenate([d_queries, d_keys, d_values], axis=1)
    grad_query_bias = jnp.sum(d_queries.astype(jnp.float32), axis=0)
    grad_value_bias = jnp.sum(d_values.astype(jnp.float32), axis=0)
    grad_qkv = contract_rows(tokens, d_projected)
    grad_tokens = d_resid_one + times_transposed(d_projected, back_qkv)
    summed = tuple(
        (
            lax.psum_scatter(grad_qkv, ("dp", "fsdp"), scatter_dimension=0, tiled=True),
            lax.psum_scatter(grad_query_bias, ("dp", "fsdp"), scatter_dimension=0, tiled=True),
            lax.psum_scatter(grad_value_bias, ("dp", "fsdp"), scatter_dimension=0, tiled=True),
            lax.psum_scatter(grad_out, ("dp", "fsdp"), scatter_dimension=0, tiled=True),
            lax.psum_scatter(grad_out_bias, ("dp", "fsdp"), scatter_dimension=0, tiled=True),
            lax.psum_scatter(grad_gain_attn, ("dp", "fsdp"), scatter_dimension=0, tiled=True),
            lax.psum_scatter(grad_shift_attn, ("dp", "fsdp"), scatter_dimension=0, tiled=True),
            lax.psum_scatter(grad_up, ("dp", "fsdp"), scatter_dimension=0, tiled=True),
            lax.psum_scatter(grad_up_bias, ("dp", "fsdp"), scatter_dimension=0, tiled=True),
            lax.psum_scatter(grad_down, ("dp", "fsdp"), scatter_dimension=0, tiled=True),
            lax.psum_scatter(grad_down_bias, ("dp", "fsdp"), scatter_dimension=0, tiled=True),
            lax.psum_scatter(grad_gain_ffn, ("dp", "fsdp"), scatter_dimension=0, tiled=True),
            lax.psum_scatter(grad_shift_ffn, ("dp", "fsdp"), scatter_dimension=0, tiled=True),
        )
    )
    return (layer_out.astype(jnp.bfloat16), grad_tokens) + summed + (tallies,)


def fast_device(
    tokens,
    cotangent,
    segment_ids,
    live_mask,
    predicted,
    targets,
    w_qkv,
    bias_query,
    bias_value,
    w_out,
    bias_out,
    gain_attn,
    shift_attn,
    w_up,
    bias_up,
    w_down,
    bias_down,
    gain_ffn,
    shift_ffn,
):

    small = jnp.stack([bias_query, bias_value, bias_out, gain_attn, shift_attn, bias_down, gain_ffn, shift_ffn])
    results = finish(
        *layer(tokens, cotangent, segment_ids, live_mask, predicted, targets, w_qkv, w_out, w_up, w_down, small, bias_up[None])
    )
    layer_out, grad_tokens, gqkv, gout, gup, gdown = results[:6]
    lines = [line.reshape(24) for line in results[6:14]]
    return (
        layer_out, grad_tokens, gqkv, lines[0], lines[1], gout, lines[2], lines[3], lines[4], gup, results[14].reshape(96), gdown,
        lines[5], lines[6], lines[7], results[15],
    )


def solution(mesh):
    in_specs = (
        P(("dp", "fsdp"), None),
        P(("dp", "fsdp"), None),
        P(("dp", "fsdp"), None),
        P(("dp", "fsdp"), None),
        P(("dp", "fsdp")),
        P(("dp", "fsdp")),
        P(("dp", "fsdp"), None),
        P(("dp", "fsdp")),
        P(("dp", "fsdp")),
        P(("dp", "fsdp"), None),
        P(("dp", "fsdp")),
        P(("dp", "fsdp")),
        P(("dp", "fsdp")),
        P(("dp", "fsdp"), None),
        P(("dp", "fsdp")),
        P(("dp", "fsdp"), None),
        P(("dp", "fsdp")),
        P(("dp", "fsdp")),
        P(("dp", "fsdp")),
    )
    out_specs = (
        P(("dp", "fsdp"), None),
        P(("dp", "fsdp"), None),
        P(("dp", "fsdp"), None),
        P(("dp", "fsdp")),
        P(("dp", "fsdp")),
        P(("dp", "fsdp"), None),
        P(("dp", "fsdp")),
        P(("dp", "fsdp")),
        P(("dp", "fsdp")),
        P(("dp", "fsdp"), None),
        P(("dp", "fsdp")),
        P(("dp", "fsdp"), None),
        P(("dp", "fsdp")),
        P(("dp", "fsdp")),
        P(("dp", "fsdp")),
        P(),
    )
    fast = tuple(mesh.shape.items()) == (("dp", 4), ("fsdp", 8))
    return jax.shard_map(
        fast_device if fast else plain_device, mesh=mesh, in_specs=in_specs, out_specs=out_specs, check_vma=False
    )
```
